128 devices in a mesh: ctx: 32 (over y, z_lo, x), tp: 4 (over z_hi, core).
Axes of the slice: x: 4, y: 4, z: 4 (z_hi: 2, z_lo: 2; z = z_hi * 2 + z_lo), core: 2. Of those that a mesh axis runs over, the one named last changes fastest.
Arguments:
- tokens_in: bfloat16 [8192, 2048], P('ctx'), may hold values from -6 to 6
- w_query: bfloat16 [2048, 2048], P('ctx', 'tp'), may hold values from -0.1875 to 0.1875
- w_key: bfloat16 [2048, 2048], P('ctx', 'tp'), may hold values from -0.1875 to 0.1875
- w_value: bfloat16 [2048, 2048], P('ctx', 'tp'), may hold values from -0.125 to 0.125
- w_output: bfloat16 [2048, 2048], P('ctx', 'tp'), may hold values from -0.75 to 0.75
- w_gate: bfloat16 [2048, 8192], P('ctx', 'tp'), may hold values from -0.125 to 0.125
- w_up: bfloat16 [2048, 8192], P('ctx', 'tp'), may hold values from -0.125 to 0.125
- w_down: bfloat16 [2048, 8192], P('ctx', 'tp'), may hold values from -0.0625 to 0.0625
- grad_out: bfloat16 [8192, 2048], P('ctx'), may hold values from -6 to 6
- block_ids: int32 [2, 4096], replicated, may hold values from 0 to 20, never falling along the last dimension, each value on 1 to 256 neighbouring positions
- tile_order: int32 [2, 64], replicated, may hold values from 0 to 63, as said below
Outputs:
- tokens_out: bfloat16 [8192, 2048], P('ctx')
- grad_in: float32 [8192, 2048], P('ctx')
- grad_query: float32 [2048, 2048], P('ctx', 'tp')
- grad_key: float32 [2048, 2048], P('ctx', 'tp')
- grad_value: float32 [2048, 2048], P('ctx', 'tp')
- grad_output: float32 [2048, 2048], P('ctx', 'tp')
- grad_gate: float32 [2048, 8192], P('ctx', 'tp')
- grad_up: float32 [2048, 8192], P('ctx', 'tp')
- grad_down: float32 [2048, 8192], P('ctx', 'tp')
The draws below stay inside these ranges and needn't reach their ends.
Inputs may be any that keep to these rules, and one draw needn't show every extreme that they name: `tile_order`: in each row every piece number appears once; columns 2 i and 2 i + 1 hold c and 63 - c with c < 32, the order of the c drawn afresh. `block_ids`: within a sequence the ids never fall and every id occurs; one block has at most 256 positions.
All inputs are finite; a program needn't handle non-finite values.
Results may differ from the reference program's by a relative error of at most 0.035.
Values may be sent and summed in bfloat16 or wider, within the bound.
No kernel may reach another device: no remote copies, remote signals or barrier semaphores. Data moves between devices by JAX's collectives and lax.ppermute only.
A program may use at most 256 MiB of HBM per device.

```python
import math
import jax
import jax.numpy as jnp
import numpy as np
from jax import lax

D = 2048
HEADS = 16
HEAD_DIM = 128
FF = 8192
TILE = 64
BLOCK = 256
SEQS = 2
TILES = 64
SEQLEN = 4096
TOK_DEV = 256
TOKENS = 8192
N_CTX = 32


def draw_tile_order(key, part):
    key = jax.random.fold_in(key, 7)
    keys = jax.random.split(key, SEQS)
    half_count = TILES // 2
    orders = jax.vmap(lambda one_key: jax.random.permutation(one_key, half_count))(keys).astype(jnp.int32)
    paired = jnp.stack([orders, TILES - 1 - orders], axis=-1)
    return paired.reshape(SEQS, TILES).astype(jnp.int32)


def level_of(own_key, shape, cuts, least, high):
    def one(position, parts):
        draws = jax.random.uniform(jax.random.fold_in(jax.random.fold_in(own_key, 6), position), (parts,), jnp.float32, least / len(cuts), high / len(cuts))
        return jnp.repeat(jnp.exp(draws), shape[position] // parts).reshape((-1,) + (1,) * (len(shape) - position - 1))

    factor_of = one(*cuts[0])
    for cut in cuts[1:]:
        factor_of = factor_of * one(*cut)
    return factor_of


def split_up(amount, total, reach, lean):
    portions = [(1 << 20) // math.isqrt(standing ** lean) + 1 for standing in range(2, amount + 1)]
    spare, holding = total - reach - (amount - 1), [1] * (amount - 1)
    while spare > 0:
        movable = [i for i in range(amount - 1) if holding[i] < reach]
        mass, budget = sum([portions[i] for i in movable]), spare
        for i in movable:
            more = min(reach - holding[i], max(1, budget * portions[i] // mass), spare)
            holding[i] = holding[i] + more
            spare = spare - more
    return np.array([reach] + holding)


def ragged_sizes(stream_key, amount, total, limit, skew):
    if amount == 2:
        one = jax.random.randint(stream_key, (), max(1, total - limit), min(limit, total - 1) + 1)
        return jnp.stack([one, total - one])
    tallies = jnp.asarray(split_up(amount, total, limit, skew), jnp.int32)
    pairs = (amount - 1) // 2
    giver, receiver = tallies[1:1 + 2 * pairs:2], tallies[2:2 + 2 * pairs:2]
    slack = jnp.minimum(giver - 1, limit - receiver)
    shifted = jax.random.randint(jax.random.fold_in(stream_key, 1), (pairs,), 0, 1 << 20) % (slack + 1)
    tallies = tallies.at[1:1 + 2 * pairs:2].set(giver - shifted).at[2:2 + 2 * pairs:2].set(receiver + shifted)
    return tallies[jax.random.permutation(jax.random.fold_in(stream_key, 2), amount)]


def gaussian(rng, shape, deviation, limit, cuts=(), kind=jnp.bfloat16):
    drawn = jax.random.normal(rng, shape, jnp.float32) * deviation
    if len(cuts) > 0:
        drawn = level_of(rng, shape, cuts, -0.22, 0.18) * drawn
    return jnp.clip(drawn, min=-limit, max=limit).astype(kind)


def setup_inputs(seed: int = 0) -> dict:
    streams_of = jax.random.split(jax.random.key(seed), 12)
    tokens_in = gaussian(streams_of[0], (TOKENS, D), 1.0, 6.0, ((0, 32),))
    w_query = gaussian(streams_of[1], (D, HEADS * HEAD_DIM), (D // 2) ** -0.5, 0.1875, ((0, 32), (1, 4)))
    w_key = gaussian(streams_of[2], (D, HEADS * HEAD_DIM), (D // 2) ** -0.5, 0.1875, ((0, 32), (1, 4)))
    w_value = gaussian(streams_of[3], (D, HEADS * HEAD_DIM), D ** -0.5, 0.125, ((0, 32), (1, 4)))
    w_output = gaussian(streams_of[4], (D, HEADS * HEAD_DIM), (HEADS * HEAD_DIM // 32) ** -0.5, 0.75, ((0, 32), (1, 4)))
    w_gate = gaussian(streams_of[5], (D, FF), D ** -0.5, 0.125, ((0, 32), (1, 4)))
    w_up = gaussian(streams_of[6], (D, FF), D ** -0.5, 0.125, ((0, 32), (1, 4)))
    w_down = gaussian(streams_of[7], (D, FF), FF ** -0.5, 0.0625, ((0, 32), (1, 4)))
    grad_out = gaussian(streams_of[8], (TOKENS, D), 1.0, 6.0, ((0, 32),))
    block_ids = jax.vmap(lambda own: jnp.searchsorted(jnp.cumsum(ragged_sizes(own, SEQLEN * 4 // (3 * BLOCK), SEQLEN, BLOCK, 1)), jnp.arange(SEQLEN), side="right"))(jax.random.split(streams_of[9], SEQS)).reshape((SEQS, SEQLEN)).astype(jnp.int32)
    tile_order = draw_tile_order(jax.random.fold_in(streams_of[11], 71), 0)
    return {"tokens_in": tokens_in, "w_query": w_query, "w_key": w_key, "w_value": w_value, "w_output": w_output, "w_gate": w_gate, "w_up": w_up, "w_down": w_down, "grad_out": grad_out, "block_ids": block_ids, "tile_order": tile_order}


@jax.custom_vjp
def low(v):
    return lax.optimization_barrier(v.astype(jnp.bfloat16)).astype(jnp.float32)

@jax.custom_vjp
def low_back(v):
    return v

def low_keep(v):
    return (low(v), None)

def low_pass(kept, grad):
    return (grad,)

def back_keep(v):
    return (v, None)

def back_low(kept, grad):
    return (low(grad),)
low.defvjp(low_keep, low_pass)
low_back.defvjp(back_keep, back_low)

def layer_norm(values):
    average = lax.optimization_barrier(jnp.mean(values, axis=-1, keepdims=True))
    centred = values - average
    return centred * lax.rsqrt(lax.optimization_barrier(jnp.mean(centred * centred, axis=-1, keepdims=True)) + 1e-05)

def matmul(left, right):
    return jnp.dot(left, right, precision=lax.Precision.HIGHEST, preferred_element_type=jnp.float32)

def tables(positions, head_width):
    inverse = 10000.0 ** (-jnp.arange(0, head_width, 2, dtype=jnp.float32) / head_width)
    angles = positions[:, None] * inverse[None, :]
    angles = jnp.concatenate([angles, angles], axis=-1)
    return (jnp.cos(angles), jnp.sin(angles))

def rotate(values, cosine, sine):
    middle = values.shape[-1] // 2
    turned = jnp.concatenate([-values[..., middle:], values[..., :middle]], axis=-1)
    return values * cosine[:, None, :] + turned * sine[:, None, :]

def attend(queries, query_blocks, keys, values, key_blocks):
    scaling = queries.shape[-1] ** (-0.5)
    raw = low_back(jnp.einsum('qhd,khd->hqk', queries, keys, precision=lax.Precision.HIGHEST) * scaling)
    masked = jnp.where(key_blocks[None, None, :] <= query_blocks[None, :, None], raw, -1e+30)
    row_max = lax.optimization_barrier(jnp.max(masked, axis=-1, keepdims=True))
    exponent = jnp.exp(masked - row_max)
    weights_soft = low(exponent / lax.optimization_barrier(jnp.sum(exponent, axis=-1, keepdims=True)))
    return jnp.einsum('hqk,khd->qhd', weights_soft, values, precision=lax.Precision.HIGHEST)

def by_sequence(values):
    shaped = values.reshape((N_CTX, SEQS, 2 * TILE) + values.shape[1:])
    return jnp.swapaxes(shaped, 0, 1).reshape((SEQS, SEQLEN) + values.shape[1:])

def from_sequence(values):
    shaped = values.reshape((SEQS, N_CTX, 2 * TILE) + values.shape[2:])
    return jnp.swapaxes(shaped, 0, 1).reshape((TOKENS,) + values.shape[2:])

def one_sequence(item):
    queries, keys, values, blocks = item
    block_rows = min(512, SEQLEN)
    block_count = SEQLEN // block_rows
    query_parts = (queries.reshape(block_count, block_rows, HEADS, HEAD_DIM), blocks.reshape(block_count, block_rows))
    outputs = lax.map(lambda part: jax.checkpoint(attend)(part[0], part[1], keys, values, blocks), query_parts)
    return outputs.reshape(SEQLEN, HEADS, HEAD_DIM)

def reference(tokens_in, w_query, w_key, w_value, w_output, w_gate, w_up, w_down, grad_out, block_ids, tile_order):
    row_ids = jnp.arange(TOKENS, dtype=jnp.int32)
    device_ids = row_ids // TOK_DEV
    within = row_ids % TOK_DEV
    sequence_ids = within // (2 * TILE)
    halves = within // TILE % 2
    offsets = row_ids % TILE
    pieces = tile_order[sequence_ids, 2 * device_ids + halves]
    positions = pieces * TILE + offsets
    blocks = block_ids[sequence_ids, positions]
    cosine, sine = tables(positions.astype(jnp.float32), HEAD_DIM)

    def forward(inputs, query_w, key_w, value_w, output_w, gate_w, up_w, down_w):
        normed = low(layer_norm(inputs))
        queries = low_back(matmul(normed, query_w)).reshape(TOKENS, HEADS, HEAD_DIM)
        queries = low(rotate(queries, cosine, sine))
        keys = low_back(matmul(normed, key_w)).reshape(TOKENS, HEADS, HEAD_DIM)
        keys = low(rotate(keys, cosine, sine))
        values = low(low_back(matmul(normed, value_w))).reshape(TOKENS, HEADS, HEAD_DIM)
        attended = lax.map(one_sequence, (by_sequence(queries), by_sequence(keys), by_sequence(values), by_sequence(blocks)))
        attended = low(low_back(from_sequence(attended).reshape(TOKENS, HEADS * HEAD_DIM)))
        middle = inputs + low_back(matmul(attended, output_w.T))
        second = low(layer_norm(middle))
        gate = low_back(matmul(second, gate_w))
        upper = low_back(matmul(second, up_w))
        hidden = low(jax.nn.silu(gate) * upper)
        return middle + matmul(hidden, down_w.T)
    floats = [w.astype(jnp.float32) for w in (tokens_in, w_query, w_key, w_value, w_output, w_gate, w_up, w_down)]
    result, pull_back = jax.vjp(forward, *floats)
    grads = pull_back(grad_out.astype(jnp.float32))
    return (result.astype(jnp.bfloat16), grads[0], grads[1], grads[2], grads[3], grads[4], grads[5], grads[6], grads[7])
```

```python
import functools

import jax
import jax.numpy as jnp
from jax import lax
from jax.experimental import pallas as pl
from jax.experimental.pallas import tpu as pltpu
from jax.sharding import PartitionSpec as P

HEAD = 128
NY, NZL, NX = 4, 2, 4
BOTH = ("ctx", "tp")
QB = 256
KC = 512
LOG2E = 1.4426950408889634
VMEM_LIMIT = 56 * 1024 * 1024
F32, BF16 = jnp.float32, jnp.bfloat16


def ctx_index(y, zl, x):
    return (y * NZL + zl) * NX + x


XY_GROUPS = [
    [ctx_index(y, zl, x) for y in range(NY) for x in range(NX)] for zl in range(NZL)
]
X_GROUPS = [
    [ctx_index(y, zl, x) for x in range(NX)] for y in range(NY) for zl in range(NZL)
]


def flip(values, zl=0, zh=0, co=0):
    pairs = []
    for y in range(NY):
        for a in range(NZL):
            for x in range(NX):
                for t in range(4):
                    here = ctx_index(y, a, x) * 4 + t
                    there = ctx_index(y, a ^ zl, x) * 4 + (t ^ (2 * zh + co))
                    pairs.append((here, there))
    return lax.ppermute(values, BOTH, pairs)


def ring(values, dx=0, dy=0):
    pairs = [
        (ctx_index(y, a, x), ctx_index((y + dy) % NY, a, (x + dx) % NX))
        for y in range(NY)
        for a in range(NZL)
        for x in range(NX)
    ]
    return lax.ppermute(values, "ctx", pairs)


def turn(values, axis, bit):
    return jnp.where(bit == 1, jnp.flip(values, axis), values)


def norm(values):
    average = jnp.mean(values, axis=-1, keepdims=True)
    centred = values - average
    inverse = lax.rsqrt(jnp.mean(centred * centred, axis=-1, keepdims=True) + 1e-05)
    return centred * inverse, inverse


def norm_back(grad, normed, inverse):
    first = jnp.mean(grad, axis=-1, keepdims=True)
    second = jnp.mean(grad * normed, axis=-1, keepdims=True)
    return inverse * (grad - first - normed * second)


def column_sum(keep, send, work=()):
    work = iter(work)

    def meanwhile(values, *sent):
        job = next(work, None)
        return values if job is None else hold(values, job(sent))

    rows = keep.shape[0] // 4
    cut = rows // 2
    got = flip(send, co=1)
    half = keep.astype(F32) + got.astype(F32)
    own, far, near, both = (half[k * rows : (k + 1) * rows] for k in range(4))
    low, high = far[:cut].astype(BF16), far[cut:].astype(BF16)
    for_both, for_near = flip(low, zl=1), flip(high, zl=1, zh=1)
    near = meanwhile(near, low, high)
    near = jnp.concatenate([near[:cut], near[cut:] + for_near.astype(F32)], axis=0).astype(BF16)
    both = jnp.concatenate([both[:cut] + for_both.astype(F32), both[cut:]], axis=0).astype(BF16)
    from_near, from_both = flip(near, zl=1), flip(both, zl=1, zh=1)
    return meanwhile(own, near, both) + from_near.astype(F32) + from_both.astype(F32)


def column_gather(rows, work=()):
    work = iter(work)

    def meanwhile(values, *sent):
        job = next(work, None)
        return values if job is None else hold(values, job(sent))

    cut = rows.shape[0] // 2
    near, both = flip(rows, zl=1), flip(rows, zl=1, zh=1)
    low, high = meanwhile(both[:cut], rows), near[cut:]
    far_low, far_high = flip(low, zl=1), flip(high, zl=1, zh=1)
    far_low = meanwhile(far_low, low, high)
    half = [rows, far_low, far_high, near, both]
    return half + [flip(piece, co=1) for piece in half]


def ring_sum(parts, **step):
    forth, back = step, {k: -v for k, v in step.items()}
    ahead, behind = ring(parts[2][0], **forth), ring(parts[2][1], **back)
    from_back, from_forth = ring(parts[1][1], **forth), ring(parts[3][0], **back)
    low = parts[1][0].astype(F32) + ahead.astype(F32)
    high = parts[3][1].astype(F32) + behind.astype(F32)
    low, high = ring(low.astype(BF16), **forth), ring(high.astype(BF16), **back)
    return (
        parts[0][0].astype(F32) + low.astype(F32) + from_forth.astype(F32),
        parts[0][1].astype(F32) + from_back.astype(F32) + high.astype(F32),
    )


def ring_gather(rows, **step):
    forth, back = step, {k: -v for k, v in step.items()}
    cut = rows.shape[0] // 2
    before, after = ring(rows, **forth), ring(rows, **back)
    return rows, after, ring(before[:cut], **forth), ring(after[cut:], **back), before


def plane_gather(rows):
    half = rows.shape[1] // 2
    own = rows[:, :half], rows[:, half:]
    lines = [[ring(own[w], **{axis: -k}) for k in (1, 2, 3)] for w, axis in enumerate(("dx", "dy"))]
    by_x, by_y = (
        jnp.concatenate([hold(own[w], lines[1 - w][1])] + lines[w], axis=0) for w in range(2)
    )
    cut = by_x.shape[0] // 2
    x_before, x_after = ring(by_x, dy=1), ring(by_x, dy=-1)
    y_before, y_after = ring(by_y, dx=1), ring(by_y, dx=-1)
    x_low, x_high = ring(hold(x_before[:cut], y_after), dy=1), ring(x_after[cut:], dy=-1)
    y_low, y_high = ring(hold(y_before[:cut], x_after), dx=1), ring(y_after[cut:], dx=-1)
    return (by_x, x_after, x_low, x_high, x_before), (by_y, y_after, y_low, y_high, y_before)


def dot(left, right):
    return jnp.dot(left, right, preferred_element_type=F32)


def dot_nt(left, right):
    return lax.dot_general(left, right, (((1,), (1,)), ((), ())), preferred_element_type=F32)


def dot_tn(left, right):
    return lax.dot_general(left, right, (((0,), (0,)), ((), ())), preferred_element_type=F32)


def call(kernel, name, outs, scalars, arrays, after=(), scratch=(), flops=1, specs=None):
    head, tail = len(scalars) + len(arrays), len(after)
    vmem = pl.BlockSpec(memory_space=pltpu.VMEM)
    specs = specs or {}
    grid = {"grid": (1,)} if specs else {}

    def body(*refs):
        kernel(*refs[:head], *refs[head + tail :])

    return pl.pallas_call(
        body,
        **grid,
        out_shape=tuple(jax.ShapeDtypeStruct(shape, dtype) for shape, dtype in outs),
        in_specs=[pl.BlockSpec(memory_space=pltpu.SMEM)] * len(scalars)
        + [specs.get(k, vmem) for k in range(len(arrays))]
        + [pl.BlockSpec(memory_space=pl.ANY)] * tail,
        out_specs=(vmem,) * len(outs),
        scratch_shapes=list(scratch),
        compiler_params=pltpu.CompilerParams(vmem_limit_bytes=VMEM_LIMIT),
        cost_estimate=pl.CostEstimate(flops=flops, bytes_accessed=1, transcendentals=0),
        name=name,
    )(*[jnp.stack(s).astype(jnp.int32) for s in scalars], *arrays, *after)


def hold(values, token):
    return values + (token.reshape(-1)[0] * 0).astype(values.dtype)


def put_rows(to_ref, refs):
    row = 0
    for ref in refs:
        to_ref[row : row + ref.shape[0], :] = ref[...]
        row += ref.shape[0]


def enter_kernel(at, x_ref, dy_ref, a_ref, dy_out, own_ref):
    tile = own_ref.shape[0]
    lane = lax.broadcasted_iota(jnp.int32, (tile, HEAD), 1)
    for k in range(4):
        row = ((k // 2) ^ at[0]) * 2 + ((k % 2) ^ at[1])
        rows = pl.ds(pl.multiple_of(row * tile, tile), tile)
        x = x_ref[rows, :].astype(F32)
        values = [(norm(x)[0], a_ref), (dy_ref[rows, :].astype(F32), dy_out)]
        if k == 0:
            values.append((x, own_ref))
        for value, to_ref in values:
            for y in range(NY):
                for half in range(NX // 2):
                    pair = [
                        value[:, c : c + HEAD]
                        for c in [(y * NZL + z) * NX * HEAD // 2 + half * HEAD for z in range(2)]
                    ]
                    turned = [pltpu.roll(v, HEAD // 2, 1) for v in pair]
                    low = jnp.where(lane < HEAD // 2, pair[0], turned[1])
                    high = jnp.where(lane < HEAD // 2, turned[0], pair[1])
                    for n, v in enumerate((low, high)):
                        c = (y * NX + 2 * half + n) * HEAD
                        to_ref[k * tile : (k + 1) * tile, c : c + HEAD] = v.astype(BF16)


def enter(co, zh, x, dy):
    rows, width = x.shape
    outs = [((rows, width), BF16)] * 2 + [((rows // 4, width), BF16)]
    return call(enter_kernel, "enter", outs, [(co, zh)], [x, dy])


def each_piece(pairs):
    own, after, low, high, before = pairs
    for dy in range(NY):
        for x in range(NX):
            ref = (own, after, (low, high)[x // 2], before)[dy]
            for k in range(4):
                yield (dy * NX + x) * 4 + k, x % 2 if dy == 2 else x, k, ref


def sort_pairs(scalars, pairs, keys, values, tile):
    for slot, x, k, ref in each_piece(pairs):
        rows = pl.ds(pl.multiple_of(scalars[slot] * tile, tile), tile)
        keys[rows, :] = ref[x, 0, k * tile : (k + 1) * tile]
        values[rows, :] = ref[x, 1, k * tile : (k + 1) * tile]


def attend_kernel(
    scalars, q_ref, kv0, kv1, kv2, kv3, kv4, qblk, kblk, o_ref, full_ref, lse_ref, keys, values, queries, *, tile
):
    tiles = keys.shape[0] // tile
    per = QB // tile
    blocks = q_ref.shape[0] // per
    factor = HEAD**-0.5 * LOG2E
    sort_pairs(scalars, (kv0, kv1, kv2, kv3, kv4), keys, values, tile)

    def block(i, carry):
        for k in range(per):
            queries[k * tile : (k + 1) * tile, :] = q_ref[scalars[tiles + i * per + k]]
        q_own = queries[...]
        rows = pl.ds(pl.multiple_of(i * QB, QB), QB)

        def chunk(c, state, masked):
            top, total, acc = state
            where = pl.ds(pl.multiple_of(c * KC, KC), KC)
            s = dot_nt(q_own, keys[where, :])
            if masked:
                s = jnp.where(qblk[rows, :] >= kblk[:, where], s, -1e30)
            new = jnp.maximum(top, jnp.max(s, axis=-1, keepdims=True))
            p = jnp.exp2((s - new) * factor)
            shrink = jnp.exp2((top - new) * factor)
            total = total * shrink + jnp.sum(p, axis=-1, keepdims=True)
            acc = acc * shrink + dot(p.astype(BF16), values[where, :])
            return new, total, acc

        base = tiles + blocks * per
        state = (
            jnp.full((QB, 1), -1e30, F32),
            jnp.zeros((QB, 1), F32),
            jnp.zeros((QB, HEAD), F32),
        )
        first, last = scalars[base + i], scalars[base + blocks + i]
        state = lax.fori_loop(0, first, functools.partial(chunk, masked=False), state)
        top, total, acc = lax.fori_loop(first, last, functools.partial(chunk, masked=True), state)
        out = acc / total
        full_ref[rows, :] = out
        low = out.astype(BF16)
        for k in range(per):
            o_ref[scalars[tiles + i * per + k]] = low[k * tile : (k + 1) * tile]
        lse = top * factor + jnp.log2(total)
        lse_ref[i] = jnp.transpose(jnp.broadcast_to(lse, (QB, HEAD)))[:8]
        return carry

    lax.fori_loop(0, blocks, block, 0)


def attend(scalars, q, kv, qblk, kblk, after):
    tile = q.shape[1]
    count = q.shape[0] * tile
    length = kblk.shape[1]
    vmem = pl.BlockSpec(memory_space=pltpu.VMEM)
    kernel = functools.partial(attend_kernel, tile=tile)

    def body(*refs):
        kernel(*refs[:9], *refs[9 + len(after) :])

    return pl.pallas_call(
        body,
        out_shape=(
            jax.ShapeDtypeStruct(q.shape, BF16),
            jax.ShapeDtypeStruct((count, HEAD), F32),
            jax.ShapeDtypeStruct((count // QB, 8, QB), F32),
        ),
        in_specs=[pl.BlockSpec(memory_space=pltpu.SMEM)]
        + [vmem] * 8
        + [pl.BlockSpec(memory_space=pl.ANY)] * len(after),
        out_specs=(vmem,) * 3,
        scratch_shapes=[
            pltpu.VMEM((length, HEAD), BF16),
            pltpu.VMEM((length, HEAD), BF16),
            pltpu.VMEM((QB, HEAD), BF16),
        ],
        compiler_params=pltpu.CompilerParams(vmem_limit_bytes=VMEM_LIMIT),
        cost_estimate=pl.CostEstimate(
            flops=4 * count * length * HEAD, bytes_accessed=1 << 22, transcendentals=count * length
        ),
        name="attend",
    )(scalars, q, *kv, qblk, kblk, *after)


def attend_back_kernel(
    scalars,
    q_ref,
    kv0,
    kv1,
    kv2,
    kv3,
    kv4,
    do_ref,
    full_ref,
    lse_ref,
    qblk,
    kblk,
    dq_ref,
    own_ref,
    after_low,
    after_high,
    far_low,
    far_high,
    before_low,
    before_high,
    keys,
    values,
    queries,
    grads,
    dk,
    dv,
    *,
    tile,
):
    tiles = keys.shape[0] // tile
    per = QB // tile
    blocks = q_ref.shape[0] // per
    scale = HEAD**-0.5
    factor = scale * LOG2E
    sort_pairs(scalars, (kv0, kv1, kv2, kv3, kv4), keys, values, tile)
    dk[...] = jnp.zeros_like(dk)
    dv[...] = jnp.zeros_like(dv)

    def block(i, carry):
        for k in range(per):
            slot = scalars[tiles + i * per + k]
            queries[k * tile : (k + 1) * tile, :] = q_ref[slot]
            grads[k * tile : (k + 1) * tile, :] = do_ref[slot]
        q_own = queries[...]
        do_own = grads[...]
        rows = pl.ds(pl.multiple_of(i * QB, QB), QB)
        product = do_own.astype(F32) * full_ref[rows, :]
        delta = jnp.sum(jnp.transpose(product), axis=0, keepdims=True)
        lse = lse_ref[i][:1]
        q_blocks = qblk[i][:1]

        def chunk(c, acc, masked):
            where = pl.ds(pl.multiple_of(c * KC, KC), KC)
            k_own = keys[where, :]
            s = dot_nt(k_own, q_own)
            if masked:
                s = jnp.where(kblk[where, :] <= q_blocks, s, -1e30)
            p = jnp.exp2(s * factor - lse)
            dp = dot_nt(values[where, :], do_own)
            ds = (p * (dp - delta)).astype(BF16)
            dv[where, :] += dot(p.astype(BF16), do_own)
            dk[where, :] += dot(ds, q_own)
            return acc + dot_tn(ds, k_own)

        base = tiles + blocks * per
        first, last = scalars[base + i], scalars[base + blocks + i]
        acc = jnp.zeros((QB, HEAD), F32)
        acc = lax.fori_loop(0, first, functools.partial(chunk, masked=False), acc)
        acc = lax.fori_loop(first, last, functools.partial(chunk, masked=True), acc)
        low = (acc * scale).astype(BF16)
        for k in range(per):
            dq_ref[scalars[tiles + i * per + k]] = low[k * tile : (k + 1) * tile]
        return carry

    lax.fori_loop(0, blocks, block, 0)

    outs = ((own_ref, own_ref), (after_low, after_high), (far_low, far_high), (before_low, before_high))
    for slot in range(tiles):
        dy, x, k = slot // 16, slot // 4 % 4, slot % 4
        rows = pl.ds(pl.multiple_of(scalars[slot] * tile, tile), tile)
        ref, x = outs[dy][x // 2], x if dy == 0 else x % 2
        here = slice(k * tile, (k + 1) * tile)
        ref[x, 0, here] = (dk[rows, :] * scale).astype(BF16)
        ref[x, 1, here] = dv[rows, :].astype(BF16)


def attend_back(scalars, q, kv, do, full, lse, qblk, kblk):
    tile = q.shape[1]
    count = q.shape[0] * tile
    length = kblk.shape[0]
    vmem = pl.BlockSpec(memory_space=pltpu.VMEM)
    return pl.pallas_call(
        functools.partial(attend_back_kernel, tile=tile),
        out_shape=(
            jax.ShapeDtypeStruct(q.shape, BF16),
            jax.ShapeDtypeStruct(kv[0].shape, BF16),
        )
        + (jax.ShapeDtypeStruct(kv[2].shape, BF16),) * 6,
        in_specs=[pl.BlockSpec(memory_space=pltpu.SMEM)] + [vmem] * 11,
        out_specs=(vmem,) * 8,
        scratch_shapes=[
            pltpu.VMEM((length, HEAD), BF16),
            pltpu.VMEM((length, HEAD), BF16),
            pltpu.VMEM((QB, HEAD), BF16),
            pltpu.VMEM((QB, HEAD), BF16),
            pltpu.VMEM((length, HEAD), F32),
            pltpu.VMEM((length, HEAD), F32),
        ],
        compiler_params=pltpu.CompilerParams(vmem_limit_bytes=VMEM_LIMIT),
        cost_estimate=pl.CostEstimate(
            flops=10 * count * length * HEAD, bytes_accessed=1 << 23, transcendentals=count * length
        ),
        name="attend_back",
    )(scalars, q, *kv, do, full, lse, qblk, kblk)


def project_kernel(at, own_ref, near_ref, other_ref, *refs):
    parts, (cos_ref, sin_ref, q_ref, kv_ref, w_ref, a_ref) = refs[:10], refs[10:]
    half = own_ref.shape[0]
    put_rows(
        a_ref, [own_ref.at[: half // 2], near_ref, own_ref.at[half // 2 :], other_ref]
    )
    y, x = at[0], at[1]
    for way in range(2):
        own, after, low, high, before = parts[5 * way : 5 * way + 5]
        columns = slice(way * w_ref.shape[1] // 2, (way + 1) * w_ref.shape[1] // 2)
        for second in range(4):
            for first in range(4):
                ref = (own, after, (low, high)[first // 2], before)[second]
                row = (first % 2 if second == 2 else first) * HEAD
                dy, dx = (second, first) if way == 0 else (first, second)
                block = ((y + dy) % NY) * NX + (x + dx) % NX
                rows = pl.ds(pl.multiple_of(block * HEAD, HEAD), HEAD)
                w_ref[rows, columns] = ref[row : row + HEAD, :]
    cosine, sine = cos_ref[...], sin_ref[...]
    for part in range(3):
        product = dot(a_ref[...], w_ref[:, part * 2 * HEAD : (part + 1) * 2 * HEAD])
        for head in range(2):
            u = product[:, head * HEAD : (head + 1) * HEAD]
            if part < 2:
                u = u * cosine + pltpu.roll(u, HEAD // 2, 1) * sine
            u = u.astype(BF16)
            for ds in range(2):
                rows = u[ds * half : (ds + 1) * half]
                if part == 0:
                    q_ref[head * 2 + ds] = rows
                else:
                    kv_ref[head * 2 + ds, part - 1] = rows


def project(y, x, a, parts, cosine, sine):
    half, width = a[0].shape
    columns = 2 * parts[0].shape[1]
    return call(
        project_kernel,
        "project",
        [
            ((4, half, HEAD), BF16),
            ((4, 2, half, HEAD), BF16),
            ((width, columns), BF16),
        ],
        [(y, x)],
        [*a, *parts, cosine, sine],
        scratch=[pltpu.VMEM((2 * half, width), BF16)],
        flops=4 * half * width * 6 * HEAD,
    )


def output_kernel(o_ref, w_ref, keep_ref, send_ref):
    half = keep_ref.shape[0]
    o = jnp.concatenate([o_ref[0], o_ref[1]], axis=1)
    for c in range(0, keep_ref.shape[1], 512):
        part = dot_nt(o, w_ref[c : c + 512, :]).astype(BF16)
        keep_ref[:, c : c + 512] = part[:half]
        send_ref[:, c : c + 512] = part[half:]


def output(o_heads, attn_w):
    rows, width = o_heads.shape[1], attn_w.shape[0]
    spec = pl.BlockSpec((width, 2 * HEAD), lambda i: (0, 3))
    outs = [((rows // 2, width), BF16)] * 2
    flops = 4 * rows * width * HEAD
    return call(output_kernel, "output", outs, [], [o_heads, attn_w], flops=flops, specs={1: spec})


def mlp_kernel(*refs):
    b_parts, dy_parts = refs[:10], refs[10:13]
    w_ref, keep_ref, send_ref, dg_ref, du_ref, hidden_ref, b_ref, dy_ref = refs[13:]
    put_rows(b_ref, b_parts)
    half = dy_parts[0].shape[0]
    own, near, other = dy_parts
    put_rows(dy_ref, [own.at[: half // 2], near, own.at[half // 2 :], other])
    units = dg_ref.shape[1]
    for j in range(0, units, 256):
        here = slice(j, j + 256)
        gate = dot(b_ref[...], w_ref[:, j : j + 256])
        upper = dot(b_ref[...], w_ref[:, units + j : units + j + 256])
        grad = dot(dy_ref[...], w_ref[:, 2 * units + j : 2 * units + j + 256])
        sigmoid = 1.0 / (1.0 + jnp.exp(-gate))
        swish = gate * sigmoid
        hidden_ref[:, here] = (swish * upper).astype(BF16)
        du_ref[:, here] = (grad * swish).astype(BF16)
        dg_ref[:, here] = (grad * upper * sigmoid * (1.0 + gate * (1.0 - sigmoid))).astype(BF16)
    for c in range(0, keep_ref.shape[1], 512):
        part = dot_nt(dg_ref[...], w_ref[c : c + 512, :units])
        part = part + dot_nt(du_ref[...], w_ref[c : c + 512, units : 2 * units])
        part = part.astype(BF16)
        keep_ref[:, c : c + 512] = part[:half]
        send_ref[:, c : c + 512] = part[half:]


def mlp(b_parts, dy_parts, mlp_w):
    half, width = dy_parts[0].shape
    units = mlp_w.shape[1] // 3
    return call(
        mlp_kernel,
        "mlp",
        [((half, width), BF16)] * 2 + [((2 * half, units), BF16)] * 3,
        [],
        [*b_parts, *dy_parts, mlp_w],
        scratch=[pltpu.VMEM((2 * half, width), BF16)] * 2,
        flops=20 * half * width * units,
    )


def down_kernel(hidden_ref, w_ref, keep_ref, send_ref):
    half = keep_ref.shape[0]
    for c in range(0, keep_ref.shape[1], 512):
        part = dot_nt(hidden_ref[...], w_ref[c : c + 512, :]).astype(BF16)
        keep_ref[:, c : c + 512] = part[:half]
        send_ref[:, c : c + 512] = part[half:]


def down(hidden, mlp_w, after):
    (rows, units), width = hidden.shape, mlp_w.shape[0]
    spec = pl.BlockSpec((width, units), lambda i: (0, 2))
    outs = [((rows // 2, width), BF16)] * 2
    flops = 2 * rows * width * units
    return call(down_kernel, "down", outs, [], [hidden, mlp_w], after, flops=flops, specs={1: spec})


def grads_kernel(*refs, count, sources):
    lefts, (right_ref, out_ref, left_ref, turned) = refs[:count], refs[-4:]
    step = pl.program_id(0)

    def put():
        if sources is None:
            put_rows(left_ref, lefts)
        else:
            half = lefts[0].shape[0]
            own, near, other = lefts
            put_rows(left_ref, [own.at[: half // 2], near, own.at[half // 2 :], other])
        for r in range(0, turned.shape[0], 256):
            turned[r : r + 256, :] = jnp.transpose(left_ref[:, r : r + 256])

    pl.when(step == 0)(put)
    blocks = out_ref.shape[1]
    if len(right_ref.shape) == 3:
        right = jnp.concatenate([right_ref[k] for k in range(blocks)], axis=1)
    else:
        right = right_ref[...]
    for r in range(0, turned.shape[0], 256):
        product = dot(turned[r : r + 256, :], right).astype(BF16)
        for k in range(2):
            for c in range(blocks):
                out_ref[r // HEAD + k, c] = product[
                    k * HEAD : (k + 1) * HEAD, c * HEAD : (c + 1) * HEAD
                ]


def weight_grads(name, left, right, whole, first, total, after=()):
    width = left[0].shape[1]
    pairs = len(left) == 3
    tokens = sum(v.shape[0] for v in left)
    if right.ndim == 3:
        blocks, steps = right.shape[0], 1
        right_spec = pl.BlockSpec(right.shape, lambda i: (0, 0, 0))
    else:
        blocks = 4
        steps = right.shape[1] // (blocks * HEAD)
        right_spec = pl.BlockSpec((tokens, blocks * HEAD), lambda i: (0, i))
    vmem = pl.BlockSpec(memory_space=pltpu.VMEM)
    anywhere = pl.BlockSpec(memory_space=pl.ANY)
    before = list(after) + ([] if whole is None else [whole])
    kernel = functools.partial(
        grads_kernel, count=len(left), sources="pairs" if pairs else None
    )

    def body(*refs):
        kernel(*refs[: len(left) + 1], *refs[len(left) + 1 + len(before) :])

    return pl.pallas_call(
        body,
        grid=(steps,),
        out_shape=jax.ShapeDtypeStruct((width // HEAD, total, HEAD, HEAD), BF16),
        in_specs=[vmem] * len(left) + [right_spec] + [anywhere] * len(before),
        out_specs=pl.BlockSpec(
            (width // HEAD, blocks, HEAD, HEAD), lambda i: (0, first // blocks + i, 0, 0)
        ),
        scratch_shapes=[pltpu.VMEM((tokens, width), BF16), pltpu.VMEM((width, tokens), BF16)],
        input_output_aliases={} if whole is None else {len(left) + len(before): 0},
        compiler_params=pltpu.CompilerParams(vmem_limit_bytes=VMEM_LIMIT),
        cost_estimate=pl.CostEstimate(
            flops=tokens * width * blocks * steps * HEAD // 2, bytes_accessed=1, transcendentals=0
        ),
        name=name,
    )(*left, right, *before)


def outward_kernel(*refs):
    parts, (w_ref, do_ref, m_ref) = refs[:10], refs[10:]
    put_rows(m_ref, parts)
    part = dot(m_ref[...], w_ref[...]).astype(BF16)
    half = part.shape[0] // 2
    for head in range(2):
        for ds in range(2):
            do_ref[head * 2 + ds] = part[
                ds * half : (ds + 1) * half, head * HEAD : (head + 1) * HEAD
            ]


def outward(m_parts, attn_w):
    width = attn_w.shape[0]
    half = sum(v.shape[0] for v in m_parts) // 2
    spec = pl.BlockSpec((width, 2 * HEAD), lambda i: (0, 3))
    return call(
        outward_kernel,
        "outward",
        [((4, half, HEAD), BF16)],
        [],
        [*m_parts, attn_w],
        scratch=[pltpu.VMEM((2 * half, width), BF16)],
        flops=8 * half * width * HEAD,
        specs={len(m_parts): spec},
    )[0]


def back_kernel(dq_ref, dkv_ref, cos_ref, sin_ref, w_ref, keep_ref, send_ref, back_ref):
    half = dq_ref.shape[1]
    cosine, sine = cos_ref[...], sin_ref[...]
    for part in range(3):
        for head in range(2):
            for ds in range(2):
                unit = head * 2 + ds
                rows = slice(ds * half, (ds + 1) * half)
                if part == 0:
                    e = dq_ref[unit].astype(F32)
                else:
                    e = dkv_ref[unit, part - 1].astype(F32)
                if part < 2:
                    e = e * cosine[rows] - pltpu.roll(e, HEAD // 2, 1) * sine[rows]
                back_ref[part * 2 + head, rows] = e.astype(BF16)
    back = jnp.concatenate([back_ref[k] for k in range(6)], axis=1)
    for c in range(0, keep_ref.shape[1], 512):
        part = dot_nt(back, w_ref[c : c + 512, :]).astype(BF16)
        keep_ref[:, c : c + 512] = part[:half]
        send_ref[:, c : c + 512] = part[half:]


def backward(dq, dkv, cosine, sine, attn_w, after):
    half, width = dq.shape[1], attn_w.shape[0]
    spec = pl.BlockSpec((width, 6 * HEAD), lambda i: (0, 0))
    return call(
        back_kernel,
        "backward",
        [((half, width), BF16)] * 2 + [((6, 2 * half, HEAD), BF16)],
        [],
        [dq, dkv, cosine, sine, attn_w],
        after,
        flops=24 * half * width * HEAD,
        specs={4: spec},
    )


def total_kernel(at, terms_ref, keep_ref, send_ref):
    rows = keep_ref.shape[1]
    for c in range(keep_ref.shape[0]):
        total = terms_ref[0, c].astype(F32)
        for p in range(1, terms_ref.shape[0]):
            total = total + terms_ref[p, c].astype(F32)
        first, second = total[:rows], total[rows:]
        keep_ref[c] = jnp.where(at[0] == 0, first, second).astype(BF16)
        send_ref[c] = jnp.where(at[0] == 0, second, first).astype(BF16)


def total(zl, terms, after=()):
    outs = [((terms.shape[1], HEAD // 2, HEAD), BF16)] * 2
    return call(total_kernel, "total", outs, [(zl,)], [terms], after)


def place_kernel(at, keep_ref, got_ref, *outs):
    block = 0
    for out_ref in outs:
        half = out_ref.shape[1] // 2
        for c in range(0, half, HEAD):
            keep, got = keep_ref[block].astype(F32), got_ref[block].astype(F32)
            out_ref[:, c : c + HEAD] = jnp.where(at[0] == 0, keep, got)
            out_ref[:, half + c : half + c + HEAD] = jnp.where(at[0] == 0, got, keep)
            block += 1


def place(zl, sums, widths, after=()):
    keep, send = total(zl, sums, after)
    outs = [((HEAD // 2, 2 * w), F32) for w in widths]
    return call(place_kernel, "place", outs, [(zl,)], [keep, flip(send, zl=1)])


def finish_kernel(at, own_ref, far_ref, pair_ref, out_ref):
    tile = own_ref.shape[0]
    co, zh = at[0], at[1]
    lane = lax.broadcasted_iota(jnp.int32, (tile, HEAD), 1)
    for k in range(4):
        ref, start = ((own_ref, 0), (far_ref, 0), (pair_ref, 0), (pair_ref, tile))[k]
        at_row = ((k // 2) ^ co) * 2 + ((k % 2) ^ zh)
        rows = pl.ds(pl.multiple_of(at_row * tile, tile), tile)
        for y in range(NY):
            for half in range(NX // 2):
                pair = [
                    ref[start : start + tile, c : c + HEAD].astype(F32)
                    for c in ((y * NX + 2 * half) * HEAD, (y * NX + 2 * half + 1) * HEAD)
                ]
                turned = [pltpu.roll(v, HEAD // 2, 1) for v in pair]
                low = jnp.where(lane < HEAD // 2, pair[0], turned[1])
                high = jnp.where(lane < HEAD // 2, turned[0], pair[1])
                for zl, value in enumerate((low, high)):
                    column = (y * NZL + zl) * NX * HEAD // 2 + half * HEAD
                    out_ref[rows, column : column + HEAD] = value.astype(out_ref.dtype)


def finish(co, zh, own, dtype):
    far = flip(own, zh=1)
    pair = flip(jnp.concatenate([own, far], axis=0), co=1)
    vmem = pl.BlockSpec(memory_space=pltpu.VMEM)
    return pl.pallas_call(
        finish_kernel,
        out_shape=jax.ShapeDtypeStruct((4 * own.shape[0], own.shape[1]), dtype),
        in_specs=[pl.BlockSpec(memory_space=pltpu.SMEM)] + [vmem] * 3,
        out_specs=vmem,
        compiler_params=pltpu.CompilerParams(vmem_limit_bytes=VMEM_LIMIT),
        cost_estimate=pl.CostEstimate(flops=1, bytes_accessed=1, transcendentals=0),
        name="finish",
    )(jnp.stack([co, zh]).astype(jnp.int32), own, far, pair)


def local(
    tokens_in,
    w_query,
    w_key,
    w_value,
    w_output,
    w_gate,
    w_up,
    w_down,
    grad_out,
    block_ids,
    tile_order,
):
    own, width = tokens_in.shape
    seqs, length = block_ids.shape
    tile = length // tile_order.shape[1]
    wide = w_query.shape[1] // 2
    units = w_gate.shape[1] // 2
    piece = w_query.shape[0]
    ctx, tp = lax.axis_index("ctx"), lax.axis_index("tp")
    y, zl, x = ctx // (NZL * NX), (ctx // NX) % NZL, ctx % NX
    zh, co = tp // 2, tp % 2

    def pair_rows(arrays):
        def cut(array, which):
            half = array.shape[1] // 2
            return lax.dynamic_slice_in_dim(array, which * half, half, 1)

        kept = jnp.concatenate([cut(array, zl) for array in arrays], axis=1)
        sent = jnp.concatenate([cut(array, 1 - zl) for array in arrays], axis=1)
        return turn(jnp.stack([kept, flip(sent, zl=1)]), 0, zl).reshape(2 * piece, -1)

    first_own, grads, x_own = enter(co, zh, tokens_in, grad_out)
    pair = pair_rows((w_query, w_key, w_value, w_output))
    by_x, by_y = plane_gather(pair)
    near = flip(hold(first_own[: own // 2], pair), zl=1)
    first_low = [first_own, near, flip(near, co=1)]
    pair = pair_rows([hold(w, near) for w in (w_gate, w_up, w_down)])

    tiles = tile_order.reshape(seqs, NY, NZL, NX, 2)
    tiles = turn(turn(turn(tiles, 0, co), 2, zl), 4, zh)
    row_tiles = lax.dynamic_index_in_dim(tiles, y, 1, keepdims=False)
    own_tiles = lax.dynamic_index_in_dim(row_tiles, x, 2, keepdims=False).reshape(-1)
    positions = (own_tiles[:, None] * tile + jnp.arange(tile, dtype=jnp.int32)).reshape(-1)
    inverse = 10000.0 ** (-jnp.arange(0, HEAD, 2, dtype=F32) / HEAD)
    angles = positions.astype(F32)[:, None] * inverse[None, :]
    cosine = jnp.concatenate([jnp.cos(angles)] * 2, axis=-1)
    sine = jnp.concatenate([-jnp.sin(angles), jnp.sin(angles)], axis=-1)
    ds_own = x % 2
    unit_tiles = lax.dynamic_index_in_dim(tiles, ds_own, 0, keepdims=False)
    turns = (y + jnp.arange(NY, dtype=jnp.int32)) % NY
    key_tiles = jnp.swapaxes(jnp.take(unit_tiles, turns, axis=0), 1, 2).reshape(-1)
    query_tiles = lax.dynamic_index_in_dim(unit_tiles, y, 0, keepdims=False)
    query_tiles = jnp.swapaxes(query_tiles, 0, 1).reshape(-1)
    tile_count, query_count = key_tiles.shape[0], query_tiles.shape[0]
    rank = jnp.sum(query_tiles[None, :] < query_tiles[:, None], axis=1)
    places = jnp.arange(query_count, dtype=jnp.int32)
    order = jnp.sum(
        jnp.where(rank[None, :] == places[:, None], places[None, :], 0), axis=1
    ).astype(jnp.int32)
    sorted_tiles = jnp.sum(
        jnp.where(rank[None, :] == places[:, None], query_tiles[None, :], 0), axis=1
    )
    key_blocks = lax.dynamic_index_in_dim(block_ids, ds_own ^ co, 0, keepdims=False)
    query_blocks = jnp.take(key_blocks.reshape(tile_count, tile), sorted_tiles, axis=0).reshape(-1)
    by_block = query_blocks.reshape(-1, QB)
    sure = jnp.sum(key_blocks[None, :] <= by_block[:, :1], axis=1) // KC
    most = (jnp.sum(key_blocks[None, :] <= by_block[:, -1:], axis=1) + KC - 1) // KC
    scalars = jnp.concatenate([key_tiles, order, sure, most]).astype(jnp.int32)
    query_rows = jnp.broadcast_to(by_block[:, None, :], (by_block.shape[0], 8, QB))

    q_send, kv_send, attn_w = project(y, x, first_low, by_x + by_y, cosine, sine)
    half = own

    def across(values):
        return lax.all_to_all(values, "ctx", 0, 0, tiled=True, axis_index_groups=X_GROUPS)

    kv = ring_gather(across(kv_send), dy=1)
    mlp_w = lax.all_gather(
        hold(pair, kv[3]), "ctx", axis=0, tiled=True, axis_index_groups=XY_GROUPS
    )
    q = across(q_send).reshape(query_count, tile, HEAD)
    near = flip(hold(grads[: own // 2], q_send), zl=1)
    grad_all = [grads, near, flip(near, co=1)]
    o, o_full, lse = attend(
        scalars, q, kv, query_blocks[:, None], key_blocks[None, :], [grad_all[2]]
    )
    o_heads = across(o.reshape(NX, half, HEAD)).reshape(2, 2 * half, HEAD)
    attn_sum = column_sum(*output(o_heads, attn_w))

    x_own = x_own.astype(F32)
    dy_own = grads[:tile].astype(F32)
    middle = x_own + attn_sum
    normed_two, inverse_two = norm(middle)
    second_low = column_gather(normed_two.astype(BF16))
    keep, send, grad_gate, grad_up, hidden = mlp(second_low, grad_all, mlp_w)
    count, many = wide // HEAD, units // HEAD
    made = []

    def job(name, left, right):
        def run(after):
            whole = made[-1] if made else None
            made.append(
                weight_grads(name, left, right, whole, len(made) * many, 3 * many, after)
            )
            return made[-1]

        return run

    jobs = [
        job("grad_gate", second_low, grad_gate),
        job("grad_up", second_low, grad_up),
        job("grad_down", grad_all, hidden),
    ]
    back_two = column_sum(keep, send, jobs[:2])
    grad_middle = dy_own + norm_back(back_two, normed_two, inverse_two)
    parts = []

    def down_job(after):
        parts.extend(down(hidden, mlp_w, after))
        return parts[0]

    middle_low = column_gather(grad_middle.astype(BF16), [jobs[2], down_job])
    sums = lax.psum_scatter(
        made[-1], "ctx", scatter_dimension=0, tiled=True, axis_index_groups=XY_GROUPS
    )

    do_send = outward(middle_low, attn_w)
    do = across(do_send).reshape(query_count, tile, HEAD)
    dq, dkv, *others = attend_back(
        scalars, q, kv, do, o_full, lse, query_rows, key_blocks[:, None]
    )
    out_terms = weight_grads("grad_output", middle_low, o_heads, None, 0, count, [dq])
    out_terms = lax.all_to_all(
        out_terms, "ctx", 0, 0, tiled=True, axis_index_groups=XY_GROUPS
    )
    pairs = [(dkv[:2], dkv[2:])] + [tuple(others[2 * k : 2 * k + 2]) for k in range(3)]
    dkv = jnp.concatenate(ring_sum(pairs, dy=1), axis=0).astype(BF16)
    out_sum = column_sum(hold(parts[0], dq), hold(parts[1], dq))
    dq = across(dq.reshape(NX, half, HEAD))
    dkv = across(hold(dkv, out_terms))
    out_low = (middle + out_sum).astype(BF16)
    keep, send, back = backward(dq, dkv, cosine, sine, attn_w, [out_low])
    back_one = column_sum(keep, send)
    normed_own, inverse_own = norm(x_own)
    grad_own = grad_middle + norm_back(back_one, normed_own, inverse_own)
    grad_in = finish(co, zh, grad_own.astype(BF16), F32)
    tokens_out = finish(co, zh, out_low, BF16)
    terms = weight_grads("grad_qkv", first_low, back, None, 0, 3 * count)
    terms = lax.all_to_all(terms, "ctx", 0, 0, tiled=True, axis_index_groups=XY_GROUPS)
    mlp_out = place(zl, sums, (units,) * 3, [dq])
    return (
        tokens_out,
        grad_in,
        *place(zl, terms, (wide,) * 3, [grad_in, tokens_out, mlp_out[0]]),
        *place(zl, out_terms, (wide,), [dq]),
        *mlp_out,
    )


def solution(mesh):
    row, both = P("ctx", None), P("ctx", "tp")
    return jax.shard_map(
        local,
        mesh=mesh,
        in_specs=(row,) + (both,) * 7 + (row, P(), P()),
        out_specs=(row, row) + (both,) * 7,
        check_vma=False,
    )
```

```python
import functools

import jax
import jax.numpy as jnp
from jax import lax
from jax.experimental import pallas as pl
from jax.experimental.pallas import tpu as pltpu
from jax.sharding import PartitionSpec as P

HEAD = 128
NY, NZL, NX = 4, 2, 4
BOTH = ("ctx", "tp")
QB = 256
KC = 512
LOG2E = 1.4426950408889634
VMEM_LIMIT = 56 * 1024 * 1024
F32, BF16 = jnp.float32, jnp.bfloat16


def ctx_index(y, zl, x):
    return (y * NZL + zl) * NX + x


XY_GROUPS = [
    [ctx_index(y, zl, x) for y in range(NY) for x in range(NX)] for zl in range(NZL)
]
X_GROUPS = [
    [ctx_index(y, zl, x) for x in range(NX)] for y in range(NY) for zl in range(NZL)
]


def flip(values, zl=0, zh=0, co=0):
    pairs = []
    for y in range(NY):
        for a in range(NZL):
            for x in range(NX):
                for t in range(4):
                    here = ctx_index(y, a, x) * 4 + t
                    there = ctx_index(y, a ^ zl, x) * 4 + (t ^ (2 * zh + co))
                    pairs.append((here, there))
    return lax.ppermute(values, BOTH, pairs)


def ring(values, dx=0, dy=0):
    pairs = [
        (ctx_index(y, a, x), ctx_index((y + dy) % NY, a, (x + dx) % NX))
        for y in range(NY)
        for a in range(NZL)
        for x in range(NX)
    ]
    return lax.ppermute(values, "ctx", pairs)


def turn(values, axis, bit):
    return jnp.where(bit == 1, jnp.flip(values, axis), values)


def norm(values):
    average = jnp.mean(values, axis=-1, keepdims=True)
    centred = values - average
    inverse = lax.rsqrt(jnp.mean(centred * centred, axis=-1, keepdims=True) + 1e-05)
    return centred * inverse, inverse


def norm_back(grad, normed, inverse):
    first = jnp.mean(grad, axis=-1, keepdims=True)
    second = jnp.mean(grad * normed, axis=-1, keepdims=True)
    return inverse * (grad - first - normed * second)


def column_sum(keep, send, token=None):
    rows = keep.shape[0] // 4
    cut = rows // 2
    got = flip(send, co=1)
    half = keep.astype(F32) + got.astype(F32)
    if token is not None:
        half = hold(half, token)
    own, far, near, both = (half[k * rows : (k + 1) * rows] for k in range(4))
    for_both = flip(far[:cut].astype(BF16), zl=1)
    for_near = flip(far[cut:].astype(BF16), zl=1, zh=1)
    near = jnp.concatenate([near[:cut], near[cut:] + for_near.astype(F32)], axis=0).astype(BF16)
    both = jnp.concatenate([both[:cut] + for_both.astype(F32), both[cut:]], axis=0).astype(BF16)
    from_near, from_both = flip(near, zl=1), flip(both, zl=1, zh=1)
    return own + from_near.astype(F32) + from_both.astype(F32)


def column_gather(rows):
    cut = rows.shape[0] // 2
    near, both = flip(rows, zl=1), flip(rows, zl=1, zh=1)
    far_low, far_high = flip(both[:cut], zl=1), flip(near[cut:], zl=1, zh=1)
    half = [rows, far_low, far_high, near, both]
    return half + [flip(piece, co=1) for piece in half]


def ring_sum(parts, **step):
    forth, back = step, {k: -v for k, v in step.items()}
    ahead, behind = ring(parts[2][0], **forth), ring(parts[2][1], **back)
    from_back, from_forth = ring(parts[1][1], **forth), ring(parts[3][0], **back)
    low = parts[1][0].astype(F32) + ahead.astype(F32)
    high = parts[3][1].astype(F32) + behind.astype(F32)
    low, high = ring(low.astype(BF16), **forth), ring(high.astype(BF16), **back)
    return (
        parts[0][0].astype(F32) + low.astype(F32) + from_forth.astype(F32),
        parts[0][1].astype(F32) + from_back.astype(F32) + high.astype(F32),
    )


def ring_gather(rows, tokens, **step):
    forth, back = step, {k: -v for k, v in step.items()}
    cut = rows.shape[0] // 2
    before, after = ring(rows, **forth), ring(rows, **back)
    low, high = before[:cut], after[cut:]
    for one in tokens:
        low, high = hold(low, one), hold(high, one)
    low, high = ring(low, **forth), ring(high, **back)
    return rows, after, low, high, before


def plane_copies(rows):
    return jnp.broadcast_to(rows[None], (NY * NX,) + rows.shape)


def plane_gather(copies):
    every = lax.all_to_all(copies, "ctx", 0, 0, tiled=True, axis_index_groups=XY_GROUPS)
    return every.reshape(-1, copies.shape[2])


def dot(left, right):
    return jnp.dot(left, right, preferred_element_type=F32)


def dot_nt(left, right):
    return lax.dot_general(left, right, (((1,), (1,)), ((), ())), preferred_element_type=F32)


def dot_tn(left, right):
    return lax.dot_general(left, right, (((0,), (0,)), ((), ())), preferred_element_type=F32)


def call(kernel, name, outs, scalars, arrays, after=(), scratch=(), flops=1, specs=None):
    head, tail = len(scalars) + len(arrays), len(after)
    vmem = pl.BlockSpec(memory_space=pltpu.VMEM)
    specs = specs or {}
    grid = {"grid": (1,)} if specs else {}

    def body(*refs):
        kernel(*refs[:head], *refs[head + tail :])

    return pl.pallas_call(
        body,
        **grid,
        out_shape=tuple(jax.ShapeDtypeStruct(shape, dtype) for shape, dtype in outs),
        in_specs=[pl.BlockSpec(memory_space=pltpu.SMEM)] * len(scalars)
        + [specs.get(k, vmem) for k in range(len(arrays))]
        + [pl.BlockSpec(memory_space=pl.ANY)] * tail,
        out_specs=(vmem,) * len(outs),
        scratch_shapes=list(scratch),
        compiler_params=pltpu.CompilerParams(vmem_limit_bytes=VMEM_LIMIT),
        cost_estimate=pl.CostEstimate(flops=flops, bytes_accessed=1, transcendentals=0),
        name=name,
    )(*[jnp.stack(s).astype(jnp.int32) for s in scalars], *arrays, *after)


def hold(values, token):
    return values + (token.reshape(-1)[0] * 0).astype(values.dtype)


def put_rows(to_ref, refs):
    row = 0
    for ref in refs:
        to_ref[row : row + ref.shape[0], :] = ref[...]
        row += ref.shape[0]


def enter_kernel(at, x_ref, dy_ref, a_ref, dy_out, own_ref):
    tile = own_ref.shape[0]
    lane = lax.broadcasted_iota(jnp.int32, (tile, HEAD), 1)
    for k in range(4):
        row = ((k // 2) ^ at[0]) * 2 + ((k % 2) ^ at[1])
        rows = pl.ds(pl.multiple_of(row * tile, tile), tile)
        x = x_ref[rows, :].astype(F32)
        values = [(norm(x)[0], a_ref), (dy_ref[rows, :].astype(F32), dy_out)]
        if k == 0:
            values.append((x, own_ref))
        for value, to_ref in values:
            for y in range(NY):
                for half in range(NX // 2):
                    pair = [
                        value[:, c : c + HEAD]
                        for c in [(y * NZL + z) * NX * HEAD // 2 + half * HEAD for z in range(2)]
                    ]
                    turned = [pltpu.roll(v, HEAD // 2, 1) for v in pair]
                    low = jnp.where(lane < HEAD // 2, pair[0], turned[1])
                    high = jnp.where(lane < HEAD // 2, turned[0], pair[1])
                    for n, v in enumerate((low, high)):
                        c = (y * NX + 2 * half + n) * HEAD
                        to_ref[k * tile : (k + 1) * tile, c : c + HEAD] = v.astype(BF16)


def enter(co, zh, x, dy, after):
    rows, width = x.shape
    outs = [((rows, width), BF16)] * 2 + [((rows // 4, width), BF16)]
    return call(enter_kernel, "enter", outs, [(co, zh)], [x, dy], after)


def each_piece(pairs):
    own, after, low, high, before = pairs
    for dy in range(NY):
        for x in range(NX):
            ref = (own, after, (low, high)[x // 2], before)[dy]
            for k in range(4):
                yield (dy * NX + x) * 4 + k, x % 2 if dy == 2 else x, k, ref


def sort_pairs(scalars, pairs, keys, values, tile):
    for slot, x, k, ref in each_piece(pairs):
        rows = pl.ds(pl.multiple_of(scalars[slot] * tile, tile), tile)
        keys[rows, :] = ref[x, 0, k * tile : (k + 1) * tile]
        values[rows, :] = ref[x, 1, k * tile : (k + 1) * tile]


def attend_kernel(
    scalars, q_ref, kv0, kv1, kv2, kv3, kv4, qblk, kblk, o_ref, full_ref, lse_ref, keys, values, queries, *, tile
):
    tiles = keys.shape[0] // tile
    per = QB // tile
    blocks = q_ref.shape[0] // per
    factor = HEAD**-0.5 * LOG2E
    sort_pairs(scalars, (kv0, kv1, kv2, kv3, kv4), keys, values, tile)

    def block(i, carry):
        for k in range(per):
            queries[k * tile : (k + 1) * tile, :] = q_ref[scalars[tiles + i * per + k]]
        q_own = queries[...]
        rows = pl.ds(pl.multiple_of(i * QB, QB), QB)

        def chunk(c, state, masked):
            top, total, acc = state
            where = pl.ds(pl.multiple_of(c * KC, KC), KC)
            s = dot_nt(q_own, keys[where, :])
            if masked:
                s = jnp.where(qblk[rows, :] >= kblk[:, where], s, -1e30)
            new = jnp.maximum(top, jnp.max(s, axis=-1, keepdims=True))
            p = jnp.exp2((s - new) * factor)
            shrink = jnp.exp2((top - new) * factor)
            total = total * shrink + jnp.sum(p, axis=-1, keepdims=True)
            acc = acc * shrink + dot(p.astype(BF16), values[where, :])
            return new, total, acc

        base = tiles + blocks * per
        state = (
            jnp.full((QB, 1), -1e30, F32),
            jnp.zeros((QB, 1), F32),
            jnp.zeros((QB, HEAD), F32),
        )
        first, last = scalars[base + i], scalars[base + blocks + i]
        state = lax.fori_loop(0, first, functools.partial(chunk, masked=False), state)
        top, total, acc = lax.fori_loop(first, last, functools.partial(chunk, masked=True), state)
        out = acc / total
        full_ref[rows, :] = out
        low = out.astype(BF16)
        for k in range(per):
            o_ref[scalars[tiles + i * per + k]] = low[k * tile : (k + 1) * tile]
        lse = top * factor + jnp.log2(total)
        lse_ref[i] = jnp.transpose(jnp.broadcast_to(lse, (QB, HEAD)))[:8]
        return carry

    lax.fori_loop(0, blocks, block, 0)


def attend(scalars, q, kv, qblk, kblk, after):
    tile = q.shape[1]
    count = q.shape[0] * tile
    length = kblk.shape[1]
    vmem = pl.BlockSpec(memory_space=pltpu.VMEM)
    kernel = functools.partial(attend_kernel, tile=tile)

    def body(*refs):
        kernel(*refs[:9], *refs[9 + len(after) :])

    return pl.pallas_call(
        body,
        out_shape=(
            jax.ShapeDtypeStruct(q.shape, BF16),
            jax.ShapeDtypeStruct((count, HEAD), F32),
            jax.ShapeDtypeStruct((count // QB, 8, QB), F32),
        ),
        in_specs=[pl.BlockSpec(memory_space=pltpu.SMEM)]
        + [vmem] * 8
        + [pl.BlockSpec(memory_space=pl.ANY)] * len(after),
        out_specs=(vmem,) * 3,
        scratch_shapes=[
            pltpu.VMEM((length, HEAD), BF16),
            pltpu.VMEM((length, HEAD), BF16),
            pltpu.VMEM((QB, HEAD), BF16),
        ],
        compiler_params=pltpu.CompilerParams(vmem_limit_bytes=VMEM_LIMIT),
        cost_estimate=pl.CostEstimate(
            flops=4 * count * length * HEAD, bytes_accessed=1 << 22, transcendentals=count * length
        ),
        name="attend",
    )(scalars, q, *kv, qblk, kblk, *after)


def attend_back_kernel(
    scalars,
    q_ref,
    kv0,
    kv1,
    kv2,
    kv3,
    kv4,
    do_ref,
    full_ref,
    lse_ref,
    qblk,
    kblk,
    dq_ref,
    own_ref,
    after_low,
    after_high,
    far_low,
    far_high,
    before_low,
    before_high,
    keys,
    values,
    queries,
    grads,
    dk,
    dv,
    *,
    tile,
):
    tiles = keys.shape[0] // tile
    per = QB // tile
    blocks = q_ref.shape[0] // per
    scale = HEAD**-0.5
    factor = scale * LOG2E
    sort_pairs(scalars, (kv0, kv1, kv2, kv3, kv4), keys, values, tile)
    dk[...] = jnp.zeros_like(dk)
    dv[...] = jnp.zeros_like(dv)

    def block(i, carry):
        for k in range(per):
            slot = scalars[tiles + i * per + k]
            queries[k * tile : (k + 1) * tile, :] = q_ref[slot]
            grads[k * tile : (k + 1) * tile, :] = do_ref[slot]
        q_own = queries[...]
        do_own = grads[...]
        rows = pl.ds(pl.multiple_of(i * QB, QB), QB)
        product = do_own.astype(F32) * full_ref[rows, :]
        delta = jnp.sum(jnp.transpose(product), axis=0, keepdims=True)
        lse = lse_ref[i][:1]
        q_blocks = qblk[i][:1]

        def chunk(c, acc, masked):
            where = pl.ds(pl.multiple_of(c * KC, KC), KC)
            k_own = keys[where, :]
            s = dot_nt(k_own, q_own)
            if masked:
                s = jnp.where(kblk[where, :] <= q_blocks, s, -1e30)
            p = jnp.exp2(s * factor - lse)
            dp = dot_nt(values[where, :], do_own)
            ds = (p * (dp - delta)).astype(BF16)
            dv[where, :] += dot(p.astype(BF16), do_own)
            dk[where, :] += dot(ds, q_own)
            return acc + dot_tn(ds, k_own)

        base = tiles + blocks * per
        first, last = scalars[base + i], scalars[base + blocks + i]
        acc = jnp.zeros((QB, HEAD), F32)
        acc = lax.fori_loop(0, first, functools.partial(chunk, masked=False), acc)
        acc = lax.fori_loop(first, last, functools.partial(chunk, masked=True), acc)
        low = (acc * scale).astype(BF16)
        for k in range(per):
            dq_ref[scalars[tiles + i * per + k]] = low[k * tile : (k + 1) * tile]
        return carry

    lax.fori_loop(0, blocks, block, 0)

    outs = ((own_ref, own_ref), (after_low, after_high), (far_low, far_high), (before_low, before_high))
    for slot in range(tiles):
        dy, x, k = slot // 16, slot // 4 % 4, slot % 4
        rows = pl.ds(pl.multiple_of(scalars[slot] * tile, tile), tile)
        ref, x = outs[dy][x // 2], x if dy == 0 else x % 2
        here = slice(k * tile, (k + 1) * tile)
        ref[x, 0, here] = (dk[rows, :] * scale).astype(BF16)
        ref[x, 1, here] = dv[rows, :].astype(BF16)


def attend_back(scalars, q, kv, do, full, lse, qblk, kblk, after):
    tile = q.shape[1]
    count = q.shape[0] * tile
    length = kblk.shape[0]
    vmem = pl.BlockSpec(memory_space=pltpu.VMEM)
    kernel = functools.partial(attend_back_kernel, tile=tile)

    def body(*refs):
        kernel(*refs[:12], *refs[12 + len(after) :])

    return pl.pallas_call(
        body,
        out_shape=(
            jax.ShapeDtypeStruct(q.shape, BF16),
            jax.ShapeDtypeStruct(kv[0].shape, BF16),
        )
        + (jax.ShapeDtypeStruct(kv[2].shape, BF16),) * 6,
        in_specs=[pl.BlockSpec(memory_space=pltpu.SMEM)]
        + [vmem] * 11
        + [pl.BlockSpec(memory_space=pl.ANY)] * len(after),
        out_specs=(vmem,) * 8,
        scratch_shapes=[
            pltpu.VMEM((length, HEAD), BF16),
            pltpu.VMEM((length, HEAD), BF16),
            pltpu.VMEM((QB, HEAD), BF16),
            pltpu.VMEM((QB, HEAD), BF16),
            pltpu.VMEM((length, HEAD), F32),
            pltpu.VMEM((length, HEAD), F32),
        ],
        compiler_params=pltpu.CompilerParams(vmem_limit_bytes=VMEM_LIMIT),
        cost_estimate=pl.CostEstimate(
            flops=10 * count * length * HEAD, bytes_accessed=1 << 23, transcendentals=count * length
        ),
        name="attend_back",
    )(scalars, q, *kv, do, full, lse, qblk, kblk, *after)


def project_kernel(own_ref, near_ref, other_ref, w_ref, cos_ref, sin_ref, q_ref, kv_ref, a_ref):
    half = own_ref.shape[0]
    spread_rows(a_ref, (own_ref, near_ref, other_ref))
    cosine, sine = cos_ref[...], sin_ref[...]
    for part in range(3):
        product = dot(a_ref[...], w_ref[:, part * 2 * HEAD : (part + 1) * 2 * HEAD])
        for head in range(2):
            u = product[:, head * HEAD : (head + 1) * HEAD]
            if part < 2:
                u = u * cosine + pltpu.roll(u, HEAD // 2, 1) * sine
            u = u.astype(BF16)
            for ds in range(2):
                rows = u[ds * half : (ds + 1) * half]
                if part == 0:
                    q_ref[head * 2 + ds] = rows
                else:
                    kv_ref[head * 2 + ds, part - 1] = rows


def project(a, weights, cosine, sine, after):
    half, width = a[0].shape
    return call(
        project_kernel,
        "project",
        [((4, half, HEAD), BF16), ((4, 2, half, HEAD), BF16)],
        [],
        [*a, weights, cosine, sine],
        after,
        scratch=[pltpu.VMEM((2 * half, width), BF16)],
        flops=4 * half * width * 6 * HEAD,
    )


def output_kernel(o_ref, w_ref, keep_ref, send_ref):
    half = keep_ref.shape[0]
    o = jnp.concatenate([o_ref[0], o_ref[1]], axis=1)
    for c in range(0, keep_ref.shape[1], 512):
        part = dot_nt(o, w_ref[c : c + 512, :]).astype(BF16)
        keep_ref[:, c : c + 512] = part[:half]
        send_ref[:, c : c + 512] = part[half:]


def output(o_heads, weights):
    rows, width = o_heads.shape[1], weights.shape[0]
    outs = [((rows // 2, width), BF16)] * 2
    flops = 4 * rows * width * HEAD
    return call(output_kernel, "output", outs, [], [o_heads, weights], flops=flops)


def mlp_kernel(*refs):
    b_parts, dy_parts = refs[:10], refs[10:13]
    gate_ref, up_ref, down_ref, rows_ref, keep_ref, send_ref, turned_ref, hidden_ref = refs[13:21]
    b_ref, dy_ref, dg_ref, du_ref = refs[21:]
    step = pl.program_id(0)
    half, units, each = dy_parts[0].shape[0], dg_ref.shape[1], gate_ref.shape[1]
    steps = units // each

    @pl.when(step == 0)
    def _():
        put_rows(b_ref, b_parts)
        spread_rows(dy_ref, dy_parts)

    @pl.when(step < steps)
    def _():
        here = pl.ds(pl.multiple_of(step * each, each), each)
        gate = dot(b_ref[...], gate_ref[...])
        upper = dot(b_ref[...], up_ref[...])
        grad = dot(dy_ref[...], down_ref[...])
        sigmoid = 1.0 / (1.0 + jnp.exp(-gate))
        swish = gate * sigmoid
        made = (
            (grad * upper * sigmoid * (1.0 + gate * (1.0 - sigmoid))).astype(BF16),
            (grad * swish).astype(BF16),
            (swish * upper).astype(BF16),
        )
        for k, value in enumerate(made):
            turned_ref[k] = jnp.transpose(value)
        dg_ref[:, here] = made[0]
        du_ref[:, here] = made[1]
        hidden_ref[...] = made[2]

    @pl.when(step >= steps)
    def _():
        part = dot_nt(dg_ref[...], rows_ref[:, :units])
        part = (part + dot_nt(du_ref[...], rows_ref[:, units:])).astype(BF16)
        keep_ref[...] = part[:half]
        send_ref[...] = part[half:]


def mlp(b_parts, dy_parts, mlp_w):
    half, width = dy_parts[0].shape
    units, each, rows = mlp_w.shape[1] // 3, 512, 512
    steps, more = units // each, width // rows
    vmem = pl.BlockSpec(memory_space=pltpu.VMEM)

    def first(i):
        return jnp.minimum(i, steps - 1)

    def second(i):
        return jnp.maximum(i - steps, 0)

    return pl.pallas_call(
        mlp_kernel,
        grid=(steps + more,),
        out_shape=(
            jax.ShapeDtypeStruct((half, width), BF16),
            jax.ShapeDtypeStruct((half, width), BF16),
            jax.ShapeDtypeStruct((3, units, 2 * half), BF16),
            jax.ShapeDtypeStruct((2 * half, units), BF16),
        ),
        in_specs=[vmem] * 13
        + [
            pl.BlockSpec((width, each), lambda i: (0, first(i))),
            pl.BlockSpec((width, each), lambda i: (0, steps + first(i))),
            pl.BlockSpec((width, each), lambda i: (0, 2 * steps + first(i))),
            pl.BlockSpec((rows, 2 * units), lambda i: (second(i), 0)),
        ],
        out_specs=(
            pl.BlockSpec((half, rows), lambda i: (0, second(i))),
            pl.BlockSpec((half, rows), lambda i: (0, second(i))),
            pl.BlockSpec((3, each, 2 * half), lambda i: (0, first(i), 0)),
            pl.BlockSpec((2 * half, each), lambda i: (0, first(i))),
        ),
        scratch_shapes=[pltpu.VMEM((2 * half, width), BF16)] * 2
        + [pltpu.VMEM((2 * half, units), BF16)] * 2,
        compiler_params=pltpu.CompilerParams(vmem_limit_bytes=VMEM_LIMIT),
        cost_estimate=pl.CostEstimate(
            flops=20 * half * width * units, bytes_accessed=1, transcendentals=0
        ),
        name="mlp",
    )(*b_parts, *dy_parts, *[mlp_w] * 4)


def down_kernel(hidden_ref, w_ref, keep_ref, send_ref):
    half = keep_ref.shape[0]
    for c in range(0, keep_ref.shape[1], 512):
        part = dot_nt(hidden_ref[...], w_ref[c : c + 512, :]).astype(BF16)
        keep_ref[:, c : c + 512] = part[:half]
        send_ref[:, c : c + 512] = part[half:]


def down(hidden, mlp_w, after):
    (rows, units), width = hidden.shape, mlp_w.shape[0]
    spec = pl.BlockSpec((width, units), lambda i: (0, 2))
    outs = [((rows // 2, width), BF16)] * 2
    flops = 2 * rows * width * units
    return call(down_kernel, "down", outs, [], [hidden, mlp_w], after, flops=flops, specs={1: spec})


def spread_rows(to_ref, parts):
    own, near, *other = parts
    half = own.shape[0] // 2
    other = other[0] if other else near.at[half:]
    put_rows(to_ref, [own.at[:half], near.at[:half], own.at[half:], other])


def put_blocks(out_ref, row, column, product):
    for r in range(0, product.shape[1], HEAD):
        for c in range(0, product.shape[0], HEAD):
            out_ref[row + r // HEAD, column + c // HEAD] = product[c : c + HEAD, r : r + HEAD]


def mlp_grads_kernel(*refs, units):
    b_parts, dy_parts = refs[:10], refs[10:13]
    left_ref, out_ref, b_ref, dy_ref = refs[13:]
    step = pl.program_id(0)
    later = 2 * units // left_ref.shape[0]

    @pl.when(step == 0)
    def _():
        put_rows(b_ref, b_parts)
        spread_rows(dy_ref, dy_parts)

    def work(right_ref):
        for r in range(0, right_ref.shape[1], 512):
            product = dot(left_ref[...], right_ref[:, r : r + 512]).astype(BF16)
            put_blocks(out_ref, r // HEAD, 0, product)

    pl.when(step < later)(lambda: work(b_ref))
    pl.when(step >= later)(lambda: work(dy_ref))


def mlp_grads(b_parts, dy_parts, turned):
    rows, tokens = turned.shape
    width, step = b_parts[0].shape[1], 512
    vmem = pl.BlockSpec(memory_space=pltpu.VMEM)
    return pl.pallas_call(
        functools.partial(mlp_grads_kernel, units=rows // 3),
        grid=(rows // step,),
        out_shape=jax.ShapeDtypeStruct((width // HEAD, rows // HEAD, HEAD, HEAD), BF16),
        in_specs=[vmem] * 13 + [pl.BlockSpec((step, tokens), lambda i: (i, 0))],
        out_specs=pl.BlockSpec(
            (width // HEAD, step // HEAD, HEAD, HEAD), lambda i: (0, i, 0, 0)
        ),
        scratch_shapes=[pltpu.VMEM((tokens, width), BF16)] * 2,
        compiler_params=pltpu.CompilerParams(vmem_limit_bytes=VMEM_LIMIT),
        cost_estimate=pl.CostEstimate(
            flops=2 * rows * tokens * width, bytes_accessed=1, transcendentals=0
        ),
        name="mlp_grads",
    )(*b_parts, *dy_parts, turned)


def outward_kernel(*refs):
    parts, (w_ref, do_ref, m_ref) = refs[:10], refs[10:]
    put_rows(m_ref, parts)
    part = dot(m_ref[...], w_ref[...]).astype(BF16)
    half = part.shape[0] // 2
    for head in range(2):
        for ds in range(2):
            do_ref[head * 2 + ds] = part[
                ds * half : (ds + 1) * half, head * HEAD : (head + 1) * HEAD
            ]


def outward(m_parts, attn_w):
    width = attn_w.shape[0]
    half = sum(v.shape[0] for v in m_parts) // 2
    return call(
        outward_kernel,
        "outward",
        [((4, half, HEAD), BF16)],
        [],
        [*m_parts, attn_w],
        scratch=[pltpu.VMEM((2 * half, width), BF16)],
        flops=8 * half * width * HEAD,
    )[0]


def turn_back(e, cosine, sine):
    return e * cosine - pltpu.roll(e, HEAD // 2, 1) * sine


def query_grads_kernel(*refs):
    parts, m_parts, (dq_ref, cos_ref, sin_ref, o_ref) = refs[:3], refs[3:13], refs[13:17]
    out_ref, rows_ref = refs[17:]
    half = dq_ref.shape[1]
    put_rows(rows_ref, m_parts)
    left = jnp.concatenate([jnp.transpose(o_ref[k]) for k in range(2)], axis=0)
    for r in range(0, rows_ref.shape[1], 512):
        put_blocks(out_ref, r // HEAD, 0, dot(left, rows_ref[:, r : r + 512]).astype(BF16))
    spread_rows(rows_ref, parts)
    left = []
    for head in range(2):
        for ds in range(2):
            rows = slice(ds * half, (ds + 1) * half)
            e = turn_back(dq_ref[head * 2 + ds].astype(F32), cos_ref[rows], sin_ref[rows])
            left.append(jnp.transpose(e.astype(BF16)))
    left = jnp.concatenate(
        [jnp.concatenate(left[2 * k : 2 * k + 2], axis=1) for k in range(2)], axis=0
    )
    for r in range(0, rows_ref.shape[1], 512):
        put_blocks(out_ref, r // HEAD, 2, dot(left, rows_ref[:, r : r + 512]).astype(BF16))


def query_grads(a_parts, m_parts, dq, cosine, sine, o_heads):
    half, width = a_parts[0].shape
    return call(
        query_grads_kernel,
        "query_grads",
        [((width // HEAD, 4, HEAD, HEAD), BF16)],
        [],
        [*a_parts, *m_parts, dq, cosine, sine, o_heads],
        scratch=[pltpu.VMEM((2 * half, width), BF16)],
    )[0]


def back_kernel(*refs):
    parts, (dq_ref, dkv_ref, cos_ref, sin_ref, w_ref) = refs[:3], refs[3:8]
    keep_ref, send_ref, out_ref, back_ref, a_ref = refs[8:]
    spread_rows(a_ref, parts)
    half = dq_ref.shape[1]
    cosine, sine = cos_ref[...], sin_ref[...]
    for part in range(3):
        for head in range(2):
            for ds in range(2):
                unit = head * 2 + ds
                rows = slice(ds * half, (ds + 1) * half)
                e = (dq_ref[unit] if part == 0 else dkv_ref[unit, part - 1]).astype(F32)
                if part < 2:
                    e = turn_back(e, cosine[rows], sine[rows])
                column = (part * 2 + head) * HEAD
                back_ref[rows, column : column + HEAD] = e.astype(BF16)
    for c in range(0, keep_ref.shape[1], 512):
        part = dot_nt(back_ref[...], w_ref[c : c + 512, :]).astype(BF16)
        keep_ref[:, c : c + 512] = part[:half]
        send_ref[:, c : c + 512] = part[half:]
    for c in range(2 * HEAD, back_ref.shape[1], 2 * HEAD):
        left = jnp.transpose(back_ref[:, c : c + 2 * HEAD])
        for r in range(0, a_ref.shape[1], 512):
            product = dot(left, a_ref[:, r : r + 512]).astype(BF16)
            put_blocks(out_ref, r // HEAD, c // HEAD - 2, product)


def backward(a_parts, dq, dkv, cosine, sine, attn_w, after):
    half, width = dq.shape[1], attn_w.shape[0]
    return call(
        back_kernel,
        "backward",
        [((half, width), BF16)] * 2 + [((width // HEAD, 4, HEAD, HEAD), BF16)],
        [],
        [*a_parts, dq, dkv, cosine, sine, attn_w],
        after,
        scratch=[
            pltpu.VMEM((2 * half, 6 * HEAD), BF16),
            pltpu.VMEM((2 * half, width), BF16),
        ],
        flops=40 * half * width * HEAD,
    )


def total_kernel(at, terms_ref, keep_ref, send_ref):
    rows = keep_ref.shape[1]
    for c in range(keep_ref.shape[0]):
        total = terms_ref[0, c].astype(F32)
        for p in range(1, terms_ref.shape[0]):
            total = total + terms_ref[p, c].astype(F32)
        total = jnp.transpose(total)
        first, second = total[:rows], total[rows:]
        keep_ref[c] = jnp.where(at[0] == 0, first, second).astype(BF16)
        send_ref[c] = jnp.where(at[0] == 0, second, first).astype(BF16)


def total(zl, terms, after=()):
    outs = [((terms.shape[1], HEAD // 2, HEAD), BF16)] * 2
    return call(total_kernel, "total", outs, [(zl,)], [terms], after)


def place_kernel(at, keep_ref, got_ref, *outs):
    block = 0
    for out_ref in outs:
        half = out_ref.shape[1] // 2
        for c in range(0, half, HEAD):
            keep, got = keep_ref[block].astype(F32), got_ref[block].astype(F32)
            out_ref[:, c : c + HEAD] = jnp.where(at[0] == 0, keep, got)
            out_ref[:, half + c : half + c + HEAD] = jnp.where(at[0] == 0, got, keep)
            block += 1


def place(zl, sums, widths, after=()):
    keep, send = total(zl, sums, after)
    outs = [((HEAD // 2, 2 * w), F32) for w in widths]
    return call(place_kernel, "place", outs, [(zl,)], [keep, flip(send, zl=1)])


def finish_kernel(at, own_ref, far_ref, pair_ref, out_ref):
    tile = own_ref.shape[0]
    co, zh = at[0], at[1]
    lane = lax.broadcasted_iota(jnp.int32, (tile, HEAD), 1)
    for k in range(4):
        ref, start = ((own_ref, 0), (far_ref, 0), (pair_ref, 0), (pair_ref, tile))[k]
        at_row = ((k // 2) ^ co) * 2 + ((k % 2) ^ zh)
        rows = pl.ds(pl.multiple_of(at_row * tile, tile), tile)
        for y in range(NY):
            for half in range(NX // 2):
                pair = [
                    ref[start : start + tile, c : c + HEAD].astype(F32)
                    for c in ((y * NX + 2 * half) * HEAD, (y * NX + 2 * half + 1) * HEAD)
                ]
                turned = [pltpu.roll(v, HEAD // 2, 1) for v in pair]
                low = jnp.where(lane < HEAD // 2, pair[0], turned[1])
                high = jnp.where(lane < HEAD // 2, turned[0], pair[1])
                for zl, value in enumerate((low, high)):
                    column = (y * NZL + zl) * NX * HEAD // 2 + half * HEAD
                    out_ref[rows, column : column + HEAD] = value.astype(out_ref.dtype)


def finish(co, zh, own, dtype):
    far = flip(own, zh=1)
    pair = flip(jnp.concatenate([own, far], axis=0), co=1)
    vmem = pl.BlockSpec(memory_space=pltpu.VMEM)
    return pl.pallas_call(
        finish_kernel,
        out_shape=jax.ShapeDtypeStruct((4 * own.shape[0], own.shape[1]), dtype),
        in_specs=[pl.BlockSpec(memory_space=pltpu.SMEM)] + [vmem] * 3,
        out_specs=vmem,
        compiler_params=pltpu.CompilerParams(vmem_limit_bytes=VMEM_LIMIT),
        cost_estimate=pl.CostEstimate(flops=1, bytes_accessed=1, transcendentals=0),
        name="finish",
    )(jnp.stack([co, zh]).astype(jnp.int32), own, far, pair)


def local(
    tokens_in,
    w_query,
    w_key,
    w_value,
    w_output,
    w_gate,
    w_up,
    w_down,
    grad_out,
    block_ids,
    tile_order,
):
    own, width = tokens_in.shape
    seqs, length = block_ids.shape
    tile = length // tile_order.shape[1]
    wide = w_query.shape[1] // 2
    units = w_gate.shape[1] // 2
    piece = w_query.shape[0]
    ctx, tp = lax.axis_index("ctx"), lax.axis_index("tp")
    y, zl, x = ctx // (NZL * NX), (ctx // NX) % NZL, ctx % NX
    zh, co = tp // 2, tp % 2

    def pair_rows(arrays):
        def cut(array, which):
            half = array.shape[1] // 2
            return lax.dynamic_slice_in_dim(array, which * half, half, 1)

        kept = jnp.concatenate([cut(array, zl) for array in arrays], axis=1)
        sent = jnp.concatenate([cut(array, 1 - zl) for array in arrays], axis=1)
        return turn(jnp.stack([kept, flip(sent, zl=1)]), 0, zl).reshape(2 * piece, -1)

    pair = pair_rows((w_query, w_key, w_value))
    copies = plane_copies(pair)
    attn_w = plane_gather(copies)
    first_own, grads, x_own = enter(co, zh, tokens_in, grad_out, [copies])
    near = flip(first_own[: own // 2], zl=1)
    first_low = [first_own, near, flip(near, co=1)]
    started = (near[0, 0] * 0).astype(jnp.int32)
    pair = pair_rows([hold(w, near) for w in (w_gate, w_up, w_down, w_output)])

    tiles = (tile_order + started).reshape(seqs, NY, NZL, NX, 2)
    tiles = turn(turn(turn(tiles, 0, co), 2, zl), 4, zh)
    row_tiles = lax.dynamic_index_in_dim(tiles, y, 1, keepdims=False)
    own_tiles = lax.dynamic_index_in_dim(row_tiles, x, 2, keepdims=False).reshape(-1)
    positions = (own_tiles[:, None] * tile + jnp.arange(tile, dtype=jnp.int32)).reshape(-1)
    inverse = 10000.0 ** (-jnp.arange(0, HEAD, 2, dtype=F32) / HEAD)
    angles = positions.astype(F32)[:, None] * inverse[None, :]
    cosine = jnp.concatenate([jnp.cos(angles)] * 2, axis=-1)
    sine = jnp.concatenate([-jnp.sin(angles), jnp.sin(angles)], axis=-1)
    ds_own = x % 2
    unit_tiles = lax.dynamic_index_in_dim(tiles, ds_own, 0, keepdims=False)
    turns = (y + jnp.arange(NY, dtype=jnp.int32)) % NY
    key_tiles = jnp.swapaxes(jnp.take(unit_tiles, turns, axis=0), 1, 2).reshape(-1)
    query_tiles = lax.dynamic_index_in_dim(unit_tiles, y, 0, keepdims=False)
    query_tiles = jnp.swapaxes(query_tiles, 0, 1).reshape(-1)
    tile_count, query_count = key_tiles.shape[0], query_tiles.shape[0]
    rank = jnp.sum(query_tiles[None, :] < query_tiles[:, None], axis=1)
    places = jnp.arange(query_count, dtype=jnp.int32)
    order = jnp.sum(
        jnp.where(rank[None, :] == places[:, None], places[None, :], 0), axis=1
    ).astype(jnp.int32)
    sorted_tiles = jnp.sum(
        jnp.where(rank[None, :] == places[:, None], query_tiles[None, :], 0), axis=1
    )
    key_blocks = lax.dynamic_index_in_dim(block_ids + started, ds_own ^ co, 0, keepdims=False)
    query_blocks = jnp.take(key_blocks.reshape(tile_count, tile), sorted_tiles, axis=0).reshape(-1)
    by_block = query_blocks.reshape(-1, QB)
    sure = jnp.sum(key_blocks[None, :] <= by_block[:, :1], axis=1) // KC
    most = (jnp.sum(key_blocks[None, :] <= by_block[:, -1:], axis=1) + KC - 1) // KC
    scalars = jnp.concatenate([key_tiles, order, sure, most]).astype(jnp.int32)
    query_rows = jnp.broadcast_to(by_block[:, None, :], (by_block.shape[0], 8, QB))

    query_column, key_column = query_blocks[:, None], key_blocks[:, None]
    tables = [scalars, query_column, key_column, query_rows]
    q_send, kv_send = project(first_low, attn_w, cosine, sine, tables)
    half = own

    def across(values):
        return lax.all_to_all(values, "ctx", 0, 0, tiled=True, axis_index_groups=X_GROUPS)

    kv_line = across(kv_send)
    q = across(q_send).reshape(query_count, tile, HEAD)
    near = flip(hold(grads[: own // 2], q_send), zl=1)
    grad_all = [grads, near, flip(near, co=1)]
    kv = ring_gather(kv_line, (q, near), dy=1)
    mlp_w = lax.all_gather(
        hold(pair[:, : 3 * units], kv_line), "ctx", axis=0, tiled=True, axis_index_groups=XY_GROUPS
    )
    w_out = plane_gather(plane_copies(hold(pair[:, 3 * units :], q)))
    o, o_full, lse = attend(
        scalars, q, kv, query_column, key_blocks[None, :], [grad_all[2]]
    )
    o_heads = across(o.reshape(NX, half, HEAD)).reshape(2, 2 * half, HEAD)
    attn_sum = column_sum(*output(o_heads, w_out))

    x_own = x_own.astype(F32)
    dy_own = grads[:tile].astype(F32)
    middle = x_own + attn_sum
    normed_two, inverse_two = norm(middle)
    second_low = column_gather(normed_two.astype(BF16))
    keep, send, turned, hidden = mlp(second_low, grad_all, mlp_w)
    terms = mlp_grads(second_low, grad_all, turned.reshape(3 * units, -1))
    sums = lax.psum_scatter(
        terms, "ctx", scatter_dimension=0, tiled=True, axis_index_groups=XY_GROUPS
    )
    back_two = column_sum(keep, send, terms)
    grad_middle = dy_own + norm_back(back_two, normed_two, inverse_two)
    middle_low = column_gather(grad_middle.astype(BF16))

    do_send = outward(middle_low, w_out)
    do = across(do_send).reshape(query_count, tile, HEAD)
    out_keep, out_send = down(hidden, mlp_w, [do_send])
    dq, dkv, *others = attend_back(
        scalars,
        q,
        kv,
        do,
        o_full,
        lse,
        query_rows,
        key_column,
        [out_keep],
    )
    pairs = [(dkv[:2], dkv[2:])] + [tuple(others[2 * k : 2 * k + 2]) for k in range(3)]
    dkv = jnp.concatenate(ring_sum(pairs, dy=1), axis=0).astype(BF16)
    out_sum = column_sum(hold(out_keep, dq), hold(out_send, dq))
    dq = across(dq.reshape(NX, half, HEAD))
    query_sums = lax.psum_scatter(
        query_grads(first_low, middle_low, dq, cosine, sine, o_heads),
        "ctx",
        scatter_dimension=0,
        tiled=True,
        axis_index_groups=XY_GROUPS,
    )
    dkv = across(hold(dkv, dq))
    out_low = (middle + out_sum).astype(BF16)
    keep, send, terms = backward(first_low, dq, dkv, cosine, sine, attn_w, [out_low])
    terms = lax.all_to_all(terms, "ctx", 0, 0, tiled=True, axis_index_groups=XY_GROUPS)
    back_one = column_sum(keep, send)
    normed_own, inverse_own = norm(x_own)
    grad_own = grad_middle + norm_back(back_one, normed_own, inverse_own)
    grad_in = finish(co, zh, grad_own.astype(BF16), F32)
    tokens_out = finish(co, zh, out_low, BF16)
    mlp_out = place(zl, sums, (units,) * 3, [send])
    output_out, query_out = place(zl, query_sums, (wide,) * 2, [send])
    after = [grad_in, tokens_out, mlp_out[0], output_out]
    key_out, value_out = place(zl, terms, (wide,) * 2, after)
    return (
        tokens_out,
        grad_in,
        query_out,
        key_out,
        value_out,
        output_out,
        *mlp_out,
    )


def solution(mesh):
    row, both = P("ctx", None), P("ctx", "tp")
    return jax.shard_map(
        local,
        mesh=mesh,
        in_specs=(row,) + (both,) * 7 + (row, P(), P()),
        out_specs=(row, row) + (both,) * 7,
        check_vma=False,
    )
```

```python
import functools

import jax
import jax.numpy as jnp
from jax import lax
from jax.experimental import pallas as pl
from jax.experimental.pallas import tpu as pltpu
from jax.sharding import PartitionSpec as P

HEAD = 128
NY, NZL, NX = 4, 2, 4
BOTH = ("ctx", "tp")
QB = 256
KC = 512
LOG2E = 1.4426950408889634
VMEM_LIMIT = 56 * 1024 * 1024
F32, BF16 = jnp.float32, jnp.bfloat16


def ctx_index(y, zl, x):
    return (y * NZL + zl) * NX + x


XY_GROUPS = [
    [ctx_index(y, zl, x) for y in range(NY) for x in range(NX)] for zl in range(NZL)
]
X_GROUPS = [
    [ctx_index(y, zl, x) for x in range(NX)] for y in range(NY) for zl in range(NZL)
]


def flip(values, zl=0, zh=0, co=0):
    pairs = []
    for y in range(NY):
        for a in range(NZL):
            for x in range(NX):
                for t in range(4):
                    here = ctx_index(y, a, x) * 4 + t
                    there = ctx_index(y, a ^ zl, x) * 4 + (t ^ (2 * zh + co))
                    pairs.append((here, there))
    return lax.ppermute(values, BOTH, pairs)


def ring(values, dx=0, dy=0):
    pairs = [
        (ctx_index(y, a, x), ctx_index((y + dy) % NY, a, (x + dx) % NX))
        for y in range(NY)
        for a in range(NZL)
        for x in range(NX)
    ]
    return lax.ppermute(values, "ctx", pairs)


def turn(values, axis, bit):
    return jnp.where(bit == 1, jnp.flip(values, axis), values)


def norm(values):
    average = jnp.mean(values, axis=-1, keepdims=True)
    centred = values - average
    inverse = lax.rsqrt(jnp.mean(centred * centred, axis=-1, keepdims=True) + 1e-05)
    return centred * inverse, inverse


def norm_back(grad, normed, inverse):
    first = jnp.mean(grad, axis=-1, keepdims=True)
    second = jnp.mean(grad * normed, axis=-1, keepdims=True)
    return inverse * (grad - first - normed * second)


def column_sum(keep, send, token=None):
    rows = keep.shape[0] // 4
    cut = rows // 2
    got = flip(send, co=1)
    half = keep.astype(F32) + got.astype(F32)
    if token is not None:
        half = hold(half, token)
    own, far, near, both = (half[k * rows : (k + 1) * rows] for k in range(4))
    for_both = flip(far[:cut].astype(BF16), zl=1)
    for_near = flip(far[cut:].astype(BF16), zl=1, zh=1)
    near = jnp.concatenate([near[:cut], near[cut:] + for_near.astype(F32)], axis=0).astype(BF16)
    both = jnp.concatenate([both[:cut] + for_both.astype(F32), both[cut:]], axis=0).astype(BF16)
    from_near, from_both = flip(near, zl=1), flip(both, zl=1, zh=1)
    return own + from_near.astype(F32) + from_both.astype(F32)


def column_gather(rows):
    cut = rows.shape[0] // 2
    near, both = flip(rows, zl=1), flip(rows, zl=1, zh=1)
    far_low, far_high = flip(both[:cut], zl=1), flip(near[cut:], zl=1, zh=1)
    half = [rows, far_low, far_high, near, both]
    return half + [flip(piece, co=1) for piece in half]


def ring_sum(parts, **step):
    forth, back = step, {k: -v for k, v in step.items()}
    ahead, behind = ring(parts[2][0], **forth), ring(parts[2][1], **back)
    from_back, from_forth = ring(parts[1][1], **forth), ring(parts[3][0], **back)
    low = parts[1][0].astype(F32) + ahead.astype(F32)
    high = parts[3][1].astype(F32) + behind.astype(F32)
    low, high = ring(low.astype(BF16), **forth), ring(high.astype(BF16), **back)
    return (
        parts[0][0].astype(F32) + low.astype(F32) + from_forth.astype(F32),
        parts[0][1].astype(F32) + from_back.astype(F32) + high.astype(F32),
    )


def ring_gather(rows, tokens, **step):
    forth, back = step, {k: -v for k, v in step.items()}
    cut = rows.shape[0] // 2
    before, after = ring(rows, **forth), ring(rows, **back)
    low, high = before[:cut], after[cut:]
    for one in tokens:
        low, high = hold(low, one), hold(high, one)
    low, high = ring(low, **forth), ring(high, **back)
    return rows, after, low, high, before


def plane_copies(rows):
    return jnp.broadcast_to(rows[None], (NY * NX,) + rows.shape)


def plane_gather(copies):
    every = lax.all_to_all(copies, "ctx", 0, 0, tiled=True, axis_index_groups=XY_GROUPS)
    return every.reshape(-1, copies.shape[2])


def dot(left, right):
    return jnp.dot(left, right, preferred_element_type=F32)


def dot_nt(left, right):
    return lax.dot_general(left, right, (((1,), (1,)), ((), ())), preferred_element_type=F32)


def dot_tn(left, right):
    return lax.dot_general(left, right, (((0,), (0,)), ((), ())), preferred_element_type=F32)


def call(kernel, name, outs, scalars, arrays, after=(), scratch=(), flops=1, specs=None):
    head, tail = len(scalars) + len(arrays), len(after)
    vmem = pl.BlockSpec(memory_space=pltpu.VMEM)
    specs = specs or {}
    grid = {"grid": (1,)} if specs else {}

    def body(*refs):
        kernel(*refs[:head], *refs[head + tail :])

    return pl.pallas_call(
        body,
        **grid,
        out_shape=tuple(jax.ShapeDtypeStruct(shape, dtype) for shape, dtype in outs),
        in_specs=[pl.BlockSpec(memory_space=pltpu.SMEM)] * len(scalars)
        + [specs.get(k, vmem) for k in range(len(arrays))]
        + [pl.BlockSpec(memory_space=pl.ANY)] * tail,
        out_specs=(vmem,) * len(outs),
        scratch_shapes=list(scratch),
        compiler_params=pltpu.CompilerParams(vmem_limit_bytes=VMEM_LIMIT),
        cost_estimate=pl.CostEstimate(flops=flops, bytes_accessed=1, transcendentals=0),
        name=name,
    )(*[jnp.stack(s).astype(jnp.int32) for s in scalars], *arrays, *after)


def hold(values, token):
    return values + (token.reshape(-1)[0] * 0).astype(values.dtype)


def put_rows(to_ref, refs):
    row = 0
    for ref in refs:
        to_ref[row : row + ref.shape[0], :] = ref[...]
        row += ref.shape[0]


def enter_kernel(at, x_ref, dy_ref, a_ref, dy_out, own_ref):
    tile = own_ref.shape[0]
    lane = lax.broadcasted_iota(jnp.int32, (tile, HEAD), 1)
    for k in range(4):
        row = ((k // 2) ^ at[0]) * 2 + ((k % 2) ^ at[1])
        rows = pl.ds(pl.multiple_of(row * tile, tile), tile)
        x = x_ref[rows, :].astype(F32)
        values = [(norm(x)[0], a_ref), (dy_ref[rows, :].astype(F32), dy_out)]
        if k == 0:
            values.append((x, own_ref))
        for value, to_ref in values:
            for y in range(NY):
                for half in range(NX // 2):
                    pair = [
                        value[:, c : c + HEAD]
                        for c in [(y * NZL + z) * NX * HEAD // 2 + half * HEAD for z in range(2)]
                    ]
                    turned = [pltpu.roll(v, HEAD // 2, 1) for v in pair]
                    low = jnp.where(lane < HEAD // 2, pair[0], turned[1])
                    high = jnp.where(lane < HEAD // 2, turned[0], pair[1])
                    for n, v in enumerate((low, high)):
                        c = (y * NX + 2 * half + n) * HEAD
                        to_ref[k * tile : (k + 1) * tile, c : c + HEAD] = v.astype(BF16)


def enter(co, zh, x, dy, after):
    rows, width = x.shape
    outs = [((rows, width), BF16)] * 2 + [((rows // 4, width), BF16)]
    return call(enter_kernel, "enter", outs, [(co, zh)], [x, dy], after)


def each_piece(pairs):
    own, after, low, high, before = pairs
    for dy in range(NY):
        for x in range(NX):
            ref = (own, after, (low, high)[x // 2], before)[dy]
            for k in range(4):
                yield (dy * NX + x) * 4 + k, x % 2 if dy == 2 else x, k, ref


def sort_pairs(scalars, pairs, keys, values, tile):
    for slot, x, k, ref in each_piece(pairs):
        rows = pl.ds(pl.multiple_of(scalars[slot] * tile, tile), tile)
        keys[rows, :] = ref[x, 0, k * tile : (k + 1) * tile]
        values[rows, :] = ref[x, 1, k * tile : (k + 1) * tile]


def attend_kernel(
    scalars, q_ref, kv0, kv1, kv2, kv3, kv4, qblk, kblk, o_ref, full_ref, lse_ref, keys, values, queries, *, tile
):
    tiles = keys.shape[0] // tile
    per = QB // tile
    blocks = q_ref.shape[0] // per
    factor = HEAD**-0.5 * LOG2E
    sort_pairs(scalars, (kv0, kv1, kv2, kv3, kv4), keys, values, tile)

    def block(i, carry):
        for k in range(per):
            queries[k * tile : (k + 1) * tile, :] = q_ref[scalars[tiles + i * per + k]]
        q_own = queries[...]
        rows = pl.ds(pl.multiple_of(i * QB, QB), QB)

        def chunk(c, state, masked):
            top, total, acc = state
            where = pl.ds(pl.multiple_of(c * KC, KC), KC)
            s = dot_nt(q_own, keys[where, :])
            if masked:
                s = jnp.where(qblk[rows, :] >= kblk[:, where], s, -1e30)
            new = jnp.maximum(top, jnp.max(s, axis=-1, keepdims=True))
            p = jnp.exp2((s - new) * factor)
            shrink = jnp.exp2((top - new) * factor)
            total = total * shrink + jnp.sum(p, axis=-1, keepdims=True)
            acc = acc * shrink + dot(p.astype(BF16), values[where, :])
            return new, total, acc

        base = tiles + blocks * per
        state = (
            jnp.full((QB, 1), -1e30, F32),
            jnp.zeros((QB, 1), F32),
            jnp.zeros((QB, HEAD), F32),
        )
        first, last = scalars[base + i], scalars[base + blocks + i]
        state = lax.fori_loop(0, first, functools.partial(chunk, masked=False), state)
        top, total, acc = lax.fori_loop(first, last, functools.partial(chunk, masked=True), state)
        out = acc / total
        full_ref[rows, :] = out
        low = out.astype(BF16)
        for k in range(per):
            o_ref[scalars[tiles + i * per + k]] = low[k * tile : (k + 1) * tile]
        lse = top * factor + jnp.log2(total)
        lse_ref[i] = jnp.transpose(jnp.broadcast_to(lse, (QB, HEAD)))[:8]
        return carry

    lax.fori_loop(0, blocks, block, 0)


def attend(scalars, q, kv, qblk, kblk, after):
    tile = q.shape[1]
    count = q.shape[0] * tile
    length = kblk.shape[1]
    vmem = pl.BlockSpec(memory_space=pltpu.VMEM)
    kernel = functools.partial(attend_kernel, tile=tile)

    def body(*refs):
        kernel(*refs[:9], *refs[9 + len(after) :])

    return pl.pallas_call(
        body,
        out_shape=(
            jax.ShapeDtypeStruct(q.shape, BF16),
            jax.ShapeDtypeStruct((count, HEAD), F32),
            jax.ShapeDtypeStruct((count // QB, 8, QB), F32),
        ),
        in_specs=[pl.BlockSpec(memory_space=pltpu.SMEM)]
        + [vmem] * 8
        + [pl.BlockSpec(memory_space=pl.ANY)] * len(after),
        out_specs=(vmem,) * 3,
        scratch_shapes=[
            pltpu.VMEM((length, HEAD), BF16),
            pltpu.VMEM((length, HEAD), BF16),
            pltpu.VMEM((QB, HEAD), BF16),
        ],
        compiler_params=pltpu.CompilerParams(vmem_limit_bytes=VMEM_LIMIT),
        cost_estimate=pl.CostEstimate(
            flops=4 * count * length * HEAD, bytes_accessed=1 << 22, transcendentals=count * length
        ),
        name="attend",
    )(scalars, q, *kv, qblk, kblk, *after)


def attend_back_kernel(
    scalars,
    q_ref,
    kv0,
    kv1,
    kv2,
    kv3,
    kv4,
    do_ref,
    full_ref,
    lse_ref,
    qblk,
    kblk,
    dq_ref,
    own_ref,
    after_low,
    after_high,
    far_low,
    far_high,
    before_low,
    before_high,
    keys,
    values,
    queries,
    grads,
    dk,
    dv,
    *,
    tile,
):
    tiles = keys.shape[0] // tile
    per = QB // tile
    blocks = q_ref.shape[0] // per
    scale = HEAD**-0.5
    factor = scale * LOG2E
    sort_pairs(scalars, (kv0, kv1, kv2, kv3, kv4), keys, values, tile)
    dk[...] = jnp.zeros_like(dk)
    dv[...] = jnp.zeros_like(dv)

    def block(i, carry):
        for k in range(per):
            slot = scalars[tiles + i * per + k]
            queries[k * tile : (k + 1) * tile, :] = q_ref[slot]
            grads[k * tile : (k + 1) * tile, :] = do_ref[slot]
        q_own = queries[...]
        do_own = grads[...]
        rows = pl.ds(pl.multiple_of(i * QB, QB), QB)
        product = do_own.astype(F32) * full_ref[rows, :]
        delta = jnp.sum(jnp.transpose(product), axis=0, keepdims=True)
        lse = lse_ref[i][:1]
        q_blocks = qblk[i][:1]

        def chunk(c, acc, masked):
            where = pl.ds(pl.multiple_of(c * KC, KC), KC)
            k_own = keys[where, :]
            s = dot_nt(k_own, q_own)
            if masked:
                s = jnp.where(kblk[where, :] <= q_blocks, s, -1e30)
            p = jnp.exp2(s * factor - lse)
            dp = dot_nt(values[where, :], do_own)
            ds = (p * (dp - delta)).astype(BF16)
            dv[where, :] += dot(p.astype(BF16), do_own)
            dk[where, :] += dot(ds, q_own)
            return acc + dot_tn(ds, k_own)

        base = tiles + blocks * per
        first, last = scalars[base + i], scalars[base + blocks + i]
        acc = jnp.zeros((QB, HEAD), F32)
        acc = lax.fori_loop(0, first, functools.partial(chunk, masked=False), acc)
        acc = lax.fori_loop(first, last, functools.partial(chunk, masked=True), acc)
        low = (acc * scale).astype(BF16)
        for k in range(per):
            dq_ref[scalars[tiles + i * per + k]] = low[k * tile : (k + 1) * tile]
        return carry

    lax.fori_loop(0, blocks, block, 0)

    outs = ((own_ref, own_ref), (after_low, after_high), (far_low, far_high), (before_low, before_high))
    for slot in range(tiles):
        dy, x, k = slot // 16, slot // 4 % 4, slot % 4
        rows = pl.ds(pl.multiple_of(scalars[slot] * tile, tile), tile)
        ref, x = outs[dy][x // 2], x if dy == 0 else x % 2
        here = slice(k * tile, (k + 1) * tile)
        ref[x, 0, here] = (dk[rows, :] * scale).astype(BF16)
        ref[x, 1, here] = dv[rows, :].astype(BF16)


def attend_back(scalars, q, kv, do, full, lse, qblk, kblk, after):
    tile = q.shape[1]
    count = q.shape[0] * tile
    length = kblk.shape[0]
    vmem = pl.BlockSpec(memory_space=pltpu.VMEM)
    kernel = functools.partial(attend_back_kernel, tile=tile)

    def body(*refs):
        kernel(*refs[:12], *refs[12 + len(after) :])

    return pl.pallas_call(
        body,
        out_shape=(
            jax.ShapeDtypeStruct(q.shape, BF16),
            jax.ShapeDtypeStruct(kv[0].shape, BF16),
        )
        + (jax.ShapeDtypeStruct(kv[2].shape, BF16),) * 6,
        in_specs=[pl.BlockSpec(memory_space=pltpu.SMEM)]
        + [vmem] * 11
        + [pl.BlockSpec(memory_space=pl.ANY)] * len(after),
        out_specs=(vmem,) * 8,
        scratch_shapes=[
            pltpu.VMEM((length, HEAD), BF16),
            pltpu.VMEM((length, HEAD), BF16),
            pltpu.VMEM((QB, HEAD), BF16),
            pltpu.VMEM((QB, HEAD), BF16),
            pltpu.VMEM((length, HEAD), F32),
            pltpu.VMEM((length, HEAD), F32),
        ],
        compiler_params=pltpu.CompilerParams(vmem_limit_bytes=VMEM_LIMIT),
        cost_estimate=pl.CostEstimate(
            flops=10 * count * length * HEAD, bytes_accessed=1 << 23, transcendentals=count * length
        ),
        name="attend_back",
    )(scalars, q, *kv, do, full, lse, qblk, kblk, *after)


def project_kernel(own_ref, near_ref, other_ref, w_ref, cos_ref, sin_ref, qkv_ref, a_ref):
    half = own_ref.shape[0]
    spread_rows(a_ref, (own_ref, near_ref, other_ref))
    cosine, sine = cos_ref[...], sin_ref[...]
    for part in range(3):
        product = dot(a_ref[...], w_ref[:, part * 2 * HEAD : (part + 1) * 2 * HEAD])
        for head in range(2):
            u = product[:, head * HEAD : (head + 1) * HEAD]
            if part < 2:
                u = u * cosine + pltpu.roll(u, HEAD // 2, 1) * sine
            u = u.astype(BF16)
            for ds in range(2):
                rows = u[ds * half : (ds + 1) * half]
                qkv_ref[head * 2 + ds, part] = rows


def project(a, weights, cosine, sine, after):
    half, width = a[0].shape
    return call(
        project_kernel,
        "project",
        [((4, 3, half, HEAD), BF16)],
        [],
        [*a, weights, cosine, sine],
        after,
        scratch=[pltpu.VMEM((2 * half, width), BF16)],
        flops=4 * half * width * 6 * HEAD,
    )[0]


def output_kernel(o_ref, w_ref, keep_ref, send_ref):
    half = keep_ref.shape[0]
    o = jnp.concatenate([o_ref[0], o_ref[1]], axis=1)
    for c in range(0, keep_ref.shape[1], 512):
        part = dot_nt(o, w_ref[c : c + 512, :]).astype(BF16)
        keep_ref[:, c : c + 512] = part[:half]
        send_ref[:, c : c + 512] = part[half:]


def output(o_heads, weights):
    rows, width = o_heads.shape[1], weights.shape[0]
    outs = [((rows // 2, width), BF16)] * 2
    flops = 4 * rows * width * HEAD
    return call(output_kernel, "output", outs, [], [o_heads, weights], flops=flops)


def mlp_kernel(*refs):
    b_parts, dy_parts = refs[:10], refs[10:13]
    gate_ref, up_ref, down_ref, rows_ref, keep_ref, send_ref, turned_ref, hidden_ref = refs[13:21]
    b_ref, dy_ref, dg_ref, du_ref = refs[21:]
    step = pl.program_id(0)
    half, units, each = dy_parts[0].shape[0], dg_ref.shape[1], gate_ref.shape[1]
    steps = units // each

    @pl.when(step == 0)
    def _():
        put_rows(b_ref, b_parts)
        spread_rows(dy_ref, dy_parts)

    @pl.when(step < steps)
    def _():
        here = pl.ds(pl.multiple_of(step * each, each), each)
        gate = dot(b_ref[...], gate_ref[...])
        upper = dot(b_ref[...], up_ref[...])
        grad = dot(dy_ref[...], down_ref[...])
        sigmoid = 1.0 / (1.0 + jnp.exp(-gate))
        swish = gate * sigmoid
        made = (
            (grad * upper * sigmoid * (1.0 + gate * (1.0 - sigmoid))).astype(BF16),
            (grad * swish).astype(BF16),
            (swish * upper).astype(BF16),
        )
        for k, value in enumerate(made):
            turned_ref[k] = jnp.transpose(value)
        dg_ref[:, here] = made[0]
        du_ref[:, here] = made[1]
        hidden_ref[...] = made[2]

    @pl.when(step >= steps)
    def _():
        part = dot_nt(dg_ref[...], rows_ref[:, :units])
        part = (part + dot_nt(du_ref[...], rows_ref[:, units:])).astype(BF16)
        keep_ref[...] = part[:half]
        send_ref[...] = part[half:]


def mlp(b_parts, dy_parts, mlp_w):
    half, width = dy_parts[0].shape
    units, each, rows = mlp_w.shape[1] // 3, 512, 512
    steps, more = units // each, width // rows
    vmem = pl.BlockSpec(memory_space=pltpu.VMEM)

    def first(i):
        return jnp.minimum(i, steps - 1)

    def second(i):
        return jnp.maximum(i - steps, 0)

    return pl.pallas_call(
        mlp_kernel,
        grid=(steps + more,),
        out_shape=(
            jax.ShapeDtypeStruct((half, width), BF16),
            jax.ShapeDtypeStruct((half, width), BF16),
            jax.ShapeDtypeStruct((3, units, 2 * half), BF16),
            jax.ShapeDtypeStruct((2 * half, units), BF16),
        ),
        in_specs=[vmem] * 13
        + [
            pl.BlockSpec((width, each), lambda i: (0, first(i))),
            pl.BlockSpec((width, each), lambda i: (0, steps + first(i))),
            pl.BlockSpec((width, each), lambda i: (0, 2 * steps + first(i))),
            pl.BlockSpec((rows, 2 * units), lambda i: (second(i), 0)),
        ],
        out_specs=(
            pl.BlockSpec((half, rows), lambda i: (0, second(i))),
            pl.BlockSpec((half, rows), lambda i: (0, second(i))),
            pl.BlockSpec((3, each, 2 * half), lambda i: (0, first(i), 0)),
            pl.BlockSpec((2 * half, each), lambda i: (0, first(i))),
        ),
        scratch_shapes=[pltpu.VMEM((2 * half, width), BF16)] * 2
        + [pltpu.VMEM((2 * half, units), BF16)] * 2,
        compiler_params=pltpu.CompilerParams(vmem_limit_bytes=VMEM_LIMIT),
        cost_estimate=pl.CostEstimate(
            flops=20 * half * width * units, bytes_accessed=1, transcendentals=0
        ),
        name="mlp",
    )(*b_parts, *dy_parts, *[mlp_w] * 4)


def down_kernel(hidden_ref, w_ref, keep_ref, send_ref):
    half = keep_ref.shape[0]
    for c in range(0, keep_ref.shape[1], 512):
        part = dot_nt(hidden_ref[...], w_ref[c : c + 512, :]).astype(BF16)
        keep_ref[:, c : c + 512] = part[:half]
        send_ref[:, c : c + 512] = part[half:]


def down(hidden, mlp_w, after):
    (rows, units), width = hidden.shape, mlp_w.shape[0]
    spec = pl.BlockSpec((width, units), lambda i: (0, 2))
    outs = [((rows // 2, width), BF16)] * 2
    flops = 2 * rows * width * units
    return call(down_kernel, "down", outs, [], [hidden, mlp_w], after, flops=flops, specs={1: spec})


def spread_rows(to_ref, parts):
    own, near, *other = parts
    half = own.shape[0] // 2
    other = other[0] if other else near.at[half:]
    put_rows(to_ref, [own.at[:half], near.at[:half], own.at[half:], other])


def put_blocks(out_ref, row, column, product):
    for r in range(0, product.shape[1], HEAD):
        for c in range(0, product.shape[0], HEAD):
            out_ref[row + r // HEAD, column + c // HEAD] = product[c : c + HEAD, r : r + HEAD]


def mlp_grads_kernel(*refs, units):
    b_parts, dy_parts = refs[:10], refs[10:13]
    left_ref, out_ref, b_ref, dy_ref = refs[13:]
    step = pl.program_id(0)
    later = 2 * units // left_ref.shape[0]

    @pl.when(step == 0)
    def _():
        put_rows(b_ref, b_parts)
        spread_rows(dy_ref, dy_parts)

    def work(right_ref):
        for r in range(0, right_ref.shape[1], 512):
            product = dot(left_ref[...], right_ref[:, r : r + 512]).astype(BF16)
            put_blocks(out_ref, r // HEAD, 0, product)

    pl.when(step < later)(lambda: work(b_ref))
    pl.when(step >= later)(lambda: work(dy_ref))


def mlp_grads(b_parts, dy_parts, turned):
    rows, tokens = turned.shape
    width, step = b_parts[0].shape[1], 512
    vmem = pl.BlockSpec(memory_space=pltpu.VMEM)
    return pl.pallas_call(
        functools.partial(mlp_grads_kernel, units=rows // 3),
        grid=(rows // step,),
        out_shape=jax.ShapeDtypeStruct((width // HEAD, rows // HEAD, HEAD, HEAD), BF16),
        in_specs=[vmem] * 13 + [pl.BlockSpec((step, tokens), lambda i: (i, 0))],
        out_specs=pl.BlockSpec(
            (width // HEAD, step // HEAD, HEAD, HEAD), lambda i: (0, i, 0, 0)
        ),
        scratch_shapes=[pltpu.VMEM((tokens, width), BF16)] * 2,
        compiler_params=pltpu.CompilerParams(vmem_limit_bytes=VMEM_LIMIT),
        cost_estimate=pl.CostEstimate(
            flops=2 * rows * tokens * width, bytes_accessed=1, transcendentals=0
        ),
        name="mlp_grads",
    )(*b_parts, *dy_parts, turned)


def outward_kernel(*refs):
    parts, (w_ref, do_ref, m_ref) = refs[:10], refs[10:]
    put_rows(m_ref, parts)
    part = dot(m_ref[...], w_ref[...]).astype(BF16)
    half = part.shape[0] // 2
    for head in range(2):
        for ds in range(2):
            do_ref[head * 2 + ds] = part[
                ds * half : (ds + 1) * half, head * HEAD : (head + 1) * HEAD
            ]


def outward(m_parts, attn_w):
    width = attn_w.shape[0]
    half = sum(v.shape[0] for v in m_parts) // 2
    return call(
        outward_kernel,
        "outward",
        [((4, half, HEAD), BF16)],
        [],
        [*m_parts, attn_w],
        scratch=[pltpu.VMEM((2 * half, width), BF16)],
        flops=8 * half * width * HEAD,
    )[0]


def back_kernel(*refs):
    parts, m_parts, (dq_ref, dkv_ref, cos_ref, sin_ref, o_ref, w_ref) = refs[:3], refs[3:13], refs[13:19]
    keep_ref, send_ref, out_ref, back_ref, a_ref = refs[19:]
    spread_rows(a_ref, parts)
    half = dq_ref.shape[1]
    cosine, sine = cos_ref[...], sin_ref[...]
    for part in range(3):
        for head in range(2):
            for ds in range(2):
                unit = head * 2 + ds
                rows = slice(ds * half, (ds + 1) * half)
                e = (dq_ref[unit] if part == 0 else dkv_ref[unit, part - 1]).astype(F32)
                if part < 2:
                    e = e * cosine[rows] - pltpu.roll(e, HEAD // 2, 1) * sine[rows]
                column = (part * 2 + head) * HEAD
                back_ref[rows, column : column + HEAD] = e.astype(BF16)
    for c in range(0, keep_ref.shape[1], 512):
        part = dot_nt(back_ref[...], w_ref[c : c + 512, :]).astype(BF16)
        keep_ref[:, c : c + 512] = part[:half]
        send_ref[:, c : c + 512] = part[half:]
    for c in range(0, back_ref.shape[1], 2 * HEAD):
        left = jnp.transpose(back_ref[:, c : c + 2 * HEAD])
        for r in range(0, a_ref.shape[1], 512):
            product = dot(left, a_ref[:, r : r + 512]).astype(BF16)
            put_blocks(out_ref, r // HEAD, c // HEAD, product)
    put_rows(a_ref, m_parts)
    left = jnp.concatenate([jnp.transpose(o_ref[k]) for k in range(2)], axis=0)
    for r in range(0, a_ref.shape[1], 512):
        put_blocks(out_ref, r // HEAD, 6, dot(left, a_ref[:, r : r + 512]).astype(BF16))


def backward(a_parts, m_parts, dq, dkv, cosine, sine, o_heads, attn_w, after):
    half, width = dq.shape[1], attn_w.shape[0]
    return call(
        back_kernel,
        "backward",
        [((half, width), BF16)] * 2 + [((width // HEAD, 8, HEAD, HEAD), BF16)],
        [],
        [*a_parts, *m_parts, dq, dkv, cosine, sine, o_heads, attn_w],
        after,
        scratch=[
            pltpu.VMEM((2 * half, 6 * HEAD), BF16),
            pltpu.VMEM((2 * half, width), BF16),
        ],
        flops=48 * half * width * HEAD,
    )


def total_kernel(at, terms_ref, keep_ref, send_ref):
    rows = keep_ref.shape[1]
    for c in range(keep_ref.shape[0]):
        total = terms_ref[0, c].astype(F32)
        for p in range(1, terms_ref.shape[0]):
            total = total + terms_ref[p, c].astype(F32)
        total = jnp.transpose(total)
        first, second = total[:rows], total[rows:]
        keep_ref[c] = jnp.where(at[0] == 0, first, second).astype(BF16)
        send_ref[c] = jnp.where(at[0] == 0, second, first).astype(BF16)


def total(zl, terms, after=()):
    outs = [((terms.shape[1], HEAD // 2, HEAD), BF16)] * 2
    return call(total_kernel, "total", outs, [(zl,)], [terms], after)


def place_kernel(at, keep_ref, got_ref, *outs):
    block = 0
    for out_ref in outs:
        half = out_ref.shape[1] // 2
        for c in range(0, half, HEAD):
            keep, got = keep_ref[block].astype(F32), got_ref[block].astype(F32)
            out_ref[:, c : c + HEAD] = jnp.where(at[0] == 0, keep, got)
            out_ref[:, half + c : half + c + HEAD] = jnp.where(at[0] == 0, got, keep)
            block += 1


def place(zl, sums, widths, after=()):
    keep, send = total(zl, sums, after)
    outs = [((HEAD // 2, 2 * w), F32) for w in widths]
    return call(place_kernel, "place", outs, [(zl,)], [keep, flip(send, zl=1)])


def finish_kernel(at, own_ref, far_ref, pair_ref, out_ref):
    tile = own_ref.shape[0]
    co, zh = at[0], at[1]
    lane = lax.broadcasted_iota(jnp.int32, (tile, HEAD), 1)
    for k in range(4):
        ref, start = ((own_ref, 0), (far_ref, 0), (pair_ref, 0), (pair_ref, tile))[k]
        at_row = ((k // 2) ^ co) * 2 + ((k % 2) ^ zh)
        rows = pl.ds(pl.multiple_of(at_row * tile, tile), tile)
        for y in range(NY):
            for half in range(NX // 2):
                pair = [
                    ref[start : start + tile, c : c + HEAD].astype(F32)
                    for c in ((y * NX + 2 * half) * HEAD, (y * NX + 2 * half + 1) * HEAD)
                ]
                turned = [pltpu.roll(v, HEAD // 2, 1) for v in pair]
                low = jnp.where(lane < HEAD // 2, pair[0], turned[1])
                high = jnp.where(lane < HEAD // 2, turned[0], pair[1])
                for zl, value in enumerate((low, high)):
                    column = (y * NZL + zl) * NX * HEAD // 2 + half * HEAD
                    out_ref[rows, column : column + HEAD] = value.astype(out_ref.dtype)


def finish(co, zh, own, dtype):
    far = flip(own, zh=1)
    pair = flip(jnp.concatenate([own, far], axis=0), co=1)
    vmem = pl.BlockSpec(memory_space=pltpu.VMEM)
    return pl.pallas_call(
        finish_kernel,
        out_shape=jax.ShapeDtypeStruct((4 * own.shape[0], own.shape[1]), dtype),
        in_specs=[pl.BlockSpec(memory_space=pltpu.SMEM)] + [vmem] * 3,
        out_specs=vmem,
        compiler_params=pltpu.CompilerParams(vmem_limit_bytes=VMEM_LIMIT),
        cost_estimate=pl.CostEstimate(flops=1, bytes_accessed=1, transcendentals=0),
        name="finish",
    )(jnp.stack([co, zh]).astype(jnp.int32), own, far, pair)


def local(
    tokens_in,
    w_query,
    w_key,
    w_value,
    w_output,
    w_gate,
    w_up,
    w_down,
    grad_out,
    block_ids,
    tile_order,
):
    own, width = tokens_in.shape
    seqs, length = block_ids.shape
    tile = length // tile_order.shape[1]
    wide = w_query.shape[1] // 2
    units = w_gate.shape[1] // 2
    piece = w_query.shape[0]
    ctx, tp = lax.axis_index("ctx"), lax.axis_index("tp")
    y, zl, x = ctx // (NZL * NX), (ctx // NX) % NZL, ctx % NX
    zh, co = tp // 2, tp % 2

    def pair_rows(arrays):
        def cut(array, which):
            half = array.shape[1] // 2
            return lax.dynamic_slice_in_dim(array, which * half, half, 1)

        kept = jnp.concatenate([cut(array, zl) for array in arrays], axis=1)
        sent = jnp.concatenate([cut(array, 1 - zl) for array in arrays], axis=1)
        return turn(jnp.stack([kept, flip(sent, zl=1)]), 0, zl).reshape(2 * piece, -1)

    pair = pair_rows((w_query, w_key, w_value))
    copies = plane_copies(pair)
    attn_w = plane_gather(copies)
    first_own, grads, x_own = enter(co, zh, tokens_in, grad_out, [copies])
    near = flip(first_own[: own // 2], zl=1)
    first_low = [first_own, near, flip(near, co=1)]
    started = (near[0, 0] * 0).astype(jnp.int32)
    pair = pair_rows([hold(w, near) for w in (w_gate, w_up, w_down, w_output)])

    tiles = (tile_order + started).reshape(seqs, NY, NZL, NX, 2)
    tiles = turn(turn(turn(tiles, 0, co), 2, zl), 4, zh)
    row_tiles = lax.dynamic_index_in_dim(tiles, y, 1, keepdims=False)
    own_tiles = lax.dynamic_index_in_dim(row_tiles, x, 2, keepdims=False).reshape(-1)
    positions = (own_tiles[:, None] * tile + jnp.arange(tile, dtype=jnp.int32)).reshape(-1)
    inverse = 10000.0 ** (-jnp.arange(0, HEAD, 2, dtype=F32) / HEAD)
    angles = positions.astype(F32)[:, None] * inverse[None, :]
    cosine = jnp.concatenate([jnp.cos(angles)] * 2, axis=-1)
    sine = jnp.concatenate([-jnp.sin(angles), jnp.sin(angles)], axis=-1)
    ds_own = x % 2
    unit_tiles = lax.dynamic_index_in_dim(tiles, ds_own, 0, keepdims=False)
    turns = (y + jnp.arange(NY, dtype=jnp.int32)) % NY
    key_tiles = jnp.swapaxes(jnp.take(unit_tiles, turns, axis=0), 1, 2).reshape(-1)
    query_tiles = lax.dynamic_index_in_dim(unit_tiles, y, 0, keepdims=False)
    query_tiles = jnp.swapaxes(query_tiles, 0, 1).reshape(-1)
    tile_count, query_count = key_tiles.shape[0], query_tiles.shape[0]
    rank = jnp.sum(query_tiles[None, :] < query_tiles[:, None], axis=1)
    places = jnp.arange(query_count, dtype=jnp.int32)
    order = jnp.sum(
        jnp.where(rank[None, :] == places[:, None], places[None, :], 0), axis=1
    ).astype(jnp.int32)
    sorted_tiles = jnp.sum(
        jnp.where(rank[None, :] == places[:, None], query_tiles[None, :], 0), axis=1
    )
    key_blocks = lax.dynamic_index_in_dim(block_ids + started, ds_own ^ co, 0, keepdims=False)
    query_blocks = jnp.take(key_blocks.reshape(tile_count, tile), sorted_tiles, axis=0).reshape(-1)
    by_block = query_blocks.reshape(-1, QB)
    sure = jnp.sum(key_blocks[None, :] <= by_block[:, :1], axis=1) // KC
    most = (jnp.sum(key_blocks[None, :] <= by_block[:, -1:], axis=1) + KC - 1) // KC
    scalars = jnp.concatenate([key_tiles, order, sure, most]).astype(jnp.int32)
    query_rows = jnp.broadcast_to(by_block[:, None, :], (by_block.shape[0], 8, QB))

    query_column, key_column = query_blocks[:, None], key_blocks[:, None]
    tables = [scalars, query_column, key_column, query_rows]
    qkv_send = project(first_low, attn_w, cosine, sine, tables)
    half = own

    def across(values):
        return lax.all_to_all(values, "ctx", 0, 0, tiled=True, axis_index_groups=X_GROUPS)

    line = across(qkv_send)
    q, kv_line = line[:, 0].reshape(query_count, tile, HEAD), line[:, 1:]
    near = flip(hold(grads[: own // 2], qkv_send), zl=1)
    grad_all = [grads, near, flip(near, co=1)]
    kv = ring_gather(kv_line, (near,), dy=1)
    mlp_w = lax.all_gather(
        hold(pair[:, : 3 * units], kv_line), "ctx", axis=0, tiled=True, axis_index_groups=XY_GROUPS
    )
    w_out = plane_gather(plane_copies(hold(pair[:, 3 * units :], line)))
    o, o_full, lse = attend(
        scalars, q, kv, query_column, key_blocks[None, :], [grad_all[2]]
    )
    o_heads = across(o.reshape(NX, half, HEAD)).reshape(2, 2 * half, HEAD)
    attn_sum = column_sum(*output(o_heads, w_out))

    x_own = x_own.astype(F32)
    dy_own = grads[:tile].astype(F32)
    middle = x_own + attn_sum
    normed_two, inverse_two = norm(middle)
    second_low = column_gather(normed_two.astype(BF16))
    keep, send, turned, hidden = mlp(second_low, grad_all, mlp_w)
    terms = mlp_grads(second_low, grad_all, turned.reshape(3 * units, -1))
    sums = lax.psum_scatter(
        terms, "ctx", scatter_dimension=0, tiled=True, axis_index_groups=XY_GROUPS
    )
    back_two = column_sum(keep, send, terms)
    grad_middle = dy_own + norm_back(back_two, normed_two, inverse_two)
    middle_low = column_gather(grad_middle.astype(BF16))

    do_send = outward(middle_low, w_out)
    do = across(do_send).reshape(query_count, tile, HEAD)
    out_keep, out_send = down(hidden, mlp_w, [do_send])
    dq, dkv, *others = attend_back(
        scalars,
        q,
        kv,
        do,
        o_full,
        lse,
        query_rows,
        key_column,
        [out_keep],
    )
    pairs = [(dkv[:2], dkv[2:])] + [tuple(others[2 * k : 2 * k + 2]) for k in range(3)]
    dkv = jnp.concatenate(ring_sum(pairs, dy=1), axis=0).astype(BF16)
    out_sum = column_sum(hold(out_keep, dq), hold(out_send, dq))
    dq = across(dq.reshape(NX, half, HEAD))
    dkv = across(hold(dkv, dq))
    out_low = (middle + out_sum).astype(BF16)
    keep, send, terms = backward(
        first_low, middle_low, dq, dkv, cosine, sine, o_heads, attn_w, [out_low]
    )
    terms = lax.all_to_all(terms, "ctx", 0, 0, tiled=True, axis_index_groups=XY_GROUPS)
    back_one = column_sum(keep, send)
    normed_own, inverse_own = norm(x_own)
    grad_own = grad_middle + norm_back(back_one, normed_own, inverse_own)
    grad_in = finish(co, zh, grad_own.astype(BF16), F32)
    tokens_out = finish(co, zh, out_low, BF16)
    mlp_out = place(zl, sums, (units,) * 3, [send])
    return (
        tokens_out,
        grad_in,
        *place(zl, terms, (wide,) * 4, [grad_in, tokens_out, mlp_out[0]]),
        *mlp_out,
    )


def solution(mesh):
    row, both = P("ctx", None), P("ctx", "tp")
    return jax.shard_map(
        local,
        mesh=mesh,
        in_specs=(row,) + (both,) * 7 + (row, P(), P()),
        out_specs=(row, row) + (both,) * 7,
        check_vma=False,
    )
```

```python
import functools

import jax
import jax.numpy as jnp
from jax import lax
from jax.experimental import pallas as pl
from jax.experimental.pallas import tpu as pltpu
from jax.sharding import PartitionSpec as P

HEAD = 128
NY, NZL, NX = 4, 2, 4
BOTH = ("ctx", "tp")
QB = 256
KC = 1024
LOG2E = 1.4426950408889634
VMEM_LIMIT = 56 * 1024 * 1024
F32, BF16 = jnp.float32, jnp.bfloat16


def ctx_index(y, zl, x):
    return (y * NZL + zl) * NX + x


XY_GROUPS = [
    [ctx_index(y, zl, x) for y in range(NY) for x in range(NX)] for zl in range(NZL)
]
X_GROUPS = [
    [ctx_index(y, zl, x) for x in range(NX)] for y in range(NY) for zl in range(NZL)
]


def flip(values, zl=0, zh=0, co=0):
    pairs = []
    for y in range(NY):
        for a in range(NZL):
            for x in range(NX):
                for t in range(4):
                    here = ctx_index(y, a, x) * 4 + t
                    there = ctx_index(y, a ^ zl, x) * 4 + (t ^ (2 * zh + co))
                    pairs.append((here, there))
    return lax.ppermute(values, BOTH, pairs)


def ring(values, dx=0, dy=0):
    pairs = [
        (ctx_index(y, a, x), ctx_index((y + dy) % NY, a, (x + dx) % NX))
        for y in range(NY)
        for a in range(NZL)
        for x in range(NX)
    ]
    return lax.ppermute(values, "ctx", pairs)


def turn(values, axis, bit):
    return jnp.where(bit == 1, jnp.flip(values, axis), values)


def norm(values):
    average = jnp.mean(values, axis=-1, keepdims=True)
    centred = values - average
    inverse = lax.rsqrt(jnp.mean(centred * centred, axis=-1, keepdims=True) + 1e-05)
    return centred * inverse, inverse


def norm_back(grad, normed, inverse):
    first = jnp.mean(grad, axis=-1, keepdims=True)
    second = jnp.mean(grad * normed, axis=-1, keepdims=True)
    return inverse * (grad - first - normed * second)


def column_sum(keep, send, token=None):
    rows = keep.shape[0] // 4
    cut = rows // 2
    got = flip(send, co=1)
    half = keep.astype(F32) + got.astype(F32)
    if token is not None:
        half = hold(half, token)
    own, far, near, both = (half[k * rows : (k + 1) * rows] for k in range(4))
    for_both = flip(far[:cut].astype(BF16), zl=1)
    for_near = flip(far[cut:].astype(BF16), zl=1, zh=1)
    near = jnp.concatenate([near[:cut], near[cut:] + for_near.astype(F32)], axis=0).astype(BF16)
    both = jnp.concatenate([both[:cut] + for_both.astype(F32), both[cut:]], axis=0).astype(BF16)
    from_near, from_both = flip(near, zl=1), flip(both, zl=1, zh=1)
    return own + from_near.astype(F32) + from_both.astype(F32)


def column_gather(rows):
    cut = rows.shape[0] // 2
    near, both = flip(rows, zl=1), flip(rows, zl=1, zh=1)
    far_low, far_high = flip(both[:cut], zl=1), flip(near[cut:], zl=1, zh=1)
    half = [rows, far_low, far_high, near, both]
    return half + [flip(piece, co=1) for piece in half]


def ring_sum(parts, **step):
    forth, back = step, {k: -v for k, v in step.items()}
    ahead, behind = ring(parts[2][0], **forth), ring(parts[2][1], **back)
    from_back, from_forth = ring(parts[1][1], **forth), ring(parts[3][0], **back)
    low = parts[1][0].astype(F32) + ahead.astype(F32)
    high = parts[3][1].astype(F32) + behind.astype(F32)
    low, high = ring(low.astype(BF16), **forth), ring(high.astype(BF16), **back)
    return (
        parts[0][0].astype(F32) + low.astype(F32) + from_forth.astype(F32),
        parts[0][1].astype(F32) + from_back.astype(F32) + high.astype(F32),
    )


def ring_gather(rows, tokens, **step):
    forth, back = step, {k: -v for k, v in step.items()}
    cut = rows.shape[0] // 2
    before, after = ring(rows, **forth), ring(rows, **back)
    low, high = before[:cut], after[cut:]
    for one in tokens:
        low, high = hold(low, one), hold(high, one)
    low, high = ring(low, **forth), ring(high, **back)
    return rows, after, low, high, before


def plane_copies(rows):
    return jnp.broadcast_to(rows[None], (NY * NX,) + rows.shape)


def plane_gather(copies):
    every = lax.all_to_all(copies, "ctx", 0, 0, tiled=True, axis_index_groups=XY_GROUPS)
    return every.reshape(-1, copies.shape[2])


def dot(left, right):
    return jnp.dot(left, right, preferred_element_type=F32)


def dot_nt(left, right):
    return lax.dot_general(left, right, (((1,), (1,)), ((), ())), preferred_element_type=F32)


def dot_tn(left, right):
    return lax.dot_general(left, right, (((0,), (0,)), ((), ())), preferred_element_type=F32)


def call(kernel, name, outs, scalars, arrays, after=(), scratch=(), flops=1, specs=None):
    head, tail = len(scalars) + len(arrays), len(after)
    vmem = pl.BlockSpec(memory_space=pltpu.VMEM)
    specs = specs or {}
    grid = {"grid": (1,)} if specs else {}

    def body(*refs):
        kernel(*refs[:head], *refs[head + tail :])

    return pl.pallas_call(
        body,
        **grid,
        out_shape=tuple(jax.ShapeDtypeStruct(shape, dtype) for shape, dtype in outs),
        in_specs=[pl.BlockSpec(memory_space=pltpu.SMEM)] * len(scalars)
        + [specs.get(k, vmem) for k in range(len(arrays))]
        + [pl.BlockSpec(memory_space=pl.ANY)] * tail,
        out_specs=(vmem,) * len(outs),
        scratch_shapes=list(scratch),
        compiler_params=pltpu.CompilerParams(vmem_limit_bytes=VMEM_LIMIT),
        cost_estimate=pl.CostEstimate(flops=flops, bytes_accessed=1, transcendentals=0),
        name=name,
    )(*[jnp.stack(s).astype(jnp.int32) for s in scalars], *arrays, *after)


def hold(values, token):
    return values + (token.reshape(-1)[0] * 0).astype(values.dtype)


def put_rows(to_ref, refs):
    row = 0
    for ref in refs:
        to_ref[row : row + ref.shape[0], :] = ref[...]
        row += ref.shape[0]


def enter_kernel(at, x_ref, dy_ref, a_ref, dy_out, own_ref):
    tile = own_ref.shape[0]
    lane = lax.broadcasted_iota(jnp.int32, (tile, HEAD), 1)
    for k in range(4):
        row = ((k // 2) ^ at[0]) * 2 + ((k % 2) ^ at[1])
        rows = pl.ds(pl.multiple_of(row * tile, tile), tile)
        x = x_ref[rows, :].astype(F32)
        values = [(norm(x)[0], a_ref), (dy_ref[rows, :].astype(F32), dy_out)]
        if k == 0:
            values.append((x, own_ref))
        for value, to_ref in values:
            for y in range(NY):
                for half in range(NX // 2):
                    pair = [
                        value[:, c : c + HEAD]
                        for c in [(y * NZL + z) * NX * HEAD // 2 + half * HEAD for z in range(2)]
                    ]
                    turned = [pltpu.roll(v, HEAD // 2, 1) for v in pair]
                    low = jnp.where(lane < HEAD // 2, pair[0], turned[1])
                    high = jnp.where(lane < HEAD // 2, turned[0], pair[1])
                    for n, v in enumerate((low, high)):
                        c = (y * NX + 2 * half + n) * HEAD
                        to_ref[k * tile : (k + 1) * tile, c : c + HEAD] = v.astype(BF16)


def enter(co, zh, x, dy, after):
    rows, width = x.shape
    outs = [((rows, width), BF16)] * 2 + [((rows // 4, width), BF16)]
    return call(enter_kernel, "enter", outs, [(co, zh)], [x, dy], after)


def each_piece(pairs):
    own, after, low, high, before = pairs
    for dy in range(NY):
        for x in range(NX):
            ref = (own, after, (low, high)[x // 2], before)[dy]
            for k in range(4):
                yield (dy * NX + x) * 4 + k, x % 2 if dy == 2 else x, k, ref


def sort_pairs(scalars, pairs, keys, values, tile):
    for slot, x, k, ref in each_piece(pairs):
        rows = pl.ds(pl.multiple_of(scalars[slot] * tile, tile), tile)
        keys[rows, :] = ref[x, 0, k * tile : (k + 1) * tile]
        values[rows, :] = ref[x, 1, k * tile : (k + 1) * tile]


def attend_kernel(
    scalars, q_ref, kv0, kv1, kv2, kv3, kv4, qblk, kblk, o_ref, full_ref, lse_ref, keys, values, queries, *, tile
):
    tiles = keys.shape[0] // tile
    per = QB // tile
    blocks = q_ref.shape[0] // per
    factor = HEAD**-0.5 * LOG2E
    sort_pairs(scalars, (kv0, kv1, kv2, kv3, kv4), keys, values, tile)

    def block(i, carry):
        for k in range(per):
            queries[k * tile : (k + 1) * tile, :] = q_ref[scalars[tiles + i * per + k]]
        q_own = queries[...]
        rows = pl.ds(pl.multiple_of(i * QB, QB), QB)

        def chunk(c, state, masked):
            top, total, acc = state
            where = pl.ds(pl.multiple_of(c * KC, KC), KC)
            s = dot_nt(q_own, keys[where, :])
            if masked:
                s = jnp.where(qblk[rows, :] >= kblk[:, where], s, -1e30)
            new = jnp.maximum(top, jnp.max(s, axis=-1, keepdims=True))
            p = jnp.exp2((s - new) * factor)
            shrink = jnp.exp2((top - new) * factor)
            total = total * shrink + jnp.sum(p, axis=-1, keepdims=True)
            acc = acc * shrink + dot(p.astype(BF16), values[where, :])
            return new, total, acc

        base = tiles + blocks * per
        state = (
            jnp.full((QB, 1), -1e30, F32),
            jnp.zeros((QB, 1), F32),
            jnp.zeros((QB, HEAD), F32),
        )
        first, last = scalars[base + i], scalars[base + blocks + i]
        state = lax.fori_loop(0, first, functools.partial(chunk, masked=False), state)
        top, total, acc = lax.fori_loop(first, last, functools.partial(chunk, masked=True), state)
        out = acc / total
        full_ref[rows, :] = out
        low = out.astype(BF16)
        for k in range(per):
            o_ref[scalars[tiles + i * per + k]] = low[k * tile : (k + 1) * tile]
        lse = top * factor + jnp.log2(total)
        lse_ref[i] = jnp.transpose(jnp.broadcast_to(lse, (QB, HEAD)))[:8]
        return carry

    lax.fori_loop(0, blocks, block, 0)


def attend(scalars, q, kv, qblk, kblk, after):
    tile = q.shape[1]
    count = q.shape[0] * tile
    length = kblk.shape[1]
    vmem = pl.BlockSpec(memory_space=pltpu.VMEM)
    kernel = functools.partial(attend_kernel, tile=tile)

    def body(*refs):
        kernel(*refs[:9], *refs[9 + len(after) :])

    return pl.pallas_call(
        body,
        out_shape=(
            jax.ShapeDtypeStruct(q.shape, BF16),
            jax.ShapeDtypeStruct((count, HEAD), F32),
            jax.ShapeDtypeStruct((count // QB, 8, QB), F32),
        ),
        in_specs=[pl.BlockSpec(memory_space=pltpu.SMEM)]
        + [vmem] * 8
        + [pl.BlockSpec(memory_space=pl.ANY)] * len(after),
        out_specs=(vmem,) * 3,
        scratch_shapes=[
            pltpu.VMEM((length, HEAD), BF16),
            pltpu.VMEM((length, HEAD), BF16),
            pltpu.VMEM((QB, HEAD), BF16),
        ],
        compiler_params=pltpu.CompilerParams(vmem_limit_bytes=VMEM_LIMIT),
        cost_estimate=pl.CostEstimate(
            flops=32 * count * length * HEAD, bytes_accessed=1 << 22, transcendentals=count * length
        ),
        name="attend",
    )(scalars, q, *kv, qblk, kblk, *after)


def attend_back_kernel(
    scalars,
    q_ref,
    kv0,
    kv1,
    kv2,
    kv3,
    kv4,
    do_ref,
    full_ref,
    lse_ref,
    qblk,
    kblk,
    dq_ref,
    own_ref,
    after_low,
    after_high,
    far_low,
    far_high,
    before_low,
    before_high,
    keys,
    values,
    queries,
    grads,
    dk,
    dv,
    *,
    tile,
):
    tiles = keys.shape[0] // tile
    per = QB // tile
    blocks = q_ref.shape[0] // per
    scale = HEAD**-0.5
    factor = scale * LOG2E
    sort_pairs(scalars, (kv0, kv1, kv2, kv3, kv4), keys, values, tile)
    dk[...] = jnp.zeros_like(dk)
    dv[...] = jnp.zeros_like(dv)

    def block(i, carry):
        for k in range(per):
            slot = scalars[tiles + i * per + k]
            queries[k * tile : (k + 1) * tile, :] = q_ref[slot]
            grads[k * tile : (k + 1) * tile, :] = do_ref[slot]
        q_own = queries[...]
        do_own = grads[...]
        rows = pl.ds(pl.multiple_of(i * QB, QB), QB)
        product = do_own.astype(F32) * full_ref[rows, :]
        delta = jnp.sum(jnp.transpose(product), axis=0, keepdims=True)
        lse = lse_ref[i][:1]
        q_blocks = qblk[i][:1]

        def chunk(c, acc, masked):
            where = pl.ds(pl.multiple_of(c * KC, KC), KC)
            k_own = keys[where, :]
            s = dot_nt(k_own, q_own)
            if masked:
                s = jnp.where(kblk[where, :] <= q_blocks, s, -1e30)
            p = jnp.exp2(s * factor - lse)
            dp = dot_nt(values[where, :], do_own)
            ds = (p * (dp - delta)).astype(BF16)
            dv[where, :] += dot(p.astype(BF16), do_own)
            dk[where, :] += dot(ds, q_own)
            return acc + dot_tn(ds, k_own)

        base = tiles + blocks * per
        first, last = scalars[base + i], scalars[base + blocks + i]
        acc = jnp.zeros((QB, HEAD), F32)
        acc = lax.fori_loop(0, first, functools.partial(chunk, masked=False), acc)
        acc = lax.fori_loop(first, last, functools.partial(chunk, masked=True), acc)
        low = (acc * scale).astype(BF16)
        for k in range(per):
            dq_ref[scalars[tiles + i * per + k]] = low[k * tile : (k + 1) * tile]
        return carry

    lax.fori_loop(0, blocks, block, 0)

    outs = ((own_ref, own_ref), (after_low, after_high), (far_low, far_high), (before_low, before_high))
    for slot in range(tiles):
        dy, x, k = slot // 16, slot // 4 % 4, slot % 4
        rows = pl.ds(pl.multiple_of(scalars[slot] * tile, tile), tile)
        ref, x = outs[dy][x // 2], x if dy == 0 else x % 2
        here = slice(k * tile, (k + 1) * tile)
        ref[x, 0, here] = (dk[rows, :] * scale).astype(BF16)
        ref[x, 1, here] = dv[rows, :].astype(BF16)


def attend_back(scalars, q, kv, do, full, lse, qblk, kblk, after):
    tile = q.shape[1]
    count = q.shape[0] * tile
    length = kblk.shape[0]
    vmem = pl.BlockSpec(memory_space=pltpu.VMEM)
    kernel = functools.partial(attend_back_kernel, tile=tile)

    def body(*refs):
        kernel(*refs[:12], *refs[12 + len(after) :])

    return pl.pallas_call(
        body,
        out_shape=(
            jax.ShapeDtypeStruct(q.shape, BF16),
            jax.ShapeDtypeStruct(kv[0].shape, BF16),
        )
        + (jax.ShapeDtypeStruct(kv[2].shape, BF16),) * 6,
        in_specs=[pl.BlockSpec(memory_space=pltpu.SMEM)]
        + [vmem] * 11
        + [pl.BlockSpec(memory_space=pl.ANY)] * len(after),
        out_specs=(vmem,) * 8,
        scratch_shapes=[
            pltpu.VMEM((length, HEAD), BF16),
            pltpu.VMEM((length, HEAD), BF16),
            pltpu.VMEM((QB, HEAD), BF16),
            pltpu.VMEM((QB, HEAD), BF16),
            pltpu.VMEM((length, HEAD), F32),
            pltpu.VMEM((length, HEAD), F32),
        ],
        compiler_params=pltpu.CompilerParams(vmem_limit_bytes=VMEM_LIMIT),
        cost_estimate=pl.CostEstimate(
            flops=40 * count * length * HEAD, bytes_accessed=1 << 23, transcendentals=count * length
        ),
        name="attend_back",
    )(scalars, q, *kv, do, full, lse, qblk, kblk, *after)


def project_kernel(own_ref, near_ref, other_ref, w_ref, cos_ref, sin_ref, qkv_ref, a_ref):
    half = own_ref.shape[0]
    spread_rows(a_ref, (own_ref, near_ref, other_ref))
    cosine, sine = cos_ref[...], sin_ref[...]
    for part in range(3):
        product = dot(a_ref[...], w_ref[:, part * 2 * HEAD : (part + 1) * 2 * HEAD])
        for head in range(2):
            u = product[:, head * HEAD : (head + 1) * HEAD]
            if part < 2:
                u = u * cosine + pltpu.roll(u, HEAD // 2, 1) * sine
            u = u.astype(BF16)
            for ds in range(2):
                rows = u[ds * half : (ds + 1) * half]
                qkv_ref[head * 2 + ds, part] = rows


def project(a, weights, cosine, sine, after):
    half, width = a[0].shape
    return call(
        project_kernel,
        "project",
        [((4, 3, half, HEAD), BF16)],
        [],
        [*a, weights, cosine, sine],
        after,
        scratch=[pltpu.VMEM((2 * half, width), BF16)],
        flops=4 * half * width * 6 * HEAD,
    )[0]


def output_kernel(o_ref, w_ref, keep_ref, send_ref):
    half = keep_ref.shape[0]
    o = jnp.concatenate([o_ref[0], o_ref[1]], axis=1)
    for c in range(0, keep_ref.shape[1], 512):
        part = dot_nt(o, w_ref[c : c + 512, :]).astype(BF16)
        keep_ref[:, c : c + 512] = part[:half]
        send_ref[:, c : c + 512] = part[half:]


def output(o_heads, weights):
    rows, width = o_heads.shape[1], weights.shape[0]
    outs = [((rows // 2, width), BF16)] * 2
    flops = 4 * rows * width * HEAD
    return call(output_kernel, "output", outs, [], [o_heads, weights], flops=flops)


def mlp_kernel(*refs):
    b_parts, dy_parts = refs[:10], refs[10:13]
    gate_ref, up_ref, down_ref, rows_ref, keep_ref, send_ref, turned_ref, hidden_ref = refs[13:21]
    b_ref, dy_ref, dg_ref, du_ref = refs[21:]
    step = pl.program_id(0)
    half, units, each = dy_parts[0].shape[0], dg_ref.shape[1], gate_ref.shape[1]
    steps = units // each

    @pl.when(step == 0)
    def _():
        put_rows(b_ref, b_parts)
        spread_rows(dy_ref, dy_parts)

    @pl.when(step < steps)
    def _():
        here = pl.ds(pl.multiple_of(step * each, each), each)
        gate = dot(b_ref[...], gate_ref[...])
        upper = dot(b_ref[...], up_ref[...])
        grad = dot(dy_ref[...], down_ref[...])
        sigmoid = 1.0 / (1.0 + jnp.exp(-gate))
        swish = gate * sigmoid
        made = (
            (grad * upper * sigmoid * (1.0 + gate * (1.0 - sigmoid))).astype(BF16),
            (grad * swish).astype(BF16),
            (swish * upper).astype(BF16),
        )
        for k, value in enumerate(made):
            turned_ref[k] = jnp.transpose(value)
        dg_ref[:, here] = made[0]
        du_ref[:, here] = made[1]
        hidden_ref[...] = made[2]

    @pl.when(step >= steps)
    def _():
        part = dot_nt(dg_ref[...], rows_ref[:, :units])
        part = (part + dot_nt(du_ref[...], rows_ref[:, units:])).astype(BF16)
        keep_ref[...] = part[:half]
        send_ref[...] = part[half:]


def mlp(b_parts, dy_parts, mlp_w, after):
    half, width = dy_parts[0].shape
    units, each, rows = mlp_w.shape[1] // 3, 512, 512
    steps, more = units // each, width // rows
    vmem = pl.BlockSpec(memory_space=pltpu.VMEM)

    def first(i):
        return jnp.minimum(i, steps - 1)

    def second(i):
        return jnp.maximum(i - steps, 0)

    def body(*refs):
        mlp_kernel(*refs[:17], *refs[17 + len(after) :])

    return pl.pallas_call(
        body,
        grid=(steps + more,),
        out_shape=(
            jax.ShapeDtypeStruct((half, width), BF16),
            jax.ShapeDtypeStruct((half, width), BF16),
            jax.ShapeDtypeStruct((3, units, 2 * half), BF16),
            jax.ShapeDtypeStruct((2 * half, units), BF16),
        ),
        in_specs=[vmem] * 13
        + [
            pl.BlockSpec((width, each), lambda i: (0, first(i))),
            pl.BlockSpec((width, each), lambda i: (0, steps + first(i))),
            pl.BlockSpec((width, each), lambda i: (0, 2 * steps + first(i))),
            pl.BlockSpec((rows, 2 * units), lambda i: (second(i), 0)),
        ]
        + [pl.BlockSpec(memory_space=pl.ANY)] * len(after),
        out_specs=(
            pl.BlockSpec((half, rows), lambda i: (0, second(i))),
            pl.BlockSpec((half, rows), lambda i: (0, second(i))),
            pl.BlockSpec((3, each, 2 * half), lambda i: (0, first(i), 0)),
            pl.BlockSpec((2 * half, each), lambda i: (0, first(i))),
        ),
        scratch_shapes=[pltpu.VMEM((2 * half, width), BF16)] * 2
        + [pltpu.VMEM((2 * half, units), BF16)] * 2,
        compiler_params=pltpu.CompilerParams(vmem_limit_bytes=VMEM_LIMIT),
        cost_estimate=pl.CostEstimate(
            flops=20 * half * width * units, bytes_accessed=1, transcendentals=0
        ),
        name="mlp",
    )(*b_parts, *dy_parts, *[mlp_w] * 4, *after)


def down_kernel(hidden_ref, w_ref, keep_ref, send_ref):
    half = keep_ref.shape[0]
    for c in range(0, keep_ref.shape[1], 512):
        part = dot_nt(hidden_ref[...], w_ref[c : c + 512, :]).astype(BF16)
        keep_ref[:, c : c + 512] = part[:half]
        send_ref[:, c : c + 512] = part[half:]


def down(hidden, mlp_w, after):
    (rows, units), width = hidden.shape, mlp_w.shape[0]
    spec = pl.BlockSpec((width, units), lambda i: (0, 2))
    outs = [((rows // 2, width), BF16)] * 2
    flops = 2 * rows * width * units
    return call(down_kernel, "down", outs, [], [hidden, mlp_w], after, flops=flops, specs={1: spec})


def spread_rows(to_ref, parts):
    own, near, *other = parts
    half = own.shape[0] // 2
    other = other[0] if other else near.at[half:]
    put_rows(to_ref, [own.at[:half], near.at[:half], own.at[half:], other])


def put_blocks(out_ref, row, column, product):
    for r in range(0, product.shape[1], HEAD):
        for c in range(0, product.shape[0], HEAD):
            out_ref[row + r // HEAD, column + c // HEAD] = product[c : c + HEAD, r : r + HEAD]


def mlp_grads_kernel(*refs, units):
    b_parts, dy_parts = refs[:10], refs[10:13]
    left_ref, out_ref, b_ref, dy_ref = refs[13:]
    step = pl.program_id(0)
    later = 2 * units // left_ref.shape[0]

    @pl.when(step == 0)
    def _():
        put_rows(b_ref, b_parts)
        spread_rows(dy_ref, dy_parts)

    def work(right_ref):
        for r in range(0, right_ref.shape[1], 512):
            product = dot(left_ref[...], right_ref[:, r : r + 512]).astype(BF16)
            put_blocks(out_ref, r // HEAD, 0, product)

    pl.when(step < later)(lambda: work(b_ref))
    pl.when(step >= later)(lambda: work(dy_ref))


def mlp_grads(b_parts, dy_parts, turned):
    rows, tokens = turned.shape
    width, step = b_parts[0].shape[1], 512
    vmem = pl.BlockSpec(memory_space=pltpu.VMEM)
    return pl.pallas_call(
        functools.partial(mlp_grads_kernel, units=rows // 3),
        grid=(rows // step,),
        out_shape=jax.ShapeDtypeStruct((width // HEAD, rows // HEAD, HEAD, HEAD), BF16),
        in_specs=[vmem] * 13 + [pl.BlockSpec((step, tokens), lambda i: (i, 0))],
        out_specs=pl.BlockSpec(
            (width // HEAD, step // HEAD, HEAD, HEAD), lambda i: (0, i, 0, 0)
        ),
        scratch_shapes=[pltpu.VMEM((tokens, width), BF16)] * 2,
        compiler_params=pltpu.CompilerParams(vmem_limit_bytes=VMEM_LIMIT),
        cost_estimate=pl.CostEstimate(
            flops=2 * rows * tokens * width, bytes_accessed=1, transcendentals=0
        ),
        name="mlp_grads",
    )(*b_parts, *dy_parts, turned)


def outward_kernel(*refs):
    parts, (w_ref, do_ref, m_ref) = refs[:10], refs[10:]
    put_rows(m_ref, parts)
    part = dot(m_ref[...], w_ref[...]).astype(BF16)
    half = part.shape[0] // 2
    for head in range(2):
        for ds in range(2):
            do_ref[head * 2 + ds] = part[
                ds * half : (ds + 1) * half, head * HEAD : (head + 1) * HEAD
            ]


def outward(m_parts, attn_w):
    width = attn_w.shape[0]
    half = sum(v.shape[0] for v in m_parts) // 2
    return call(
        outward_kernel,
        "outward",
        [((4, half, HEAD), BF16)],
        [],
        [*m_parts, attn_w],
        scratch=[pltpu.VMEM((2 * half, width), BF16)],
        flops=8 * half * width * HEAD,
    )[0]


def back_kernel(*refs):
    parts, m_parts, (dq_ref, dkv_ref, cos_ref, sin_ref, o_ref, w_ref) = refs[:3], refs[3:13], refs[13:19]
    keep_ref, send_ref, out_ref, back_ref, a_ref = refs[19:]
    spread_rows(a_ref, parts)
    half = dq_ref.shape[1]
    cosine, sine = cos_ref[...], sin_ref[...]
    for part in range(3):
        for head in range(2):
            for ds in range(2):
                unit = head * 2 + ds
                rows = slice(ds * half, (ds + 1) * half)
                e = (dq_ref[unit] if part == 0 else dkv_ref[unit, part - 1]).astype(F32)
                if part < 2:
                    e = e * cosine[rows] - pltpu.roll(e, HEAD // 2, 1) * sine[rows]
                column = (part * 2 + head) * HEAD
                back_ref[rows, column : column + HEAD] = e.astype(BF16)
    for c in range(0, keep_ref.shape[1], 512):
        part = dot_nt(back_ref[...], w_ref[c : c + 512, :]).astype(BF16)
        keep_ref[:, c : c + 512] = part[:half]
        send_ref[:, c : c + 512] = part[half:]
    for c in range(0, back_ref.shape[1], 2 * HEAD):
        left = jnp.transpose(back_ref[:, c : c + 2 * HEAD])
        for r in range(0, a_ref.shape[1], 512):
            product = dot(left, a_ref[:, r : r + 512]).astype(BF16)
            put_blocks(out_ref, r // HEAD, c // HEAD, product)
    put_rows(a_ref, m_parts)
    left = jnp.concatenate([jnp.transpose(o_ref[k]) for k in range(2)], axis=0)
    for r in range(0, a_ref.shape[1], 512):
        put_blocks(out_ref, r // HEAD, 6, dot(left, a_ref[:, r : r + 512]).astype(BF16))


def backward(a_parts, m_parts, dq, dkv, cosine, sine, o_heads, attn_w, after):
    half, width = dq.shape[1], attn_w.shape[0]
    return call(
        back_kernel,
        "backward",
        [((half, width), BF16)] * 2 + [((width // HEAD, 8, HEAD, HEAD), BF16)],
        [],
        [*a_parts, *m_parts, dq, dkv, cosine, sine, o_heads, attn_w],
        after,
        scratch=[
            pltpu.VMEM((2 * half, 6 * HEAD), BF16),
            pltpu.VMEM((2 * half, width), BF16),
        ],
        flops=48 * half * width * HEAD,
    )


def total_kernel(at, terms_ref, keep_ref, send_ref):
    rows = keep_ref.shape[1]
    for c in range(keep_ref.shape[0]):
        total = terms_ref[0, c].astype(F32)
        for p in range(1, terms_ref.shape[0]):
            total = total + terms_ref[p, c].astype(F32)
        total = jnp.transpose(total)
        first, second = total[:rows], total[rows:]
        keep_ref[c] = jnp.where(at[0] == 0, first, second).astype(BF16)
        send_ref[c] = jnp.where(at[0] == 0, second, first).astype(BF16)


def total(zl, terms, after=()):
    outs = [((terms.shape[1], HEAD // 2, HEAD), BF16)] * 2
    return call(total_kernel, "total", outs, [(zl,)], [terms], after)


def place_kernel(at, keep_ref, got_ref, *outs):
    block = 0
    for out_ref in outs:
        half = out_ref.shape[1] // 2
        for c in range(0, half, HEAD):
            keep, got = keep_ref[block].astype(F32), got_ref[block].astype(F32)
            out_ref[:, c : c + HEAD] = jnp.where(at[0] == 0, keep, got)
            out_ref[:, half + c : half + c + HEAD] = jnp.where(at[0] == 0, got, keep)
            block += 1


def place(zl, sums, widths, after=()):
    keep, send = total(zl, sums, after)
    outs = [((HEAD // 2, 2 * w), F32) for w in widths]
    return call(place_kernel, "place", outs, [(zl,)], [keep, flip(send, zl=1)])


def finish_kernel(at, own_ref, far_ref, pair_ref, out_ref):
    tile = own_ref.shape[0]
    co, zh = at[0], at[1]
    lane = lax.broadcasted_iota(jnp.int32, (tile, HEAD), 1)
    for k in range(4):
        ref, start = ((own_ref, 0), (far_ref, 0), (pair_ref, 0), (pair_ref, tile))[k]
        at_row = ((k // 2) ^ co) * 2 + ((k % 2) ^ zh)
        rows = pl.ds(pl.multiple_of(at_row * tile, tile), tile)
        for y in range(NY):
            for half in range(NX // 2):
                pair = [
                    ref[start : start + tile, c : c + HEAD].astype(F32)
                    for c in ((y * NX + 2 * half) * HEAD, (y * NX + 2 * half + 1) * HEAD)
                ]
                turned = [pltpu.roll(v, HEAD // 2, 1) for v in pair]
                low = jnp.where(lane < HEAD // 2, pair[0], turned[1])
                high = jnp.where(lane < HEAD // 2, turned[0], pair[1])
                for zl, value in enumerate((low, high)):
                    column = (y * NZL + zl) * NX * HEAD // 2 + half * HEAD
                    out_ref[rows, column : column + HEAD] = value.astype(out_ref.dtype)


def finish(co, zh, own, dtype):
    far = flip(own, zh=1)
    pair = flip(jnp.concatenate([own, far], axis=0), co=1)
    vmem = pl.BlockSpec(memory_space=pltpu.VMEM)
    return pl.pallas_call(
        finish_kernel,
        out_shape=jax.ShapeDtypeStruct((4 * own.shape[0], own.shape[1]), dtype),
        in_specs=[pl.BlockSpec(memory_space=pltpu.SMEM)] + [vmem] * 3,
        out_specs=vmem,
        compiler_params=pltpu.CompilerParams(vmem_limit_bytes=VMEM_LIMIT),
        cost_estimate=pl.CostEstimate(flops=1, bytes_accessed=1, transcendentals=0),
        name="finish",
    )(jnp.stack([co, zh]).astype(jnp.int32), own, far, pair)


def local(
    tokens_in,
    w_query,
    w_key,
    w_value,
    w_output,
    w_gate,
    w_up,
    w_down,
    grad_out,
    block_ids,
    tile_order,
):
    own, width = tokens_in.shape
    seqs, length = block_ids.shape
    tile = length // tile_order.shape[1]
    wide = w_query.shape[1] // 2
    units = w_gate.shape[1] // 2
    piece = w_query.shape[0]
    ctx, tp = lax.axis_index("ctx"), lax.axis_index("tp")
    y, zl, x = ctx // (NZL * NX), (ctx // NX) % NZL, ctx % NX
    zh, co = tp // 2, tp % 2

    def pair_rows(arrays):
        def cut(array, which):
            half = array.shape[1] // 2
            return lax.dynamic_slice_in_dim(array, which * half, half, 1)

        kept = jnp.concatenate([cut(array, zl) for array in arrays], axis=1)
        sent = jnp.concatenate([cut(array, 1 - zl) for array in arrays], axis=1)
        return turn(jnp.stack([kept, flip(sent, zl=1)]), 0, zl).reshape(2 * piece, -1)

    pair = pair_rows((w_query, w_key, w_value))
    copies = plane_copies(pair)
    attn_w = plane_gather(copies)
    first_own, grads, x_own = enter(co, zh, tokens_in, grad_out, [copies])
    near = flip(first_own[: own // 2], zl=1)
    first_low = [first_own, near, flip(near, co=1)]
    started = (near[0, 0] * 0).astype(jnp.int32)
    pair = pair_rows([hold(w, near) for w in (w_gate, w_up, w_down, w_output)])

    tiles = (tile_order + started).reshape(seqs, NY, NZL, NX, 2)
    tiles = turn(turn(turn(tiles, 0, co), 2, zl), 4, zh)
    row_tiles = lax.dynamic_index_in_dim(tiles, y, 1, keepdims=False)
    own_tiles = lax.dynamic_index_in_dim(row_tiles, x, 2, keepdims=False).reshape(-1)
    positions = (own_tiles[:, None] * tile + jnp.arange(tile, dtype=jnp.int32)).reshape(-1)
    inverse = 10000.0 ** (-jnp.arange(0, HEAD, 2, dtype=F32) / HEAD)
    angles = positions.astype(F32)[:, None] * inverse[None, :]
    cosine = jnp.concatenate([jnp.cos(angles)] * 2, axis=-1)
    sine = jnp.concatenate([-jnp.sin(angles), jnp.sin(angles)], axis=-1)
    ds_own = x % 2
    unit_tiles = lax.dynamic_index_in_dim(tiles, ds_own, 0, keepdims=False)
    turns = (y + jnp.arange(NY, dtype=jnp.int32)) % NY
    key_tiles = jnp.swapaxes(jnp.take(unit_tiles, turns, axis=0), 1, 2).reshape(-1)
    query_tiles = lax.dynamic_index_in_dim(unit_tiles, y, 0, keepdims=False)
    query_tiles = jnp.swapaxes(query_tiles, 0, 1).reshape(-1)
    tile_count, query_count = key_tiles.shape[0], query_tiles.shape[0]
    rank = jnp.sum(query_tiles[None, :] < query_tiles[:, None], axis=1)
    places = jnp.arange(query_count, dtype=jnp.int32)
    order = jnp.sum(
        jnp.where(rank[None, :] == places[:, None], places[None, :], 0), axis=1
    ).astype(jnp.int32)
    sorted_tiles = jnp.sum(
        jnp.where(rank[None, :] == places[:, None], query_tiles[None, :], 0), axis=1
    )
    key_blocks = lax.dynamic_index_in_dim(block_ids + started, ds_own ^ co, 0, keepdims=False)
    query_blocks = jnp.take(key_blocks.reshape(tile_count, tile), sorted_tiles, axis=0).reshape(-1)
    by_block = query_blocks.reshape(-1, QB)
    sure = jnp.sum(key_blocks[None, :] <= by_block[:, :1], axis=1) // KC
    most = (jnp.sum(key_blocks[None, :] <= by_block[:, -1:], axis=1) + KC - 1) // KC
    scalars = jnp.concatenate([key_tiles, order, sure, most]).astype(jnp.int32)
    query_rows = jnp.broadcast_to(by_block[:, None, :], (by_block.shape[0], 8, QB))

    query_column, key_column = query_blocks[:, None], key_blocks[:, None]
    tables = [scalars, query_column]
    qkv_send = project(first_low, attn_w, cosine, sine, tables)
    half = own

    def across(values):
        return lax.all_to_all(values, "ctx", 0, 0, tiled=True, axis_index_groups=X_GROUPS)

    line = across(qkv_send)
    q, kv_line = line[:, 0].reshape(query_count, tile, HEAD), line[:, 1:]
    near = flip(hold(grads[: own // 2], qkv_send), zl=1)
    kv = ring_gather(kv_line, (), dy=1)
    mlp_w = lax.all_gather(
        hold(pair[:, : 3 * units], kv_line), "ctx", axis=0, tiled=True, axis_index_groups=XY_GROUPS
    )
    w_out = plane_gather(plane_copies(hold(pair[:, 3 * units :], line)))
    o, o_full, lse = attend(
        scalars, q, kv, query_column, key_blocks[None, :], [near]
    )
    grad_all = [grads, near, flip(hold(near, o), co=1)]
    o_heads = across(hold(o.reshape(NX, half, HEAD), w_out)).reshape(2, 2 * half, HEAD)
    attn_sum = column_sum(*output(o_heads, w_out))

    x_own = x_own.astype(F32)
    dy_own = grads[:tile].astype(F32)
    middle = x_own + attn_sum
    normed_two, inverse_two = norm(middle)
    second_low = column_gather(normed_two.astype(BF16))
    keep, send, turned, hidden = mlp(second_low, grad_all, mlp_w, [key_column, query_rows])
    terms = mlp_grads(second_low, grad_all, turned.reshape(3 * units, -1))
    sums = lax.psum_scatter(
        terms, "ctx", scatter_dimension=0, tiled=True, axis_index_groups=XY_GROUPS
    )
    back_two = column_sum(keep, send, terms)
    grad_middle = dy_own + norm_back(back_two, normed_two, inverse_two)
    middle_low = column_gather(grad_middle.astype(BF16))

    do_send = outward(middle_low, w_out)
    do = across(do_send).reshape(query_count, tile, HEAD)
    out_keep, out_send = down(hidden, mlp_w, [do_send])
    dq, dkv, *others = attend_back(
        scalars,
        q,
        kv,
        do,
        o_full,
        lse,
        query_rows,
        key_column,
        [out_keep],
    )
    pairs = [(dkv[:2], dkv[2:])] + [tuple(others[2 * k : 2 * k + 2]) for k in range(3)]
    dkv = jnp.concatenate(ring_sum(pairs, dy=1), axis=0).astype(BF16)
    out_sum = column_sum(hold(out_keep, dq), hold(out_send, dq))
    dq = across(dq.reshape(NX, half, HEAD))
    dkv = across(hold(dkv, dq))
    out_low = (middle + out_sum).astype(BF16)
    keep, send, terms = backward(
        first_low, middle_low, dq, dkv, cosine, sine, o_heads, attn_w, [out_low]
    )
    terms = lax.all_to_all(terms, "ctx", 0, 0, tiled=True, axis_index_groups=XY_GROUPS)
    back_one = column_sum(keep, send)
    normed_own, inverse_own = norm(x_own)
    grad_own = grad_middle + norm_back(back_one, normed_own, inverse_own)
    grad_in = finish(co, zh, grad_own.astype(BF16), F32)
    tokens_out = finish(co, zh, out_low, BF16)
    mlp_out = place(zl, sums, (units,) * 3, [send])
    return (
        tokens_out,
        grad_in,
        *place(zl, terms, (wide,) * 4, [grad_in, tokens_out, mlp_out[0]]),
        *mlp_out,
    )


def solution(mesh):
    row, both = P("ctx", None), P("ctx", "tp")
    return jax.shard_map(
        local,
        mesh=mesh,
        in_specs=(row,) + (both,) * 7 + (row, P(), P()),
        out_specs=(row, row) + (both,) * 7,
        check_vma=False,
    )
```

```python
import functools

import jax
import jax.numpy as jnp
from jax import lax
from jax.experimental import pallas as pl
from jax.experimental.pallas import tpu as pltpu
from jax.sharding import PartitionSpec as P

HEAD = 128
NY, NZL, NX = 4, 2, 4
BOTH = ("ctx", "tp")
QB = 256
KC = 1024
LOG2E = 1.4426950408889634
VMEM_LIMIT = 56 * 1024 * 1024
F32, BF16 = jnp.float32, jnp.bfloat16


def ctx_index(y, zl, x):
    return (y * NZL + zl) * NX + x


XY_GROUPS = [
    [ctx_index(y, zl, x) for y in range(NY) for x in range(NX)] for zl in range(NZL)
]
X_GROUPS = [
    [ctx_index(y, zl, x) for x in range(NX)] for y in range(NY) for zl in range(NZL)
]


def flip(values, zl=0, zh=0, co=0):
    pairs = []
    for y in range(NY):
        for a in range(NZL):
            for x in range(NX):
                for t in range(4):
                    here = ctx_index(y, a, x) * 4 + t
                    there = ctx_index(y, a ^ zl, x) * 4 + (t ^ (2 * zh + co))
                    pairs.append((here, there))
    return lax.ppermute(values, BOTH, pairs)


def ring(values, dx=0, dy=0):
    pairs = [
        (ctx_index(y, a, x), ctx_index((y + dy) % NY, a, (x + dx) % NX))
        for y in range(NY)
        for a in range(NZL)
        for x in range(NX)
    ]
    return lax.ppermute(values, "ctx", pairs)


def turn(values, axis, bit):
    return jnp.where(bit == 1, jnp.flip(values, axis), values)


def norm(values):
    average = jnp.mean(values, axis=-1, keepdims=True)
    centred = values - average
    inverse = lax.rsqrt(jnp.mean(centred * centred, axis=-1, keepdims=True) + 1e-05)
    return centred * inverse, inverse


def norm_back(grad, normed, inverse):
    first = jnp.mean(grad, axis=-1, keepdims=True)
    second = jnp.mean(grad * normed, axis=-1, keepdims=True)
    return inverse * (grad - first - normed * second)


def column_sum(keep, send, token=None):
    rows = keep.shape[0] // 4
    cut = rows // 2
    got = flip(send, co=1)
    half = keep.astype(F32) + got.astype(F32)
    if token is not None:
        half = hold(half, token)
    own, far, near, both = (half[k * rows : (k + 1) * rows] for k in range(4))
    for_both = flip(far[:cut].astype(BF16), zl=1)
    for_near = flip(far[cut:].astype(BF16), zl=1, zh=1)
    near = jnp.concatenate([near[:cut], near[cut:] + for_near.astype(F32)], axis=0).astype(BF16)
    both = jnp.concatenate([both[:cut] + for_both.astype(F32), both[cut:]], axis=0).astype(BF16)
    from_near, from_both = flip(near, zl=1), flip(both, zl=1, zh=1)
    return own + from_near.astype(F32) + from_both.astype(F32), near


def column_gather(rows):
    cut = rows.shape[0] // 2
    near, both = flip(rows, zl=1), flip(rows, zl=1, zh=1)
    far_low, far_high = flip(both[:cut], zl=1), flip(near[cut:], zl=1, zh=1)
    half = [rows, far_low, far_high, near, both]
    return half + [flip(piece, co=1) for piece in half]


def ring_sum(parts, **step):
    forth, back = step, {k: -v for k, v in step.items()}
    ahead, behind = ring(parts[2][0], **forth), ring(parts[2][1], **back)
    from_back, from_forth = ring(parts[1][1], **forth), ring(parts[3][0], **back)
    low = parts[1][0].astype(F32) + ahead.astype(F32)
    high = parts[3][1].astype(F32) + behind.astype(F32)
    low, high = ring(low.astype(BF16), **forth), ring(high.astype(BF16), **back)
    return (
        parts[0][0].astype(F32) + low.astype(F32) + from_forth.astype(F32),
        parts[0][1].astype(F32) + from_back.astype(F32) + high.astype(F32),
    )


def ring_gather(rows, tokens, **step):
    forth, back = step, {k: -v for k, v in step.items()}
    cut = rows.shape[0] // 2
    before, after = ring(rows, **forth), ring(rows, **back)
    low, high = before[:cut], after[cut:]
    for one in tokens:
        low, high = hold(low, one), hold(high, one)
    low, high = ring(low, **forth), ring(high, **back)
    return rows, after, low, high, before


def plane_copies(rows):
    return jnp.broadcast_to(rows[None], (NY * NX,) + rows.shape)


def plane_gather(copies):
    every = lax.all_to_all(copies, "ctx", 0, 0, tiled=True, axis_index_groups=XY_GROUPS)
    return every.reshape(-1, copies.shape[2])


def dot(left, right):
    return jnp.dot(left, right, preferred_element_type=F32)


def dot_nt(left, right):
    return lax.dot_general(left, right, (((1,), (1,)), ((), ())), preferred_element_type=F32)


def dot_tn(left, right):
    return lax.dot_general(left, right, (((0,), (0,)), ((), ())), preferred_element_type=F32)


def call(kernel, name, outs, scalars, arrays, after=(), scratch=(), flops=1, specs=None):
    head, tail = len(scalars) + len(arrays), len(after)
    vmem = pl.BlockSpec(memory_space=pltpu.VMEM)
    specs = specs or {}
    grid = {"grid": (1,)} if specs else {}

    def body(*refs):
        kernel(*refs[:head], *refs[head + tail :])

    return pl.pallas_call(
        body,
        **grid,
        out_shape=tuple(jax.ShapeDtypeStruct(shape, dtype) for shape, dtype in outs),
        in_specs=[pl.BlockSpec(memory_space=pltpu.SMEM)] * len(scalars)
        + [specs.get(k, vmem) for k in range(len(arrays))]
        + [pl.BlockSpec(memory_space=pl.ANY)] * tail,
        out_specs=(vmem,) * len(outs),
        scratch_shapes=list(scratch),
        compiler_params=pltpu.CompilerParams(vmem_limit_bytes=VMEM_LIMIT),
        cost_estimate=pl.CostEstimate(flops=flops, bytes_accessed=1, transcendentals=0),
        name=name,
    )(*[jnp.stack(s).astype(jnp.int32) for s in scalars], *arrays, *after)


def hold(values, token):
    return values + (token.reshape(-1)[0] * 0).astype(values.dtype)


def put_rows(to_ref, refs):
    row = 0
    for ref in refs:
        to_ref[row : row + ref.shape[0], :] = ref[...]
        row += ref.shape[0]


def enter_kernel(at, x_ref, dy_ref, a_ref, dy_out, own_ref):
    tile = own_ref.shape[0]
    lane = lax.broadcasted_iota(jnp.int32, (tile, HEAD), 1)
    for k in range(4):
        row = ((k // 2) ^ at[0]) * 2 + ((k % 2) ^ at[1])
        rows = pl.ds(pl.multiple_of(row * tile, tile), tile)
        x = x_ref[rows, :].astype(F32)
        values = [(norm(x)[0], a_ref), (dy_ref[rows, :].astype(F32), dy_out)]
        if k == 0:
            values.append((x, own_ref))
        for value, to_ref in values:
            for y in range(NY):
                for half in range(NX // 2):
                    pair = [
                        value[:, c : c + HEAD]
                        for c in [(y * NZL + z) * NX * HEAD // 2 + half * HEAD for z in range(2)]
                    ]
                    turned = [pltpu.roll(v, HEAD // 2, 1) for v in pair]
                    low = jnp.where(lane < HEAD // 2, pair[0], turned[1])
                    high = jnp.where(lane < HEAD // 2, turned[0], pair[1])
                    for n, v in enumerate((low, high)):
                        c = (y * NX + 2 * half + n) * HEAD
                        to_ref[k * tile : (k + 1) * tile, c : c + HEAD] = v.astype(BF16)


def enter(co, zh, x, dy, after):
    rows, width = x.shape
    outs = [((rows, width), BF16)] * 2 + [((rows // 4, width), BF16)]
    return call(enter_kernel, "enter", outs, [(co, zh)], [x, dy], after)


def each_piece(pairs):
    own, after, low, high, before = pairs
    for dy in range(NY):
        for x in range(NX):
            ref = (own, after, (low, high)[x // 2], before)[dy]
            for k in range(4):
                yield (dy * NX + x) * 4 + k, x % 2 if dy == 2 else x, k, ref


def sort_pairs(scalars, pairs, keys, values, tile):
    for slot, x, k, ref in each_piece(pairs):
        rows = pl.ds(pl.multiple_of(scalars[slot] * tile, tile), tile)
        keys[rows, :] = ref[x, 0, k * tile : (k + 1) * tile]
        values[rows, :] = ref[x, 1, k * tile : (k + 1) * tile]


def attend_kernel(
    scalars, q_ref, kv0, kv1, kv2, kv3, kv4, qblk, kblk, o_ref, full_ref, lse_ref, keys, values, queries, *, tile
):
    tiles = keys.shape[0] // tile
    per = QB // tile
    blocks = q_ref.shape[0] // per
    factor = HEAD**-0.5 * LOG2E
    sort_pairs(scalars, (kv0, kv1, kv2, kv3, kv4), keys, values, tile)

    def block(i, carry):
        for k in range(per):
            queries[k * tile : (k + 1) * tile, :] = q_ref[scalars[tiles + i * per + k]]
        q_own = queries[...]
        rows = pl.ds(pl.multiple_of(i * QB, QB), QB)

        def chunk(c, state, masked):
            top, total, acc = state
            where = pl.ds(pl.multiple_of(c * KC, KC), KC)
            s = dot_nt(q_own, keys[where, :])
            if masked:
                s = jnp.where(qblk[rows, :] >= kblk[:, where], s, -1e30)
            new = jnp.maximum(top, jnp.max(s, axis=-1, keepdims=True))
            p = jnp.exp2((s - new) * factor)
            shrink = jnp.exp2((top - new) * factor)
            total = total * shrink + jnp.sum(p, axis=-1, keepdims=True)
            acc = acc * shrink + dot(p.astype(BF16), values[where, :])
            return new, total, acc

        base = tiles + blocks * per
        state = (
            jnp.full((QB, 1), -1e30, F32),
            jnp.zeros((QB, 1), F32),
            jnp.zeros((QB, HEAD), F32),
        )
        first, last = scalars[base + i], scalars[base + blocks + i]
        state = lax.fori_loop(0, first, functools.partial(chunk, masked=False), state)
        top, total, acc = lax.fori_loop(first, last, functools.partial(chunk, masked=True), state)
        out = acc / total
        full_ref[rows, :] = out
        low = out.astype(BF16)
        for k in range(per):
            o_ref[scalars[tiles + i * per + k]] = low[k * tile : (k + 1) * tile]
        lse = top * factor + jnp.log2(total)
        lse_ref[i] = jnp.transpose(jnp.broadcast_to(lse, (QB, HEAD)))[:8]
        return carry

    lax.fori_loop(0, blocks, block, 0)


def attend(scalars, q, kv, qblk, kblk, after):
    tile = q.shape[1]
    count = q.shape[0] * tile
    length = kblk.shape[1]
    vmem = pl.BlockSpec(memory_space=pltpu.VMEM)
    kernel = functools.partial(attend_kernel, tile=tile)

    def body(*refs):
        kernel(*refs[:9], *refs[9 + len(after) :])

    return pl.pallas_call(
        body,
        out_shape=(
            jax.ShapeDtypeStruct(q.shape, BF16),
            jax.ShapeDtypeStruct((count, HEAD), F32),
            jax.ShapeDtypeStruct((count // QB, 8, QB), F32),
        ),
        in_specs=[pl.BlockSpec(memory_space=pltpu.SMEM)]
        + [vmem] * 8
        + [pl.BlockSpec(memory_space=pl.ANY)] * len(after),
        out_specs=(vmem,) * 3,
        scratch_shapes=[
            pltpu.VMEM((length, HEAD), BF16),
            pltpu.VMEM((length, HEAD), BF16),
            pltpu.VMEM((QB, HEAD), BF16),
        ],
        compiler_params=pltpu.CompilerParams(vmem_limit_bytes=VMEM_LIMIT),
        cost_estimate=pl.CostEstimate(
            flops=32 * count * length * HEAD, bytes_accessed=1 << 22, transcendentals=count * length
        ),
        name="attend",
    )(scalars, q, *kv, qblk, kblk, *after)


def attend_back_kernel(
    scalars,
    q_ref,
    kv0,
    kv1,
    kv2,
    kv3,
    kv4,
    do_ref,
    full_ref,
    lse_ref,
    qblk,
    kblk,
    dq_ref,
    own_ref,
    after_low,
    after_high,
    far_low,
    far_high,
    before_low,
    before_high,
    keys,
    values,
    queries,
    grads,
    dk,
    dv,
    *,
    tile,
):
    tiles = keys.shape[0] // tile
    per = QB // tile
    blocks = q_ref.shape[0] // per
    scale = HEAD**-0.5
    factor = scale * LOG2E
    sort_pairs(scalars, (kv0, kv1, kv2, kv3, kv4), keys, values, tile)
    dk[...] = jnp.zeros_like(dk)
    dv[...] = jnp.zeros_like(dv)

    def block(i, carry):
        for k in range(per):
            slot = scalars[tiles + i * per + k]
            queries[k * tile : (k + 1) * tile, :] = q_ref[slot]
            grads[k * tile : (k + 1) * tile, :] = do_ref[slot]
        q_own = queries[...]
        do_own = grads[...]
        rows = pl.ds(pl.multiple_of(i * QB, QB), QB)
        product = do_own.astype(F32) * full_ref[rows, :]
        delta = jnp.sum(jnp.transpose(product), axis=0, keepdims=True)
        lse = lse_ref[i][:1]
        q_blocks = qblk[i][:1]

        def chunk(c, acc, masked):
            where = pl.ds(pl.multiple_of(c * KC, KC), KC)
            k_own = keys[where, :]
            s = dot_nt(k_own, q_own)
            if masked:
                s = jnp.where(kblk[where, :] <= q_blocks, s, -1e30)
            p = jnp.exp2(s * factor - lse)
            dp = dot_nt(values[where, :], do_own)
            ds = (p * (dp - delta)).astype(BF16)
            dv[where, :] += dot(p.astype(BF16), do_own)
            dk[where, :] += dot(ds, q_own)
            return acc + dot_tn(ds, k_own)

        base = tiles + blocks * per
        first, last = scalars[base + i], scalars[base + blocks + i]
        acc = jnp.zeros((QB, HEAD), F32)
        acc = lax.fori_loop(0, first, functools.partial(chunk, masked=False), acc)
        acc = lax.fori_loop(first, last, functools.partial(chunk, masked=True), acc)
        low = (acc * scale).astype(BF16)
        for k in range(per):
            dq_ref[scalars[tiles + i * per + k]] = low[k * tile : (k + 1) * tile]
        return carry

    lax.fori_loop(0, blocks, block, 0)

    outs = ((own_ref, own_ref), (after_low, after_high), (far_low, far_high), (before_low, before_high))
    for slot in range(tiles):
        dy, x, k = slot // 16, slot // 4 % 4, slot % 4
        rows = pl.ds(pl.multiple_of(scalars[slot] * tile, tile), tile)
        ref, x = outs[dy][x // 2], x if dy == 0 else x % 2
        here = slice(k * tile, (k + 1) * tile)
        ref[x, 0, here] = (dk[rows, :] * scale).astype(BF16)
        ref[x, 1, here] = dv[rows, :].astype(BF16)


def attend_back(scalars, q, kv, do, full, lse, qblk, kblk, after):
    tile = q.shape[1]
    count = q.shape[0] * tile
    length = kblk.shape[0]
    vmem = pl.BlockSpec(memory_space=pltpu.VMEM)
    kernel = functools.partial(attend_back_kernel, tile=tile)

    def body(*refs):
        kernel(*refs[:12], *refs[12 + len(after) :])

    return pl.pallas_call(
        body,
        out_shape=(
            jax.ShapeDtypeStruct(q.shape, BF16),
            jax.ShapeDtypeStruct(kv[0].shape, BF16),
        )
        + (jax.ShapeDtypeStruct(kv[2].shape, BF16),) * 6,
        in_specs=[pl.BlockSpec(memory_space=pltpu.SMEM)]
        + [vmem] * 11
        + [pl.BlockSpec(memory_space=pl.ANY)] * len(after),
        out_specs=(vmem,) * 8,
        scratch_shapes=[
            pltpu.VMEM((length, HEAD), BF16),
            pltpu.VMEM((length, HEAD), BF16),
            pltpu.VMEM((QB, HEAD), BF16),
            pltpu.VMEM((QB, HEAD), BF16),
            pltpu.VMEM((length, HEAD), F32),
            pltpu.VMEM((length, HEAD), F32),
        ],
        compiler_params=pltpu.CompilerParams(vmem_limit_bytes=VMEM_LIMIT),
        cost_estimate=pl.CostEstimate(
            flops=40 * count * length * HEAD, bytes_accessed=1 << 23, transcendentals=count * length
        ),
        name="attend_back",
    )(scalars, q, *kv, do, full, lse, qblk, kblk, *after)


def project_kernel(own_ref, near_ref, other_ref, w_ref, cos_ref, sin_ref, qkv_ref, a_ref):
    half = own_ref.shape[0]
    spread_rows(a_ref, (own_ref, near_ref, other_ref))
    cosine, sine = cos_ref[...], sin_ref[...]
    for part in range(3):
        product = dot(a_ref[...], w_ref[:, part * 2 * HEAD : (part + 1) * 2 * HEAD])
        for head in range(2):
            u = product[:, head * HEAD : (head + 1) * HEAD]
            if part < 2:
                u = u * cosine + pltpu.roll(u, HEAD // 2, 1) * sine
            u = u.astype(BF16)
            for ds in range(2):
                rows = u[ds * half : (ds + 1) * half]
                qkv_ref[head * 2 + ds, part] = rows


def project(a, weights, cosine, sine, after):
    half, width = a[0].shape
    return call(
        project_kernel,
        "project",
        [((4, 3, half, HEAD), BF16)],
        [],
        [*a, weights, cosine, sine],
        after,
        scratch=[pltpu.VMEM((2 * half, width), BF16)],
        flops=4 * half * width * 6 * HEAD,
    )[0]


def output_kernel(o_ref, w_ref, keep_ref, send_ref):
    half = keep_ref.shape[0]
    o = jnp.concatenate([o_ref[0], o_ref[1]], axis=1)
    for c in range(0, keep_ref.shape[1], 512):
        part = dot_nt(o, w_ref[c : c + 512, :]).astype(BF16)
        keep_ref[:, c : c + 512] = part[:half]
        send_ref[:, c : c + 512] = part[half:]


def output(o_heads, weights):
    rows, width = o_heads.shape[1], weights.shape[0]
    outs = [((rows // 2, width), BF16)] * 2
    flops = 4 * rows * width * HEAD
    return call(output_kernel, "output", outs, [], [o_heads, weights], flops=flops)


def mlp_kernel(*refs):
    b_parts, dy_parts = refs[:10], refs[10:13]
    gate_ref, up_ref, down_ref, rows_ref, keep_ref, send_ref, turned_ref, hidden_ref = refs[13:21]
    b_ref, dy_ref, dg_ref, du_ref = refs[21:]
    step = pl.program_id(0)
    half, units, each = dy_parts[0].shape[0], dg_ref.shape[1], gate_ref.shape[1]
    steps = units // each

    @pl.when(step == 0)
    def _():
        put_rows(b_ref, b_parts)
        spread_rows(dy_ref, dy_parts)

    @pl.when(step < steps)
    def _():
        here = pl.ds(pl.multiple_of(step * each, each), each)
        gate = dot(b_ref[...], gate_ref[...])
        upper = dot(b_ref[...], up_ref[...])
        grad = dot(dy_ref[...], down_ref[...])
        sigmoid = 1.0 / (1.0 + jnp.exp(-gate))
        swish = gate * sigmoid
        made = (
            (grad * upper * sigmoid * (1.0 + gate * (1.0 - sigmoid))).astype(BF16),
            (grad * swish).astype(BF16),
            (swish * upper).astype(BF16),
        )
        for k, value in enumerate(made):
            turned_ref[k] = jnp.transpose(value)
        dg_ref[:, here] = made[0]
        du_ref[:, here] = made[1]
        hidden_ref[...] = made[2]

    @pl.when(step >= steps)
    def _():
        part = dot_nt(dg_ref[...], rows_ref[:, :units])
        part = (part + dot_nt(du_ref[...], rows_ref[:, units:])).astype(BF16)
        keep_ref[...] = part[:half]
        send_ref[...] = part[half:]


def mlp(b_parts, dy_parts, mlp_w, after):
    half, width = dy_parts[0].shape
    units, each, rows = mlp_w.shape[1] // 3, 512, 512
    steps, more = units // each, width // rows
    vmem = pl.BlockSpec(memory_space=pltpu.VMEM)

    def first(i):
        return jnp.minimum(i, steps - 1)

    def second(i):
        return jnp.maximum(i - steps, 0)

    def body(*refs):
        mlp_kernel(*refs[:17], *refs[17 + len(after) :])

    return pl.pallas_call(
        body,
        grid=(steps + more,),
        out_shape=(
            jax.ShapeDtypeStruct((half, width), BF16),
            jax.ShapeDtypeStruct((half, width), BF16),
            jax.ShapeDtypeStruct((3, units, 2 * half), BF16),
            jax.ShapeDtypeStruct((2 * half, units), BF16),
        ),
        in_specs=[vmem] * 13
        + [
            pl.BlockSpec((width, each), lambda i: (0, first(i))),
            pl.BlockSpec((width, each), lambda i: (0, steps + first(i))),
            pl.BlockSpec((width, each), lambda i: (0, 2 * steps + first(i))),
            pl.BlockSpec((rows, 2 * units), lambda i: (second(i), 0)),
        ]
        + [pl.BlockSpec(memory_space=pl.ANY)] * len(after),
        out_specs=(
            pl.BlockSpec((half, rows), lambda i: (0, second(i))),
            pl.BlockSpec((half, rows), lambda i: (0, second(i))),
            pl.BlockSpec((3, each, 2 * half), lambda i: (0, first(i), 0)),
            pl.BlockSpec((2 * half, each), lambda i: (0, first(i))),
        ),
        scratch_shapes=[pltpu.VMEM((2 * half, width), BF16)] * 2
        + [pltpu.VMEM((2 * half, units), BF16)] * 2,
        compiler_params=pltpu.CompilerParams(vmem_limit_bytes=VMEM_LIMIT),
        cost_estimate=pl.CostEstimate(
            flops=20 * half * width * units, bytes_accessed=1, transcendentals=0
        ),
        name="mlp",
    )(*b_parts, *dy_parts, *[mlp_w] * 4, *after)


def down_kernel(hidden_ref, w_ref, keep_ref, send_ref):
    half = keep_ref.shape[0]
    for c in range(0, keep_ref.shape[1], 512):
        part = dot_nt(hidden_ref[...], w_ref[c : c + 512, :]).astype(BF16)
        keep_ref[:, c : c + 512] = part[:half]
        send_ref[:, c : c + 512] = part[half:]


def down(hidden, mlp_w, after):
    (rows, units), width = hidden.shape, mlp_w.shape[0]
    spec = pl.BlockSpec((width, units), lambda i: (0, 2))
    outs = [((rows // 2, width), BF16)] * 2
    flops = 2 * rows * width * units
    return call(down_kernel, "down", outs, [], [hidden, mlp_w], after, flops=flops, specs={1: spec})


def spread_rows(to_ref, parts):
    own, near, *other = parts
    half = own.shape[0] // 2
    other = other[0] if other else near.at[half:]
    put_rows(to_ref, [own.at[:half], near.at[:half], own.at[half:], other])


def put_blocks(out_ref, row, column, product):
    for r in range(0, product.shape[1], HEAD):
        for c in range(0, product.shape[0], HEAD):
            out_ref[row + r // HEAD, column + c // HEAD] = product[c : c + HEAD, r : r + HEAD]


def mlp_grads_kernel(*refs, units):
    b_parts, dy_parts = refs[:10], refs[10:13]
    left_ref, out_ref, b_ref, dy_ref = refs[13:]
    step = pl.program_id(0)
    later = 2 * units // left_ref.shape[0]

    @pl.when(step == 0)
    def _():
        put_rows(b_ref, b_parts)
        spread_rows(dy_ref, dy_parts)

    def work(right_ref):
        for r in range(0, right_ref.shape[1], 512):
            product = dot(left_ref[...], right_ref[:, r : r + 512]).astype(BF16)
            put_blocks(out_ref, r // HEAD, 0, product)

    pl.when(step < later)(lambda: work(b_ref))
    pl.when(step >= later)(lambda: work(dy_ref))


def mlp_grads(b_parts, dy_parts, turned):
    rows, tokens = turned.shape
    width, step = b_parts[0].shape[1], 512
    vmem = pl.BlockSpec(memory_space=pltpu.VMEM)
    return pl.pallas_call(
        functools.partial(mlp_grads_kernel, units=rows // 3),
        grid=(rows // step,),
        out_shape=jax.ShapeDtypeStruct((width // HEAD, rows // HEAD, HEAD, HEAD), BF16),
        in_specs=[vmem] * 13 + [pl.BlockSpec((step, tokens), lambda i: (i, 0))],
        out_specs=pl.BlockSpec(
            (width // HEAD, step // HEAD, HEAD, HEAD), lambda i: (0, i, 0, 0)
        ),
        scratch_shapes=[pltpu.VMEM((tokens, width), BF16)] * 2,
        compiler_params=pltpu.CompilerParams(vmem_limit_bytes=VMEM_LIMIT),
        cost_estimate=pl.CostEstimate(
            flops=2 * rows * tokens * width, bytes_accessed=1, transcendentals=0
        ),
        name="mlp_grads",
    )(*b_parts, *dy_parts, turned)


def outward_kernel(*refs):
    parts, (w_ref, do_ref, m_ref) = refs[:10], refs[10:]
    put_rows(m_ref, parts)
    part = dot(m_ref[...], w_ref[...]).astype(BF16)
    half = part.shape[0] // 2
    for head in range(2):
        for ds in range(2):
            do_ref[head * 2 + ds] = part[
                ds * half : (ds + 1) * half, head * HEAD : (head + 1) * HEAD
            ]


def outward(m_parts, attn_w):
    width = attn_w.shape[0]
    half = sum(v.shape[0] for v in m_parts) // 2
    return call(
        outward_kernel,
        "outward",
        [((4, half, HEAD), BF16)],
        [],
        [*m_parts, attn_w],
        scratch=[pltpu.VMEM((2 * half, width), BF16)],
        flops=8 * half * width * HEAD,
    )[0]


def back_kernel(*refs):
    parts, m_parts, (dqkv_ref, cos_ref, sin_ref, o_ref, w_ref) = refs[:3], refs[3:13], refs[13:18]
    keep_ref, send_ref, out_ref, back_ref, a_ref = refs[18:]
    spread_rows(a_ref, parts)
    half = dqkv_ref.shape[2]
    cosine, sine = cos_ref[...], sin_ref[...]
    for part in range(3):
        for head in range(2):
            for ds in range(2):
                rows = slice(ds * half, (ds + 1) * half)
                e = dqkv_ref[head * 2 + ds, part].astype(F32)
                if part < 2:
                    e = e * cosine[rows] - pltpu.roll(e, HEAD // 2, 1) * sine[rows]
                column = (part * 2 + head) * HEAD
                back_ref[rows, column : column + HEAD] = e.astype(BF16)
    for c in range(0, keep_ref.shape[1], 512):
        part = dot_nt(back_ref[...], w_ref[c : c + 512, :]).astype(BF16)
        keep_ref[:, c : c + 512] = part[:half]
        send_ref[:, c : c + 512] = part[half:]
    for c in range(0, back_ref.shape[1], 2 * HEAD):
        left = jnp.transpose(back_ref[:, c : c + 2 * HEAD])
        for r in range(0, a_ref.shape[1], 512):
            product = dot(left, a_ref[:, r : r + 512]).astype(BF16)
            put_blocks(out_ref, r // HEAD, c // HEAD, product)
    put_rows(a_ref, m_parts)
    left = jnp.concatenate([jnp.transpose(o_ref[k]) for k in range(2)], axis=0)
    for r in range(0, a_ref.shape[1], 512):
        put_blocks(out_ref, r // HEAD, 6, dot(left, a_ref[:, r : r + 512]).astype(BF16))


def backward(a_parts, m_parts, dqkv, cosine, sine, o_heads, attn_w, after):
    half, width = dqkv.shape[2], attn_w.shape[0]
    return call(
        back_kernel,
        "backward",
        [((half, width), BF16)] * 2 + [((width // HEAD, 8, HEAD, HEAD), BF16)],
        [],
        [*a_parts, *m_parts, dqkv, cosine, sine, o_heads, attn_w],
        after,
        scratch=[
            pltpu.VMEM((2 * half, 6 * HEAD), BF16),
            pltpu.VMEM((2 * half, width), BF16),
        ],
        flops=48 * half * width * HEAD,
    )


def total_kernel(at, terms_ref, keep_ref, send_ref):
    rows = keep_ref.shape[1]
    for c in range(keep_ref.shape[0]):
        total = terms_ref[0, c].astype(F32)
        for p in range(1, terms_ref.shape[0]):
            total = total + terms_ref[p, c].astype(F32)
        total = jnp.transpose(total)
        first, second = total[:rows], total[rows:]
        keep_ref[c] = jnp.where(at[0] == 0, first, second).astype(BF16)
        send_ref[c] = jnp.where(at[0] == 0, second, first).astype(BF16)


def total(zl, terms, after=()):
    outs = [((terms.shape[1], HEAD // 2, HEAD), BF16)] * 2
    return call(total_kernel, "total", outs, [(zl,)], [terms], after)


def place_kernel(at, keep_ref, got_ref, *outs):
    block = 0
    for out_ref in outs:
        half = out_ref.shape[1] // 2
        for c in range(0, half, HEAD):
            keep, got = keep_ref[block].astype(F32), got_ref[block].astype(F32)
            out_ref[:, c : c + HEAD] = jnp.where(at[0] == 0, keep, got)
            out_ref[:, half + c : half + c + HEAD] = jnp.where(at[0] == 0, got, keep)
            block += 1


def place(zl, sums, widths, after=()):
    keep, send = total(zl, sums, after)
    outs = [((HEAD // 2, 2 * w), F32) for w in widths]
    return call(place_kernel, "place", outs, [(zl,)], [keep, flip(send, zl=1)])


def finish_kernel(at, own_ref, far_ref, pair_ref, out_ref):
    tile = own_ref.shape[0]
    co, zh = at[0], at[1]
    lane = lax.broadcasted_iota(jnp.int32, (tile, HEAD), 1)
    for k in range(4):
        ref, start = ((own_ref, 0), (far_ref, 0), (pair_ref, 0), (pair_ref, tile))[k]
        at_row = ((k // 2) ^ co) * 2 + ((k % 2) ^ zh)
        rows = pl.ds(pl.multiple_of(at_row * tile, tile), tile)
        for y in range(NY):
            for half in range(NX // 2):
                pair = [
                    ref[start : start + tile, c : c + HEAD].astype(F32)
                    for c in ((y * NX + 2 * half) * HEAD, (y * NX + 2 * half + 1) * HEAD)
                ]
                turned = [pltpu.roll(v, HEAD // 2, 1) for v in pair]
                low = jnp.where(lane < HEAD // 2, pair[0], turned[1])
                high = jnp.where(lane < HEAD // 2, turned[0], pair[1])
                for zl, value in enumerate((low, high)):
                    column = (y * NZL + zl) * NX * HEAD // 2 + half * HEAD
                    out_ref[rows, column : column + HEAD] = value.astype(out_ref.dtype)


def finish(co, zh, own, dtype):
    far = flip(own, zh=1)
    pair = flip(jnp.concatenate([own, far], axis=0), co=1)
    vmem = pl.BlockSpec(memory_space=pltpu.VMEM)
    return pl.pallas_call(
        finish_kernel,
        out_shape=jax.ShapeDtypeStruct((4 * own.shape[0], own.shape[1]), dtype),
        in_specs=[pl.BlockSpec(memory_space=pltpu.SMEM)] + [vmem] * 3,
        out_specs=vmem,
        compiler_params=pltpu.CompilerParams(vmem_limit_bytes=VMEM_LIMIT),
        cost_estimate=pl.CostEstimate(flops=1, bytes_accessed=1, transcendentals=0),
        name="finish",
    )(jnp.stack([co, zh]).astype(jnp.int32), own, far, pair)


def local(
    tokens_in,
    w_query,
    w_key,
    w_value,
    w_output,
    w_gate,
    w_up,
    w_down,
    grad_out,
    block_ids,
    tile_order,
):
    own, width = tokens_in.shape
    seqs, length = block_ids.shape
    tile = length // tile_order.shape[1]
    wide = w_query.shape[1] // 2
    units = w_gate.shape[1] // 2
    piece = w_query.shape[0]
    ctx, tp = lax.axis_index("ctx"), lax.axis_index("tp")
    y, zl, x = ctx // (NZL * NX), (ctx // NX) % NZL, ctx % NX
    zh, co = tp // 2, tp % 2

    def pair_rows(arrays):
        def cut(array, which):
            half = array.shape[1] // 2
            return lax.dynamic_slice_in_dim(array, which * half, half, 1)

        kept = jnp.concatenate([cut(array, zl) for array in arrays], axis=1)
        sent = jnp.concatenate([cut(array, 1 - zl) for array in arrays], axis=1)
        return turn(jnp.stack([kept, flip(sent, zl=1)]), 0, zl).reshape(2 * piece, -1)

    pair = pair_rows((w_query, w_key, w_value))
    copies = plane_copies(pair)
    attn_w = plane_gather(copies)
    first_own, grads, x_own = enter(co, zh, tokens_in, grad_out, [])
    near = flip(hold(first_own[: own // 2], copies), zl=1)
    first_low = [first_own, near, flip(near, co=1)]
    started = (near[0, 0] * 0).astype(jnp.int32)
    pair = pair_rows([hold(w, near) for w in (w_gate, w_up, w_down, w_output)])

    tiles = (tile_order + started).reshape(seqs, NY, NZL, NX, 2)
    tiles = turn(turn(turn(tiles, 0, co), 2, zl), 4, zh)
    row_tiles = lax.dynamic_index_in_dim(tiles, y, 1, keepdims=False)
    own_tiles = lax.dynamic_index_in_dim(row_tiles, x, 2, keepdims=False).reshape(-1)
    positions = (own_tiles[:, None] * tile + jnp.arange(tile, dtype=jnp.int32)).reshape(-1)
    inverse = 10000.0 ** (-jnp.arange(0, HEAD, 2, dtype=F32) / HEAD)
    angles = positions.astype(F32)[:, None] * inverse[None, :]
    cosine = jnp.concatenate([jnp.cos(angles)] * 2, axis=-1)
    sine = jnp.concatenate([-jnp.sin(angles), jnp.sin(angles)], axis=-1)
    ds_own = x % 2
    unit_tiles = lax.dynamic_index_in_dim(tiles, ds_own, 0, keepdims=False)
    turns = (y + jnp.arange(NY, dtype=jnp.int32)) % NY
    key_tiles = jnp.swapaxes(jnp.take(unit_tiles, turns, axis=0), 1, 2).reshape(-1)
    query_tiles = lax.dynamic_index_in_dim(unit_tiles, y, 0, keepdims=False)
    query_tiles = jnp.swapaxes(query_tiles, 0, 1).reshape(-1)
    tile_count, query_count = key_tiles.shape[0], query_tiles.shape[0]
    rank = jnp.sum(query_tiles[None, :] < query_tiles[:, None], axis=1)
    places = jnp.arange(query_count, dtype=jnp.int32)
    order = jnp.sum(
        jnp.where(rank[None, :] == places[:, None], places[None, :], 0), axis=1
    ).astype(jnp.int32)
    sorted_tiles = jnp.sum(
        jnp.where(rank[None, :] == places[:, None], query_tiles[None, :], 0), axis=1
    )
    key_blocks = lax.dynamic_index_in_dim(block_ids + started, ds_own ^ co, 0, keepdims=False)
    query_blocks = jnp.take(key_blocks.reshape(tile_count, tile), sorted_tiles, axis=0).reshape(-1)
    by_block = query_blocks.reshape(-1, QB)
    sure = jnp.sum(key_blocks[None, :] <= by_block[:, :1], axis=1) // KC
    most = (jnp.sum(key_blocks[None, :] <= by_block[:, -1:], axis=1) + KC - 1) // KC
    scalars = jnp.concatenate([key_tiles, order, sure, most]).astype(jnp.int32)
    query_rows = jnp.broadcast_to(by_block[:, None, :], (by_block.shape[0], 8, QB))

    query_column, key_column = query_blocks[:, None], key_blocks[:, None]
    tables = [scalars, query_column]
    qkv_send = project(first_low, attn_w, cosine, sine, tables)
    half = own

    def across(values):
        return lax.all_to_all(values, "ctx", 0, 0, tiled=True, axis_index_groups=X_GROUPS)

    line = across(qkv_send)
    q, kv_line = line[:, 0].reshape(query_count, tile, HEAD), line[:, 1:]
    near = flip(hold(grads[: own // 2], qkv_send), zl=1)
    kv = ring_gather(kv_line, (), dy=1)
    mlp_w = lax.all_gather(
        hold(pair[:, : 3 * units], kv_line), "ctx", axis=0, tiled=True, axis_index_groups=XY_GROUPS
    )
    w_out = plane_gather(plane_copies(hold(pair[:, 3 * units :], line)))
    o, o_full, lse = attend(
        scalars, q, kv, query_column, key_blocks[None, :], [near]
    )
    grad_all = [grads, near, flip(hold(near, o), co=1)]
    o_heads = across(hold(o.reshape(NX, half, HEAD), w_out)).reshape(2, 2 * half, HEAD)
    attn_sum, _ = column_sum(*output(o_heads, w_out))

    x_own = x_own.astype(F32)
    dy_own = grads[:tile].astype(F32)
    middle = x_own + attn_sum
    normed_two, inverse_two = norm(middle)
    second_low = column_gather(normed_two.astype(BF16))
    keep, send, turned, hidden = mlp(second_low, grad_all, mlp_w, [key_column, query_rows])
    terms = mlp_grads(second_low, grad_all, turned.reshape(3 * units, -1))
    sums = lax.psum_scatter(
        terms, "ctx", scatter_dimension=0, tiled=True, axis_index_groups=XY_GROUPS
    )
    back_two, _ = column_sum(keep, send, terms)
    grad_middle = dy_own + norm_back(back_two, normed_two, inverse_two)
    middle_low = column_gather(grad_middle.astype(BF16))

    do_send = outward(middle_low, w_out)
    do = across(do_send).reshape(query_count, tile, HEAD)
    out_keep, out_send = down(hidden, mlp_w, [do_send])
    dq, dkv, *others = attend_back(
        scalars,
        q,
        kv,
        do,
        o_full,
        lse,
        query_rows,
        key_column,
        [out_keep],
    )
    pairs = [(dkv[:2], dkv[2:])] + [tuple(others[2 * k : 2 * k + 2]) for k in range(3)]
    dkv = jnp.concatenate(ring_sum(pairs, dy=1), axis=0).astype(BF16)
    dqkv = across(jnp.concatenate([dq.reshape(NX, 1, half, HEAD), dkv], axis=1))
    keep, send, terms = backward(
        first_low, middle_low, dqkv, cosine, sine, o_heads, attn_w, []
    )
    terms = lax.all_to_all(terms, "ctx", 0, 0, tiled=True, axis_index_groups=XY_GROUPS)
    back_one, sent = column_sum(keep, send)
    out_sum, _ = column_sum(hold(out_keep, sent), hold(out_send, sent))
    out_low = (middle + out_sum).astype(BF16)
    normed_own, inverse_own = norm(x_own)
    grad_own = grad_middle + norm_back(back_one, normed_own, inverse_own)
    grad_in = finish(co, zh, grad_own.astype(BF16), F32)
    tokens_out = finish(co, zh, out_low, BF16)
    mlp_out = place(zl, sums, (units,) * 3, [send])
    return (
        tokens_out,
        grad_in,
        *place(zl, terms, (wide,) * 4, [grad_in, tokens_out, mlp_out[0]]),
        *mlp_out,
    )


def solution(mesh):
    row, both = P("ctx", None), P("ctx", "tp")
    return jax.shard_map(
        local,
        mesh=mesh,
        in_specs=(row,) + (both,) * 7 + (row, P(), P()),
        out_specs=(row, row) + (both,) * 7,
        check_vma=False,
    )
```

```python
import functools

import jax
import jax.numpy as jnp
from jax import lax
from jax.experimental import pallas as pl
from jax.experimental.pallas import tpu as pltpu
from jax.sharding import PartitionSpec as P

HEAD = 128
NY, NZL, NX = 4, 2, 4
BOTH = ("ctx", "tp")
QB = 256
KC = 1024
LOG2E = 1.4426950408889634
VMEM_LIMIT = 56 * 1024 * 1024
F32, BF16 = jnp.float32, jnp.bfloat16


def ctx_index(y, zl, x):
    return (y * NZL + zl) * NX + x


XY_GROUPS = [
    [ctx_index(y, zl, x) for y in range(NY) for x in range(NX)] for zl in range(NZL)
]
X_GROUPS = [
    [ctx_index(y, zl, x) for x in range(NX)] for y in range(NY) for zl in range(NZL)
]


def flip(values, zl=0, zh=0, co=0):
    pairs = []
    for y in range(NY):
        for a in range(NZL):
            for x in range(NX):
                for t in range(4):
                    here = ctx_index(y, a, x) * 4 + t
                    there = ctx_index(y, a ^ zl, x) * 4 + (t ^ (2 * zh + co))
                    pairs.append((here, there))
    return lax.ppermute(values, BOTH, pairs)


def ring(values, dx=0, dy=0):
    pairs = [
        (ctx_index(y, a, x), ctx_index((y + dy) % NY, a, (x + dx) % NX))
        for y in range(NY)
        for a in range(NZL)
        for x in range(NX)
    ]
    return lax.ppermute(values, "ctx", pairs)


def turn(values, axis, bit):
    return jnp.where(bit == 1, jnp.flip(values, axis), values)


def norm(values):
    average = jnp.mean(values, axis=-1, keepdims=True)
    centred = values - average
    inverse = lax.rsqrt(jnp.mean(centred * centred, axis=-1, keepdims=True) + 1e-05)
    return centred * inverse, inverse


def norm_back(grad, normed, inverse):
    first = jnp.mean(grad, axis=-1, keepdims=True)
    second = jnp.mean(grad * normed, axis=-1, keepdims=True)
    return inverse * (grad - first - normed * second)


def column_sum(keep, send, token=None):
    rows = keep.shape[0] // 4
    cut = rows // 2
    got = flip(send, co=1)
    half = keep.astype(F32) + got.astype(F32)
    if token is not None:
        half = hold(half, token)
    own, far, near, both = (half[k * rows : (k + 1) * rows] for k in range(4))
    for_both = flip(far[:cut].astype(BF16), zl=1)
    for_near = flip(far[cut:].astype(BF16), zl=1, zh=1)
    near = jnp.concatenate([near[:cut], near[cut:] + for_near.astype(F32)], axis=0).astype(BF16)
    both = jnp.concatenate([both[:cut] + for_both.astype(F32), both[cut:]], axis=0).astype(BF16)
    from_near, from_both = flip(near, zl=1), flip(both, zl=1, zh=1)
    return own + from_near.astype(F32) + from_both.astype(F32)


def column_gather(rows):
    cut = rows.shape[0] // 2
    near, both = flip(rows, zl=1), flip(rows, zl=1, zh=1)
    far_low, far_high = flip(both[:cut], zl=1), flip(near[cut:], zl=1, zh=1)
    half = [rows, far_low, far_high, near, both]
    return half + [flip(piece, co=1) for piece in half]


def ring_sum(parts, **step):
    forth, back = step, {k: -v for k, v in step.items()}
    ahead, behind = ring(parts[2][0], **forth), ring(parts[2][1], **back)
    from_back, from_forth = ring(parts[1][1], **forth), ring(parts[3][0], **back)
    low = parts[1][0].astype(F32) + ahead.astype(F32)
    high = parts[3][1].astype(F32) + behind.astype(F32)
    low, high = ring(low.astype(BF16), **forth), ring(high.astype(BF16), **back)
    return (
        parts[0][0].astype(F32) + low.astype(F32) + from_forth.astype(F32),
        parts[0][1].astype(F32) + from_back.astype(F32) + high.astype(F32),
    )


def ring_gather(rows, tokens, **step):
    forth, back = step, {k: -v for k, v in step.items()}
    cut = rows.shape[0] // 2
    before, after = ring(rows, **forth), ring(rows, **back)
    low, high = before[:cut], after[cut:]
    for one in tokens:
        low, high = hold(low, one), hold(high, one)
    low, high = ring(low, **forth), ring(high, **back)
    return rows, after, low, high, before


def plane_copies(rows):
    return jnp.broadcast_to(rows[None], (NY * NX,) + rows.shape)


def plane_gather(copies):
    every = lax.all_to_all(copies, "ctx", 0, 0, tiled=True, axis_index_groups=XY_GROUPS)
    return every.reshape(-1, copies.shape[2])


def dot(left, right):
    return jnp.dot(left, right, preferred_element_type=F32)


def dot_nt(left, right):
    return lax.dot_general(left, right, (((1,), (1,)), ((), ())), preferred_element_type=F32)


def dot_tn(left, right):
    return lax.dot_general(left, right, (((0,), (0,)), ((), ())), preferred_element_type=F32)


def call(kernel, name, outs, scalars, arrays, after=(), scratch=(), flops=1, specs=None):
    head, tail = len(scalars) + len(arrays), len(after)
    vmem = pl.BlockSpec(memory_space=pltpu.VMEM)
    specs = specs or {}
    grid = {"grid": (1,)} if specs else {}

    def body(*refs):
        kernel(*refs[:head], *refs[head + tail :])

    return pl.pallas_call(
        body,
        **grid,
        out_shape=tuple(jax.ShapeDtypeStruct(shape, dtype) for shape, dtype in outs),
        in_specs=[pl.BlockSpec(memory_space=pltpu.SMEM)] * len(scalars)
        + [specs.get(k, vmem) for k in range(len(arrays))]
        + [pl.BlockSpec(memory_space=pl.ANY)] * tail,
        out_specs=(vmem,) * len(outs),
        scratch_shapes=list(scratch),
        compiler_params=pltpu.CompilerParams(vmem_limit_bytes=VMEM_LIMIT),
        cost_estimate=pl.CostEstimate(flops=flops, bytes_accessed=1, transcendentals=0),
        name=name,
    )(*[jnp.stack(s).astype(jnp.int32) for s in scalars], *arrays, *after)


def hold(values, token):
    return values + (token[(0,) * token.ndim] * 0).astype(values.dtype)


def put_rows(to_ref, refs):
    row = 0
    for ref in refs:
        to_ref[row : row + ref.shape[0], :] = ref[...]
        row += ref.shape[0]


def enter_kernel(at, x_ref, dy_ref, a_ref, dy_out, own_ref):
    tile = own_ref.shape[0]
    lane = lax.broadcasted_iota(jnp.int32, (tile, HEAD), 1)
    for k in range(4):
        row = ((k // 2) ^ at[0]) * 2 + ((k % 2) ^ at[1])
        rows = pl.ds(pl.multiple_of(row * tile, tile), tile)
        x = x_ref[rows, :].astype(F32)
        values = [(norm(x)[0], a_ref), (dy_ref[rows, :].astype(F32), dy_out)]
        if k == 0:
            values.append((x, own_ref))
        for value, to_ref in values:
            for y in range(NY):
                for half in range(NX // 2):
                    pair = [
                        value[:, c : c + HEAD]
                        for c in [(y * NZL + z) * NX * HEAD // 2 + half * HEAD for z in range(2)]
                    ]
                    turned = [pltpu.roll(v, HEAD // 2, 1) for v in pair]
                    low = jnp.where(lane < HEAD // 2, pair[0], turned[1])
                    high = jnp.where(lane < HEAD // 2, turned[0], pair[1])
                    for n, v in enumerate((low, high)):
                        c = (y * NX + 2 * half + n) * HEAD
                        to_ref[k * tile : (k + 1) * tile, c : c + HEAD] = v.astype(BF16)


def enter(co, zh, x, dy, after):
    rows, width = x.shape
    outs = [((rows, width), BF16)] * 2 + [((rows // 4, width), BF16)]
    return call(enter_kernel, "enter", outs, [(co, zh)], [x, dy], after)


def each_piece(pairs):
    own, after, low, high, before = pairs
    for dy in range(NY):
        for x in range(NX):
            ref = (own, after, (low, high)[x // 2], before)[dy]
            for k in range(4):
                yield (dy * NX + x) * 4 + k, x % 2 if dy == 2 else x, k, ref


def sort_pairs(scalars, pairs, keys, values, tile):
    for slot, x, k, ref in each_piece(pairs):
        rows = pl.ds(pl.multiple_of(scalars[slot] * tile, tile), tile)
        keys[rows, :] = ref[x, 0, k * tile : (k + 1) * tile]
        values[rows, :] = ref[x, 1, k * tile : (k + 1) * tile]


def attend_kernel(
    scalars, q_ref, kv0, kv1, kv2, kv3, kv4, qblk, kblk, o_ref, full_ref, lse_ref, keys, values, queries, *, tile
):
    tiles = keys.shape[0] // tile
    per = QB // tile
    blocks = q_ref.shape[0] // per
    factor = HEAD**-0.5 * LOG2E
    sort_pairs(scalars, (kv0, kv1, kv2, kv3, kv4), keys, values, tile)

    def block(i, carry):
        for k in range(per):
            queries[k * tile : (k + 1) * tile, :] = q_ref[scalars[tiles + i * per + k]]
        q_own = queries[...]
        rows = pl.ds(pl.multiple_of(i * QB, QB), QB)

        def chunk(c, state, masked):
            top, total, acc = state
            where = pl.ds(pl.multiple_of(c * KC, KC), KC)
            s = dot_nt(q_own, keys[where, :])
            if masked:
                s = jnp.where(qblk[rows, :] >= kblk[:, where], s, -1e30)
            new = jnp.maximum(top, jnp.max(s, axis=-1, keepdims=True))
            p = jnp.exp2((s - new) * factor)
            shrink = jnp.exp2((top - new) * factor)
            total = total * shrink + jnp.sum(p, axis=-1, keepdims=True)
            acc = acc * shrink + dot(p.astype(BF16), values[where, :])
            return new, total, acc

        base = tiles + blocks * per
        state = (
            jnp.full((QB, 1), -1e30, F32),
            jnp.zeros((QB, 1), F32),
            jnp.zeros((QB, HEAD), F32),
        )
        first, last = scalars[base + i], scalars[base + blocks + i]
        state = lax.fori_loop(0, first, functools.partial(chunk, masked=False), state)
        top, total, acc = lax.fori_loop(first, last, functools.partial(chunk, masked=True), state)
        out = acc / total
        full_ref[rows, :] = out
        low = out.astype(BF16)
        for k in range(per):
            o_ref[scalars[tiles + i * per + k]] = low[k * tile : (k + 1) * tile]
        lse = top * factor + jnp.log2(total)
        lse_ref[i] = jnp.transpose(jnp.broadcast_to(lse, (QB, HEAD)))[:8]
        return carry

    lax.fori_loop(0, blocks, block, 0)


def attend(scalars, q, kv, qblk, kblk, after):
    tile = q.shape[1]
    count = q.shape[0] * tile
    length = kblk.shape[1]
    vmem = pl.BlockSpec(memory_space=pltpu.VMEM)
    kernel = functools.partial(attend_kernel, tile=tile)

    def body(*refs):
        kernel(*refs[:9], *refs[9 + len(after) :])

    return pl.pallas_call(
        body,
        out_shape=(
            jax.ShapeDtypeStruct(q.shape, BF16),
            jax.ShapeDtypeStruct((count, HEAD), F32),
            jax.ShapeDtypeStruct((count // QB, 8, QB), F32),
        ),
        in_specs=[pl.BlockSpec(memory_space=pltpu.SMEM)]
        + [vmem] * 8
        + [pl.BlockSpec(memory_space=pl.ANY)] * len(after),
        out_specs=(vmem,) * 3,
        scratch_shapes=[
            pltpu.VMEM((length, HEAD), BF16),
            pltpu.VMEM((length, HEAD), BF16),
            pltpu.VMEM((QB, HEAD), BF16),
        ],
        compiler_params=pltpu.CompilerParams(vmem_limit_bytes=VMEM_LIMIT),
        cost_estimate=pl.CostEstimate(
            flops=32 * count * length * HEAD, bytes_accessed=1 << 22, transcendentals=count * length
        ),
        name="attend",
    )(scalars, q, *kv, qblk, kblk, *after)


def attend_back_kernel(
    scalars,
    q_ref,
    kv0,
    kv1,
    kv2,
    kv3,
    kv4,
    do_ref,
    full_ref,
    lse_ref,
    qblk,
    kblk,
    dq_ref,
    own_ref,
    after_low,
    after_high,
    far_low,
    far_high,
    before_low,
    before_high,
    keys,
    values,
    queries,
    grads,
    dk,
    dv,
    *,
    tile,
):
    tiles = keys.shape[0] // tile
    per = QB // tile
    blocks = q_ref.shape[0] // per
    scale = HEAD**-0.5
    factor = scale * LOG2E
    sort_pairs(scalars, (kv0, kv1, kv2, kv3, kv4), keys, values, tile)
    dk[...] = jnp.zeros_like(dk)
    dv[...] = jnp.zeros_like(dv)

    def block(i, carry):
        for k in range(per):
            slot = scalars[tiles + i * per + k]
            queries[k * tile : (k + 1) * tile, :] = q_ref[slot]
            grads[k * tile : (k + 1) * tile, :] = do_ref[slot]
        q_own = queries[...]
        do_own = grads[...]
        rows = pl.ds(pl.multiple_of(i * QB, QB), QB)
        product = do_own.astype(F32) * full_ref[rows, :]
        delta = jnp.sum(jnp.transpose(product), axis=0, keepdims=True)
        lse = lse_ref[i][:1]
        q_blocks = qblk[i][:1]

        def chunk(c, acc, masked):
            where = pl.ds(pl.multiple_of(c * KC, KC), KC)
            k_own = keys[where, :]
            s = dot_nt(k_own, q_own)
            if masked:
                s = jnp.where(kblk[where, :] <= q_blocks, s, -1e30)
            p = jnp.exp2(s * factor - lse)
            dp = dot_nt(values[where, :], do_own)
            ds = (p * (dp - delta)).astype(BF16)
            dv[where, :] += dot(p.astype(BF16), do_own)
            dk[where, :] += dot(ds, q_own)
            return acc + dot_tn(ds, k_own)

        base = tiles + blocks * per
        first, last = scalars[base + i], scalars[base + blocks + i]
        acc = jnp.zeros((QB, HEAD), F32)
        acc = lax.fori_loop(0, first, functools.partial(chunk, masked=False), acc)
        acc = lax.fori_loop(first, last, functools.partial(chunk, masked=True), acc)
        low = (acc * scale).astype(BF16)
        for k in range(per):
            dq_ref[scalars[tiles + i * per + k]] = low[k * tile : (k + 1) * tile]
        return carry

    lax.fori_loop(0, blocks, block, 0)

    outs = ((own_ref, own_ref), (after_low, after_high), (far_low, far_high), (before_low, before_high))
    for slot in range(tiles):
        dy, x, k = slot // 16, slot // 4 % 4, slot % 4
        rows = pl.ds(pl.multiple_of(scalars[slot] * tile, tile), tile)
        ref, x = outs[dy][x // 2], x if dy == 0 else x % 2
        here = slice(k * tile, (k + 1) * tile)
        ref[x, 0, here] = (dk[rows, :] * scale).astype(BF16)
        ref[x, 1, here] = dv[rows, :].astype(BF16)


def attend_back(scalars, q, kv, do, full, lse, qblk, kblk, after):
    tile = q.shape[1]
    count = q.shape[0] * tile
    length = kblk.shape[0]
    vmem = pl.BlockSpec(memory_space=pltpu.VMEM)
    kernel = functools.partial(attend_back_kernel, tile=tile)

    def body(*refs):
        kernel(*refs[:12], *refs[12 + len(after) :])

    return pl.pallas_call(
        body,
        out_shape=(
            jax.ShapeDtypeStruct(q.shape, BF16),
            jax.ShapeDtypeStruct(kv[0].shape, BF16),
        )
        + (jax.ShapeDtypeStruct(kv[2].shape, BF16),) * 6,
        in_specs=[pl.BlockSpec(memory_space=pltpu.SMEM)]
        + [vmem] * 11
        + [pl.BlockSpec(memory_space=pl.ANY)] * len(after),
        out_specs=(vmem,) * 8,
        scratch_shapes=[
            pltpu.VMEM((length, HEAD), BF16),
            pltpu.VMEM((length, HEAD), BF16),
            pltpu.VMEM((QB, HEAD), BF16),
            pltpu.VMEM((QB, HEAD), BF16),
            pltpu.VMEM((length, HEAD), F32),
            pltpu.VMEM((length, HEAD), F32),
        ],
        compiler_params=pltpu.CompilerParams(vmem_limit_bytes=VMEM_LIMIT),
        cost_estimate=pl.CostEstimate(
            flops=40 * count * length * HEAD, bytes_accessed=1 << 23, transcendentals=count * length
        ),
        name="attend_back",
    )(scalars, q, *kv, do, full, lse, qblk, kblk, *after)


def project_kernel(own_ref, near_ref, other_ref, w_ref, cos_ref, sin_ref, qkv_ref, a_ref):
    half = own_ref.shape[0]
    spread_rows(a_ref, (own_ref, near_ref, other_ref))
    cosine, sine = cos_ref[...], sin_ref[...]
    for part in range(3):
        product = dot(a_ref[...], w_ref[:, part * 2 * HEAD : (part + 1) * 2 * HEAD])
        for head in range(2):
            u = product[:, head * HEAD : (head + 1) * HEAD]
            if part < 2:
                u = u * cosine + pltpu.roll(u, HEAD // 2, 1) * sine
            u = u.astype(BF16)
            for ds in range(2):
                rows = u[ds * half : (ds + 1) * half]
                qkv_ref[head * 2 + ds, part] = rows


def project(a, weights, cosine, sine, after):
    half, width = a[0].shape
    return call(
        project_kernel,
        "project",
        [((4, 3, half, HEAD), BF16)],
        [],
        [*a, weights, cosine, sine],
        after,
        scratch=[pltpu.VMEM((2 * half, width), BF16)],
        flops=4 * half * width * 6 * HEAD,
    )[0]


def output_kernel(o_ref, w_ref, keep_ref, send_ref):
    half = keep_ref.shape[0]
    o = jnp.concatenate([o_ref[0], o_ref[1]], axis=1)
    for c in range(0, keep_ref.shape[1], 512):
        part = dot_nt(o, w_ref[c : c + 512, :]).astype(BF16)
        keep_ref[:, c : c + 512] = part[:half]
        send_ref[:, c : c + 512] = part[half:]


def output(o_heads, weights):
    rows, width = o_heads.shape[1], weights.shape[0]
    outs = [((rows // 2, width), BF16)] * 2
    flops = 4 * rows * width * HEAD
    return call(output_kernel, "output", outs, [], [o_heads, weights], flops=flops)


def mlp_kernel(*refs):
    b_parts, dy_parts = refs[:10], refs[10:13]
    gate_ref, up_ref, down_ref, rows_ref, keep_ref, send_ref, turned_ref, hidden_ref = refs[13:21]
    b_ref, dy_ref, dg_ref, du_ref = refs[21:]
    step = pl.program_id(0)
    half, units, each = dy_parts[0].shape[0], dg_ref.shape[1], gate_ref.shape[1]
    steps = units // each

    @pl.when(step == 0)
    def _():
        put_rows(b_ref, b_parts)
        spread_rows(dy_ref, dy_parts)

    @pl.when(step < steps)
    def _():
        here = pl.ds(pl.multiple_of(step * each, each), each)
        gate = dot(b_ref[...], gate_ref[...])
        upper = dot(b_ref[...], up_ref[...])
        grad = dot(dy_ref[...], down_ref[...])
        sigmoid = 1.0 / (1.0 + jnp.exp(-gate))
        swish = gate * sigmoid
        made = (
            (grad * upper * sigmoid * (1.0 + gate * (1.0 - sigmoid))).astype(BF16),
            (grad * swish).astype(BF16),
            (swish * upper).astype(BF16),
        )
        for k, value in enumerate(made):
            turned_ref[k] = jnp.transpose(value)
        dg_ref[:, here] = made[0]
        du_ref[:, here] = made[1]
        hidden_ref[...] = made[2]

    @pl.when(step >= steps)
    def _():
        part = dot_nt(dg_ref[...], rows_ref[:, :units])
        part = (part + dot_nt(du_ref[...], rows_ref[:, units:])).astype(BF16)
        keep_ref[...] = part[:half]
        send_ref[...] = part[half:]


def mlp(b_parts, dy_parts, mlp_w, after):
    half, width = dy_parts[0].shape
    units, each, rows = mlp_w.shape[1] // 3, 512, 512
    steps, more = units // each, width // rows
    vmem = pl.BlockSpec(memory_space=pltpu.VMEM)

    def first(i):
        return jnp.minimum(i, steps - 1)

    def second(i):
        return jnp.maximum(i - steps, 0)

    def body(*refs):
        mlp_kernel(*refs[:17], *refs[17 + len(after) :])

    return pl.pallas_call(
        body,
        grid=(steps + more,),
        out_shape=(
            jax.ShapeDtypeStruct((half, width), BF16),
            jax.ShapeDtypeStruct((half, width), BF16),
            jax.ShapeDtypeStruct((3, units, 2 * half), BF16),
            jax.ShapeDtypeStruct((2 * half, units), BF16),
        ),
        in_specs=[vmem] * 13
        + [
            pl.BlockSpec((width, each), lambda i: (0, first(i))),
            pl.BlockSpec((width, each), lambda i: (0, steps + first(i))),
            pl.BlockSpec((width, each), lambda i: (0, 2 * steps + first(i))),
            pl.BlockSpec((rows, 2 * units), lambda i: (second(i), 0)),
        ]
        + [pl.BlockSpec(memory_space=pl.ANY)] * len(after),
        out_specs=(
            pl.BlockSpec((half, rows), lambda i: (0, second(i))),
            pl.BlockSpec((half, rows), lambda i: (0, second(i))),
            pl.BlockSpec((3, each, 2 * half), lambda i: (0, first(i), 0)),
            pl.BlockSpec((2 * half, each), lambda i: (0, first(i))),
        ),
        scratch_shapes=[pltpu.VMEM((2 * half, width), BF16)] * 2
        + [pltpu.VMEM((2 * half, units), BF16)] * 2,
        compiler_params=pltpu.CompilerParams(vmem_limit_bytes=VMEM_LIMIT),
        cost_estimate=pl.CostEstimate(
            flops=20 * half * width * units, bytes_accessed=1, transcendentals=0
        ),
        name="mlp",
    )(*b_parts, *dy_parts, *[mlp_w] * 4, *after)


def down_kernel(hidden_ref, w_ref, keep_ref, send_ref):
    half = keep_ref.shape[0]
    for c in range(0, keep_ref.shape[1], 512):
        part = dot_nt(hidden_ref[...], w_ref[c : c + 512, :]).astype(BF16)
        keep_ref[:, c : c + 512] = part[:half]
        send_ref[:, c : c + 512] = part[half:]


def down(hidden, mlp_w, after):
    (rows, units), width = hidden.shape, mlp_w.shape[0]
    spec = pl.BlockSpec((width, units), lambda i: (0, 2))
    outs = [((rows // 2, width), BF16)] * 2
    flops = 2 * rows * width * units
    return call(down_kernel, "down", outs, [], [hidden, mlp_w], after, flops=flops, specs={1: spec})


def spread_rows(to_ref, parts):
    own, near, *other = parts
    half = own.shape[0] // 2
    other = other[0] if other else near.at[half:]
    put_rows(to_ref, [own.at[:half], near.at[:half], own.at[half:], other])


def put_blocks(out_ref, row, column, product):
    for r in range(0, product.shape[1], HEAD):
        for c in range(0, product.shape[0], HEAD):
            out_ref[row + r // HEAD, column + c // HEAD] = product[c : c + HEAD, r : r + HEAD]


def mlp_grads_kernel(*refs, units):
    b_parts, dy_parts = refs[:10], refs[10:13]
    left_ref, out_ref, b_ref, dy_ref = refs[13:]
    step = pl.program_id(0)
    later = 2 * units // left_ref.shape[0]

    @pl.when(step == 0)
    def _():
        put_rows(b_ref, b_parts)
        spread_rows(dy_ref, dy_parts)

    def work(right_ref):
        for r in range(0, right_ref.shape[1], 512):
            product = dot(left_ref[...], right_ref[:, r : r + 512]).astype(BF16)
            put_blocks(out_ref, r // HEAD, 0, product)

    pl.when(step < later)(lambda: work(b_ref))
    pl.when(step >= later)(lambda: work(dy_ref))


def mlp_grads(b_parts, dy_parts, turned):
    rows, tokens = turned.shape
    width, step = b_parts[0].shape[1], 512
    vmem = pl.BlockSpec(memory_space=pltpu.VMEM)
    return pl.pallas_call(
        functools.partial(mlp_grads_kernel, units=rows // 3),
        grid=(rows // step,),
        out_shape=jax.ShapeDtypeStruct((width // HEAD, rows // HEAD, HEAD, HEAD), BF16),
        in_specs=[vmem] * 13 + [pl.BlockSpec((step, tokens), lambda i: (i, 0))],
        out_specs=pl.BlockSpec(
            (width // HEAD, step // HEAD, HEAD, HEAD), lambda i: (0, i, 0, 0)
        ),
        scratch_shapes=[pltpu.VMEM((tokens, width), BF16)] * 2,
        compiler_params=pltpu.CompilerParams(vmem_limit_bytes=VMEM_LIMIT),
        cost_estimate=pl.CostEstimate(
            flops=2 * rows * tokens * width, bytes_accessed=1, transcendentals=0
        ),
        name="mlp_grads",
    )(*b_parts, *dy_parts, turned)


def outward_kernel(*refs):
    parts, (w_ref, do_ref, m_ref) = refs[:10], refs[10:]
    put_rows(m_ref, parts)
    part = dot(m_ref[...], w_ref[...]).astype(BF16)
    half = part.shape[0] // 2
    for head in range(2):
        for ds in range(2):
            do_ref[head * 2 + ds] = part[
                ds * half : (ds + 1) * half, head * HEAD : (head + 1) * HEAD
            ]


def outward(m_parts, attn_w):
    width = attn_w.shape[0]
    half = sum(v.shape[0] for v in m_parts) // 2
    return call(
        outward_kernel,
        "outward",
        [((4, half, HEAD), BF16)],
        [],
        [*m_parts, attn_w],
        scratch=[pltpu.VMEM((2 * half, width), BF16)],
        flops=8 * half * width * HEAD,
    )[0]


def back_kernel(*refs):
    parts, m_parts, (dqkv_ref, cos_ref, sin_ref, o_ref, w_ref) = refs[:3], refs[3:13], refs[13:18]
    keep_ref, send_ref, out_ref, back_ref, a_ref = refs[18:]
    spread_rows(a_ref, parts)
    half = dqkv_ref.shape[2]
    cosine, sine = cos_ref[...], sin_ref[...]
    for part in range(3):
        for head in range(2):
            for ds in range(2):
                rows = slice(ds * half, (ds + 1) * half)
                e = dqkv_ref[head * 2 + ds, part].astype(F32)
                if part < 2:
                    e = e * cosine[rows] - pltpu.roll(e, HEAD // 2, 1) * sine[rows]
                column = (part * 2 + head) * HEAD
                back_ref[rows, column : column + HEAD] = e.astype(BF16)
    for c in range(0, keep_ref.shape[1], 512):
        part = dot_nt(back_ref[...], w_ref[c : c + 512, :]).astype(BF16)
        keep_ref[:, c : c + 512] = part[:half]
        send_ref[:, c : c + 512] = part[half:]
    for c in range(0, back_ref.shape[1], 2 * HEAD):
        left = jnp.transpose(back_ref[:, c : c + 2 * HEAD])
        for r in range(0, a_ref.shape[1], 512):
            product = dot(left, a_ref[:, r : r + 512]).astype(BF16)
            put_blocks(out_ref, r // HEAD, c // HEAD, product)
    put_rows(a_ref, m_parts)
    left = jnp.concatenate([jnp.transpose(o_ref[k]) for k in range(2)], axis=0)
    for r in range(0, a_ref.shape[1], 512):
        put_blocks(out_ref, r // HEAD, 6, dot(left, a_ref[:, r : r + 512]).astype(BF16))


def backward(a_parts, m_parts, dqkv, cosine, sine, o_heads, attn_w, after):
    half, width = dqkv.shape[2], attn_w.shape[0]
    return call(
        back_kernel,
        "backward",
        [((half, width), BF16)] * 2 + [((width // HEAD, 8, HEAD, HEAD), BF16)],
        [],
        [*a_parts, *m_parts, dqkv, cosine, sine, o_heads, attn_w],
        after,
        scratch=[
            pltpu.VMEM((2 * half, 6 * HEAD), BF16),
            pltpu.VMEM((2 * half, width), BF16),
        ],
        flops=48 * half * width * HEAD,
    )


def total_kernel(at, terms_ref, keep_ref, send_ref):
    rows = keep_ref.shape[1]
    for c in range(keep_ref.shape[0]):
        total = terms_ref[0, c].astype(F32)
        for p in range(1, terms_ref.shape[0]):
            total = total + terms_ref[p, c].astype(F32)
        total = jnp.transpose(total)
        first, second = total[:rows], total[rows:]
        keep_ref[c] = jnp.where(at[0] == 0, first, second).astype(BF16)
        send_ref[c] = jnp.where(at[0] == 0, second, first).astype(BF16)


def total(zl, terms, after=()):
    outs = [((terms.shape[1], HEAD // 2, HEAD), BF16)] * 2
    return call(total_kernel, "total", outs, [(zl,)], [terms], after)


def place_kernel(at, keep_ref, got_ref, *outs):
    block = 0
    for out_ref in outs:
        half = out_ref.shape[1] // 2
        for c in range(0, half, HEAD):
            keep, got = keep_ref[block].astype(F32), got_ref[block].astype(F32)
            out_ref[:, c : c + HEAD] = jnp.where(at[0] == 0, keep, got)
            out_ref[:, half + c : half + c + HEAD] = jnp.where(at[0] == 0, got, keep)
            block += 1


def place(zl, sums, widths, after=()):
    keep, send = total(zl, sums, after)
    outs = [((HEAD // 2, 2 * w), F32) for w in widths]
    return call(place_kernel, "place", outs, [(zl,)], [keep, flip(send, zl=1)])


def finish_kernel(at, own_ref, far_ref, pair_ref, out_ref):
    tile = own_ref.shape[0]
    co, zh = at[0], at[1]
    lane = lax.broadcasted_iota(jnp.int32, (tile, HEAD), 1)
    for k in range(4):
        ref, start = ((own_ref, 0), (far_ref, 0), (pair_ref, 0), (pair_ref, tile))[k]
        at_row = ((k // 2) ^ co) * 2 + ((k % 2) ^ zh)
        rows = pl.ds(pl.multiple_of(at_row * tile, tile), tile)
        for y in range(NY):
            for half in range(NX // 2):
                pair = [
                    ref[start : start + tile, c : c + HEAD].astype(F32)
                    for c in ((y * NX + 2 * half) * HEAD, (y * NX + 2 * half + 1) * HEAD)
                ]
                turned = [pltpu.roll(v, HEAD // 2, 1) for v in pair]
                low = jnp.where(lane < HEAD // 2, pair[0], turned[1])
                high = jnp.where(lane < HEAD // 2, turned[0], pair[1])
                for zl, value in enumerate((low, high)):
                    column = (y * NZL + zl) * NX * HEAD // 2 + half * HEAD
                    out_ref[rows, column : column + HEAD] = value.astype(out_ref.dtype)


def finish(co, zh, own, dtype):
    far = flip(own, zh=1)
    pair = flip(jnp.concatenate([own, far], axis=0), co=1)
    vmem = pl.BlockSpec(memory_space=pltpu.VMEM)
    return pl.pallas_call(
        finish_kernel,
        out_shape=jax.ShapeDtypeStruct((4 * own.shape[0], own.shape[1]), dtype),
        in_specs=[pl.BlockSpec(memory_space=pltpu.SMEM)] + [vmem] * 3,
        out_specs=vmem,
        compiler_params=pltpu.CompilerParams(vmem_limit_bytes=VMEM_LIMIT),
        cost_estimate=pl.CostEstimate(flops=1, bytes_accessed=1, transcendentals=0),
        name="finish",
    )(jnp.stack([co, zh]).astype(jnp.int32), own, far, pair)


def local(
    tokens_in,
    w_query,
    w_key,
    w_value,
    w_output,
    w_gate,
    w_up,
    w_down,
    grad_out,
    block_ids,
    tile_order,
):
    own, width = tokens_in.shape
    seqs, length = block_ids.shape
    tile = length // tile_order.shape[1]
    wide = w_query.shape[1] // 2
    units = w_gate.shape[1] // 2
    piece = w_query.shape[0]
    ctx, tp = lax.axis_index("ctx"), lax.axis_index("tp")
    y, zl, x = ctx // (NZL * NX), (ctx // NX) % NZL, ctx % NX
    zh, co = tp // 2, tp % 2

    def pair_rows(arrays):
        def cut(array, which):
            half = array.shape[1] // 2
            return lax.dynamic_slice_in_dim(array, which * half, half, 1)

        kept = jnp.concatenate([cut(array, zl) for array in arrays], axis=1)
        sent = jnp.concatenate([cut(array, 1 - zl) for array in arrays], axis=1)
        return turn(jnp.stack([kept, flip(sent, zl=1)]), 0, zl).reshape(2 * piece, -1)

    pair = pair_rows((w_query, w_key, w_value))
    copies = plane_copies(pair)
    attn_w = plane_gather(copies)
    first_own, grads, x_own = enter(co, zh, tokens_in, grad_out, [copies])
    near = flip(first_own[: own // 2], zl=1)
    first_low = [first_own, near, flip(near, co=1)]
    started = (near[0, 0] * 0).astype(jnp.int32)
    pair = pair_rows([hold(w, near) for w in (w_gate, w_up, w_down, w_output)])

    tiles = (tile_order + started).reshape(seqs, NY, NZL, NX, 2)
    tiles = turn(turn(turn(tiles, 0, co), 2, zl), 4, zh)
    row_tiles = lax.dynamic_index_in_dim(tiles, y, 1, keepdims=False)
    own_tiles = lax.dynamic_index_in_dim(row_tiles, x, 2, keepdims=False).reshape(-1)
    positions = (own_tiles[:, None] * tile + jnp.arange(tile, dtype=jnp.int32)).reshape(-1)
    inverse = 10000.0 ** (-jnp.arange(0, HEAD, 2, dtype=F32) / HEAD)
    angles = positions.astype(F32)[:, None] * inverse[None, :]
    cosine = jnp.concatenate([jnp.cos(angles)] * 2, axis=-1)
    sine = jnp.concatenate([-jnp.sin(angles), jnp.sin(angles)], axis=-1)
    ds_own = x % 2
    unit_tiles = lax.dynamic_index_in_dim(tiles, ds_own, 0, keepdims=False)
    turns = (y + jnp.arange(NY, dtype=jnp.int32)) % NY
    key_tiles = jnp.swapaxes(jnp.take(unit_tiles, turns, axis=0), 1, 2).reshape(-1)
    query_tiles = lax.dynamic_index_in_dim(unit_tiles, y, 0, keepdims=False)
    query_tiles = jnp.swapaxes(query_tiles, 0, 1).reshape(-1)
    tile_count, query_count = key_tiles.shape[0], query_tiles.shape[0]
    rank = jnp.sum(query_tiles[None, :] < query_tiles[:, None], axis=1)
    places = jnp.arange(query_count, dtype=jnp.int32)
    order = jnp.sum(
        jnp.where(rank[None, :] == places[:, None], places[None, :], 0), axis=1
    ).astype(jnp.int32)
    sorted_tiles = jnp.sum(
        jnp.where(rank[None, :] == places[:, None], query_tiles[None, :], 0), axis=1
    )
    key_blocks = lax.dynamic_index_in_dim(block_ids + started, ds_own ^ co, 0, keepdims=False)
    query_blocks = jnp.take(key_blocks.reshape(tile_count, tile), sorted_tiles, axis=0).reshape(-1)
    by_block = query_blocks.reshape(-1, QB)
    sure = jnp.sum(key_blocks[None, :] <= by_block[:, :1], axis=1) // KC
    most = (jnp.sum(key_blocks[None, :] <= by_block[:, -1:], axis=1) + KC - 1) // KC
    scalars = jnp.concatenate([key_tiles, order, sure, most]).astype(jnp.int32)
    query_rows = jnp.broadcast_to(by_block[:, None, :], (by_block.shape[0], 8, QB))

    query_column, key_column = query_blocks[:, None], key_blocks[:, None]
    tables = [scalars, query_column]
    qkv_send = project(first_low, attn_w, cosine, sine, tables)
    half = own

    def across(values):
        return lax.all_to_all(values, "ctx", 0, 0, tiled=True, axis_index_groups=X_GROUPS)

    line = across(qkv_send)
    q, kv_line = line[:, 0].reshape(query_count, tile, HEAD), line[:, 1:]
    near = flip(hold(grads[: own // 2], qkv_send), zl=1)
    kv = ring_gather(kv_line, (), dy=1)
    mlp_w = lax.all_gather(
        hold(pair[:, : 3 * units], kv_line), "ctx", axis=0, tiled=True, axis_index_groups=XY_GROUPS
    )
    w_out = plane_gather(plane_copies(hold(pair[:, 3 * units :], line)))
    o, o_full, lse = attend(
        scalars, q, kv, query_column, key_blocks[None, :], [near]
    )
    grad_all = [grads, near, flip(hold(near, o), co=1)]
    o_heads = across(hold(o.reshape(NX, half, HEAD), w_out)).reshape(2, 2 * half, HEAD)
    attn_sum = column_sum(*output(o_heads, w_out))

    x_own = x_own.astype(F32)
    dy_own = grads[:tile].astype(F32)
    middle = x_own + attn_sum
    normed_two, inverse_two = norm(middle)
    second_low = column_gather(normed_two.astype(BF16))
    keep, send, turned, hidden = mlp(second_low, grad_all, mlp_w, [key_column, query_rows])
    terms = mlp_grads(second_low, grad_all, turned.reshape(3 * units, -1))
    sums = lax.psum_scatter(
        terms, "ctx", scatter_dimension=0, tiled=True, axis_index_groups=XY_GROUPS
    )
    back_two = column_sum(keep, send, terms)
    grad_middle = dy_own + norm_back(back_two, normed_two, inverse_two)
    middle_low = column_gather(grad_middle.astype(BF16))

    do_send = outward(middle_low, w_out)
    do = across(do_send).reshape(query_count, tile, HEAD)
    out_keep, out_send = down(hidden, mlp_w, [do_send])
    dq, dkv, *others = attend_back(
        scalars,
        q,
        kv,
        do,
        o_full,
        lse,
        query_rows,
        key_column,
        [out_keep],
    )
    pairs = [(dkv[:2], dkv[2:])] + [tuple(others[2 * k : 2 * k + 2]) for k in range(3)]
    dkv = jnp.concatenate(ring_sum(pairs, dy=1), axis=0).astype(BF16)
    dqkv = across(jnp.concatenate([dq.reshape(NX, 1, half, HEAD), dkv], axis=1))
    keep, send, terms = backward(
        first_low, middle_low, dqkv, cosine, sine, o_heads, attn_w, []
    )
    out_low = (middle + column_sum(out_keep, hold(out_send, send))).astype(BF16)
    terms = lax.all_to_all(terms, "ctx", 0, 0, tiled=True, axis_index_groups=XY_GROUPS)
    back_one = column_sum(keep, send)
    normed_own, inverse_own = norm(x_own)
    grad_own = grad_middle + norm_back(back_one, normed_own, inverse_own)
    grad_in = finish(co, zh, grad_own.astype(BF16), F32)
    tokens_out = finish(co, zh, out_low, BF16)
    mlp_out = place(zl, sums, (units,) * 3, [send])
    return (
        tokens_out,
        grad_in,
        *place(zl, terms, (wide,) * 4, [grad_in, tokens_out, mlp_out[0]]),
        *mlp_out,
    )


def solution(mesh):
    row, both = P("ctx", None), P("ctx", "tp")
    return jax.shard_map(
        local,
        mesh=mesh,
        in_specs=(row,) + (both,) * 7 + (row, P(), P()),
        out_specs=(row, row) + (both,) * 7,
        check_vma=False,
    )
```

```python
import functools

import jax
import jax.numpy as jnp
from jax import lax
from jax.experimental import pallas as pl
from jax.experimental.pallas import tpu as pltpu
from jax.sharding import PartitionSpec as P

HEAD = 128
NY, NZL, NX = 4, 2, 4
BOTH = ("ctx", "tp")
QB = 256
KC = 1024
LOG2E = 1.4426950408889634
VMEM_LIMIT = 56 * 1024 * 1024
F32, BF16 = jnp.float32, jnp.bfloat16


def ctx_index(y, zl, x):
    return (y * NZL + zl) * NX + x


XY_GROUPS = [
    [ctx_index(y, zl, x) for y in range(NY) for x in range(NX)] for zl in range(NZL)
]
X_GROUPS = [
    [ctx_index(y, zl, x) for x in range(NX)] for y in range(NY) for zl in range(NZL)
]


def flip(values, zl=0, zh=0, co=0):
    pairs = []
    for y in range(NY):
        for a in range(NZL):
            for x in range(NX):
                for t in range(4):
                    here = ctx_index(y, a, x) * 4 + t
                    there = ctx_index(y, a ^ zl, x) * 4 + (t ^ (2 * zh + co))
                    pairs.append((here, there))
    return lax.ppermute(values, BOTH, pairs)


def ring(values, dx=0, dy=0):
    pairs = [
        (ctx_index(y, a, x), ctx_index((y + dy) % NY, a, (x + dx) % NX))
        for y in range(NY)
        for a in range(NZL)
        for x in range(NX)
    ]
    return lax.ppermute(values, "ctx", pairs)


def turn(values, axis, bit):
    return jnp.where(bit == 1, jnp.flip(values, axis), values)


def norm(values):
    average = jnp.mean(values, axis=-1, keepdims=True)
    centred = values - average
    inverse = lax.rsqrt(jnp.mean(centred * centred, axis=-1, keepdims=True) + 1e-05)
    return centred * inverse, inverse


def norm_back(grad, normed, inverse):
    first = jnp.mean(grad, axis=-1, keepdims=True)
    second = jnp.mean(grad * normed, axis=-1, keepdims=True)
    return inverse * (grad - first - normed * second)


def column_sum(keep, send, token=None):
    rows = keep.shape[0] // 4
    cut = rows // 2
    got = flip(send, co=1)
    half = keep.astype(F32) + got.astype(F32)
    if token is not None:
        half = hold(half, token)
    own, far, near, both = (half[k * rows : (k + 1) * rows] for k in range(4))
    for_both = flip(far[:cut].astype(BF16), zl=1)
    for_near = flip(far[cut:].astype(BF16), zl=1, zh=1)
    near = jnp.concatenate([near[:cut], near[cut:] + for_near.astype(F32)], axis=0).astype(BF16)
    both = jnp.concatenate([both[:cut] + for_both.astype(F32), both[cut:]], axis=0).astype(BF16)
    from_near, from_both = flip(near, zl=1), flip(both, zl=1, zh=1)
    return own + from_near.astype(F32) + from_both.astype(F32)


def column_gather(rows):
    cut = rows.shape[0] // 2
    near, both = flip(rows, zl=1), flip(rows, zl=1, zh=1)
    far_low, far_high = flip(both[:cut], zl=1), flip(near[cut:], zl=1, zh=1)
    half = [rows, far_low, far_high, near, both]
    return half + [flip(piece, co=1) for piece in half]


def ring_sum(parts, **step):
    forth, back = step, {k: -v for k, v in step.items()}
    ahead, behind = ring(parts[2][0], **forth), ring(parts[2][1], **back)
    from_back, from_forth = ring(parts[1][1], **forth), ring(parts[3][0], **back)
    low = parts[1][0].astype(F32) + ahead.astype(F32)
    high = parts[3][1].astype(F32) + behind.astype(F32)
    low, high = ring(low.astype(BF16), **forth), ring(high.astype(BF16), **back)
    return (
        parts[0][0].astype(F32) + low.astype(F32) + from_forth.astype(F32),
        parts[0][1].astype(F32) + from_back.astype(F32) + high.astype(F32),
    )


def ring_gather(rows, tokens, **step):
    forth, back = step, {k: -v for k, v in step.items()}
    cut = rows.shape[0] // 2
    before, after = ring(rows, **forth), ring(rows, **back)
    low, high = before[:cut], after[cut:]
    for one in tokens:
        low, high = hold(low, one), hold(high, one)
    low, high = ring(low, **forth), ring(high, **back)
    return rows, after, low, high, before


def plane_copies(rows):
    return jnp.broadcast_to(rows[None], (NY * NX,) + rows.shape)


def plane_gather(copies):
    every = lax.all_to_all(copies, "ctx", 0, 0, tiled=True, axis_index_groups=XY_GROUPS)
    return every.reshape(-1, copies.shape[2])


def dot(left, right):
    return jnp.dot(left, right, preferred_element_type=F32)


def dot_nt(left, right):
    return lax.dot_general(left, right, (((1,), (1,)), ((), ())), preferred_element_type=F32)


def dot_tn(left, right):
    return lax.dot_general(left, right, (((0,), (0,)), ((), ())), preferred_element_type=F32)


def call(kernel, name, outs, scalars, arrays, after=(), scratch=(), flops=1, specs=None):
    head, tail = len(scalars) + len(arrays), len(after)
    vmem = pl.BlockSpec(memory_space=pltpu.VMEM)
    specs = specs or {}
    grid = {"grid": (1,)} if specs else {}

    def body(*refs):
        kernel(*refs[:head], *refs[head + tail :])

    return pl.pallas_call(
        body,
        **grid,
        out_shape=tuple(jax.ShapeDtypeStruct(shape, dtype) for shape, dtype in outs),
        in_specs=[pl.BlockSpec(memory_space=pltpu.SMEM)] * len(scalars)
        + [specs.get(k, vmem) for k in range(len(arrays))]
        + [pl.BlockSpec(memory_space=pl.ANY)] * tail,
        out_specs=(vmem,) * len(outs),
        scratch_shapes=list(scratch),
        compiler_params=pltpu.CompilerParams(vmem_limit_bytes=VMEM_LIMIT),
        cost_estimate=pl.CostEstimate(flops=flops, bytes_accessed=1, transcendentals=0),
        name=name,
    )(*[jnp.stack(s).astype(jnp.int32) for s in scalars], *arrays, *after)


def hold(values, token):
    return values + (token[(0,) * token.ndim] * 0).astype(values.dtype)


def put_rows(to_ref, refs):
    row = 0
    for ref in refs:
        to_ref[row : row + ref.shape[0], :] = ref[...]
        row += ref.shape[0]


def enter_kernel(at, x_ref, dy_ref, a_ref, dy_out, own_ref):
    tile = own_ref.shape[0]
    lane = lax.broadcasted_iota(jnp.int32, (tile, HEAD), 1)
    for k in range(4):
        row = ((k // 2) ^ at[0]) * 2 + ((k % 2) ^ at[1])
        rows = pl.ds(pl.multiple_of(row * tile, tile), tile)
        x = x_ref[rows, :].astype(F32)
        values = [(norm(x)[0], a_ref), (dy_ref[rows, :].astype(F32), dy_out)]
        if k == 0:
            values.append((x, own_ref))
        for value, to_ref in values:
            for y in range(NY):
                for half in range(NX // 2):
                    pair = [
                        value[:, c : c + HEAD]
                        for c in [(y * NZL + z) * NX * HEAD // 2 + half * HEAD for z in range(2)]
                    ]
                    turned = [pltpu.roll(v, HEAD // 2, 1) for v in pair]
                    low = jnp.where(lane < HEAD // 2, pair[0], turned[1])
                    high = jnp.where(lane < HEAD // 2, turned[0], pair[1])
                    for n, v in enumerate((low, high)):
                        c = (y * NX + 2 * half + n) * HEAD
                        to_ref[k * tile : (k + 1) * tile, c : c + HEAD] = v.astype(BF16)


def enter(co, zh, x, dy, after):
    rows, width = x.shape
    outs = [((rows, width), BF16)] * 2 + [((rows // 4, width), BF16)]
    return call(enter_kernel, "enter", outs, [(co, zh)], [x, dy], after)


def each_piece(pairs):
    own, after, low, high, before = pairs
    for dy in range(NY):
        for x in range(NX):
            ref = (own, after, (low, high)[x // 2], before)[dy]
            for k in range(4):
                yield (dy * NX + x) * 4 + k, x % 2 if dy == 2 else x, k, ref


def sort_pairs(scalars, pairs, keys, values, tile):
    for slot, x, k, ref in each_piece(pairs):
        rows = pl.ds(pl.multiple_of(scalars[slot] * tile, tile), tile)
        keys[rows, :] = ref[x, 0, k * tile : (k + 1) * tile]
        values[rows, :] = ref[x, 1, k * tile : (k + 1) * tile]


def attend_kernel(
    scalars, q_ref, kv0, kv1, kv2, kv3, kv4, qblk, kblk, o_ref, full_ref, lse_ref, keys, values, queries, *, tile
):
    tiles = keys.shape[0] // tile
    per = QB // tile
    blocks = q_ref.shape[0] // per
    factor = HEAD**-0.5 * LOG2E
    sort_pairs(scalars, (kv0, kv1, kv2, kv3, kv4), keys, values, tile)

    def block(i, carry):
        for k in range(per):
            queries[k * tile : (k + 1) * tile, :] = q_ref[scalars[tiles + i * per + k]]
        q_own = queries[...]
        rows = pl.ds(pl.multiple_of(i * QB, QB), QB)

        def chunk(c, state, masked):
            top, total, acc = state
            where = pl.ds(pl.multiple_of(c * KC, KC), KC)
            s = dot_nt(q_own, keys[where, :])
            if masked:
                s = jnp.where(qblk[rows, :] >= kblk[:, where], s, -1e30)
            new = jnp.maximum(top, jnp.max(s, axis=-1, keepdims=True))
            p = jnp.exp2((s - new) * factor)
            shrink = jnp.exp2((top - new) * factor)
            total = total * shrink + jnp.sum(p, axis=-1, keepdims=True)
            acc = acc * shrink + dot(p.astype(BF16), values[where, :])
            return new, total, acc

        base = tiles + blocks * per
        state = (
            jnp.full((QB, 1), -1e30, F32),
            jnp.zeros((QB, 1), F32),
            jnp.zeros((QB, HEAD), F32),
        )
        first, last = scalars[base + i], scalars[base + blocks + i]
        state = lax.fori_loop(0, first, functools.partial(chunk, masked=False), state)
        top, total, acc = lax.fori_loop(first, last, functools.partial(chunk, masked=True), state)
        out = acc / total
        full_ref[rows, :] = out
        low = out.astype(BF16)
        for k in range(per):
            o_ref[scalars[tiles + i * per + k]] = low[k * tile : (k + 1) * tile]
        lse = top * factor + jnp.log2(total)
        lse_ref[i] = jnp.transpose(jnp.broadcast_to(lse, (QB, HEAD)))[:8]
        return carry

    lax.fori_loop(0, blocks, block, 0)


def attend(scalars, q, kv, qblk, kblk, after):
    tile = q.shape[1]
    count = q.shape[0] * tile
    length = kblk.shape[1]
    vmem = pl.BlockSpec(memory_space=pltpu.VMEM)
    kernel = functools.partial(attend_kernel, tile=tile)

    def body(*refs):
        kernel(*refs[:9], *refs[9 + len(after) :])

    return pl.pallas_call(
        body,
        out_shape=(
            jax.ShapeDtypeStruct(q.shape, BF16),
            jax.ShapeDtypeStruct((count, HEAD), F32),
            jax.ShapeDtypeStruct((count // QB, 8, QB), F32),
        ),
        in_specs=[pl.BlockSpec(memory_space=pltpu.SMEM)]
        + [vmem] * 8
        + [pl.BlockSpec(memory_space=pl.ANY)] * len(after),
        out_specs=(vmem,) * 3,
        scratch_shapes=[
            pltpu.VMEM((length, HEAD), BF16),
            pltpu.VMEM((length, HEAD), BF16),
            pltpu.VMEM((QB, HEAD), BF16),
        ],
        compiler_params=pltpu.CompilerParams(vmem_limit_bytes=VMEM_LIMIT),
        cost_estimate=pl.CostEstimate(
            flops=32 * count * length * HEAD, bytes_accessed=1 << 22, transcendentals=count * length
        ),
        name="attend",
    )(scalars, q, *kv, qblk, kblk, *after)


def attend_back_kernel(
    scalars,
    q_ref,
    kv0,
    kv1,
    kv2,
    kv3,
    kv4,
    do_ref,
    full_ref,
    lse_ref,
    qblk,
    kblk,
    dq_ref,
    own_ref,
    after_low,
    after_high,
    far_low,
    far_high,
    before_low,
    before_high,
    keys,
    values,
    queries,
    grads,
    dk,
    dv,
    *,
    tile,
):
    tiles = keys.shape[0] // tile
    per = QB // tile
    blocks = q_ref.shape[0] // per
    scale = HEAD**-0.5
    factor = scale * LOG2E
    sort_pairs(scalars, (kv0, kv1, kv2, kv3, kv4), keys, values, tile)
    dk[...] = jnp.zeros_like(dk)
    dv[...] = jnp.zeros_like(dv)

    def block(i, carry):
        for k in range(per):
            slot = scalars[tiles + i * per + k]
            queries[k * tile : (k + 1) * tile, :] = q_ref[slot]
            grads[k * tile : (k + 1) * tile, :] = do_ref[slot]
        q_own = queries[...]
        do_own = grads[...]
        rows = pl.ds(pl.multiple_of(i * QB, QB), QB)
        product = do_own.astype(F32) * full_ref[rows, :]
        delta = jnp.sum(jnp.transpose(product), axis=0, keepdims=True)
        lse = lse_ref[i][:1]
        q_blocks = qblk[i][:1]

        def chunk(c, acc, masked):
            where = pl.ds(pl.multiple_of(c * KC, KC), KC)
            k_own = keys[where, :]
            s = dot_nt(k_own, q_own)
            if masked:
                s = jnp.where(kblk[where, :] <= q_blocks, s, -1e30)
            p = jnp.exp2(s * factor - lse)
            dp = dot_nt(values[where, :], do_own)
            ds = (p * (dp - delta)).astype(BF16)
            dv[where, :] += dot(p.astype(BF16), do_own)
            dk[where, :] += dot(ds, q_own)
            return acc + dot_tn(ds, k_own)

        base = tiles + blocks * per
        first, last = scalars[base + i], scalars[base + blocks + i]
        acc = jnp.zeros((QB, HEAD), F32)
        acc = lax.fori_loop(0, first, functools.partial(chunk, masked=False), acc)
        acc = lax.fori_loop(first, last, functools.partial(chunk, masked=True), acc)
        low = (acc * scale).astype(BF16)
        for k in range(per):
            dq_ref[scalars[tiles + i * per + k]] = low[k * tile : (k + 1) * tile]
        return carry

    lax.fori_loop(0, blocks, block, 0)

    outs = ((own_ref, own_ref), (after_low, after_high), (far_low, far_high), (before_low, before_high))
    for slot in range(tiles):
        dy, x, k = slot // 16, slot // 4 % 4, slot % 4
        rows = pl.ds(pl.multiple_of(scalars[slot] * tile, tile), tile)
        ref, x = outs[dy][x // 2], x if dy == 0 else x % 2
        here = slice(k * tile, (k + 1) * tile)
        ref[x, 0, here] = (dk[rows, :] * scale).astype(BF16)
        ref[x, 1, here] = dv[rows, :].astype(BF16)


def attend_back(scalars, q, kv, do, full, lse, qblk, kblk, after):
    tile = q.shape[1]
    count = q.shape[0] * tile
    length = kblk.shape[0]
    vmem = pl.BlockSpec(memory_space=pltpu.VMEM)
    kernel = functools.partial(attend_back_kernel, tile=tile)

    def body(*refs):
        kernel(*refs[:12], *refs[12 + len(after) :])

    return pl.pallas_call(
        body,
        out_shape=(
            jax.ShapeDtypeStruct(q.shape, BF16),
            jax.ShapeDtypeStruct(kv[0].shape, BF16),
        )
        + (jax.ShapeDtypeStruct(kv[2].shape, BF16),) * 6,
        in_specs=[pl.BlockSpec(memory_space=pltpu.SMEM)]
        + [vmem] * 11
        + [pl.BlockSpec(memory_space=pl.ANY)] * len(after),
        out_specs=(vmem,) * 8,
        scratch_shapes=[
            pltpu.VMEM((length, HEAD), BF16),
            pltpu.VMEM((length, HEAD), BF16),
            pltpu.VMEM((QB, HEAD), BF16),
            pltpu.VMEM((QB, HEAD), BF16),
            pltpu.VMEM((length, HEAD), F32),
            pltpu.VMEM((length, HEAD), F32),
        ],
        compiler_params=pltpu.CompilerParams(vmem_limit_bytes=VMEM_LIMIT),
        cost_estimate=pl.CostEstimate(
            flops=40 * count * length * HEAD, bytes_accessed=1 << 23, transcendentals=count * length
        ),
        name="attend_back",
    )(scalars, q, *kv, do, full, lse, qblk, kblk, *after)


def project_kernel(own_ref, near_ref, other_ref, w_ref, cos_ref, sin_ref, qkv_ref, a_ref):
    half = own_ref.shape[0]
    spread_rows(a_ref, (own_ref, near_ref, other_ref))
    cosine, sine = cos_ref[...], sin_ref[...]
    for part in range(3):
        product = dot(a_ref[...], w_ref[:, part * 2 * HEAD : (part + 1) * 2 * HEAD])
        for head in range(2):
            u = product[:, head * HEAD : (head + 1) * HEAD]
            if part < 2:
                u = u * cosine + pltpu.roll(u, HEAD // 2, 1) * sine
            u = u.astype(BF16)
            for ds in range(2):
                rows = u[ds * half : (ds + 1) * half]
                qkv_ref[head * 2 + ds, part] = rows


def project(a, weights, cosine, sine, after):
    half, width = a[0].shape
    return call(
        project_kernel,
        "project",
        [((4, 3, half, HEAD), BF16)],
        [],
        [*a, weights, cosine, sine],
        after,
        scratch=[pltpu.VMEM((2 * half, width), BF16)],
        flops=4 * half * width * 6 * HEAD,
    )[0]


def output_kernel(o_ref, w_ref, keep_ref, send_ref):
    half = keep_ref.shape[0]
    o = jnp.concatenate([o_ref[0], o_ref[1]], axis=1)
    for c in range(0, keep_ref.shape[1], 512):
        part = dot_nt(o, w_ref[c : c + 512, :]).astype(BF16)
        keep_ref[:, c : c + 512] = part[:half]
        send_ref[:, c : c + 512] = part[half:]


def output(o_heads, weights):
    rows, width = o_heads.shape[1], weights.shape[0]
    outs = [((rows // 2, width), BF16)] * 2
    flops = 4 * rows * width * HEAD
    return call(output_kernel, "output", outs, [], [o_heads, weights], flops=flops)


def mlp_kernel(*refs):
    b_parts, dy_parts = refs[:10], refs[10:13]
    gate_ref, up_ref, down_ref, rows_ref, keep_ref, send_ref, turned_ref, hidden_ref = refs[13:21]
    b_ref, dy_ref, dg_ref, du_ref = refs[21:]
    step = pl.program_id(0)
    half, units, each = dy_parts[0].shape[0], dg_ref.shape[1], gate_ref.shape[1]
    steps = units // each

    @pl.when(step == 0)
    def _():
        put_rows(b_ref, b_parts)
        spread_rows(dy_ref, dy_parts)

    @pl.when(step < steps)
    def _():
        here = pl.ds(pl.multiple_of(step * each, each), each)
        gate = dot(b_ref[...], gate_ref[...])
        upper = dot(b_ref[...], up_ref[...])
        grad = dot(dy_ref[...], down_ref[...])
        sigmoid = 1.0 / (1.0 + jnp.exp(-gate))
        swish = gate * sigmoid
        made = (
            (grad * upper * sigmoid * (1.0 + gate * (1.0 - sigmoid))).astype(BF16),
            (grad * swish).astype(BF16),
            (swish * upper).astype(BF16),
        )
        for k, value in enumerate(made):
            turned_ref[k] = jnp.transpose(value)
        dg_ref[:, here] = made[0]
        du_ref[:, here] = made[1]
        hidden_ref[...] = made[2]

    @pl.when(step >= steps)
    def _():
        part = dot_nt(dg_ref[...], rows_ref[:, :units])
        part = (part + dot_nt(du_ref[...], rows_ref[:, units:])).astype(BF16)
        keep_ref[...] = part[:half]
        send_ref[...] = part[half:]


def mlp(b_parts, dy_parts, mlp_w, after):
    half, width = dy_parts[0].shape
    units, each, rows = mlp_w.shape[1] // 3, 512, 512
    steps, more = units // each, width // rows
    vmem = pl.BlockSpec(memory_space=pltpu.VMEM)

    def first(i):
        return jnp.minimum(i, steps - 1)

    def second(i):
        return jnp.maximum(i - steps, 0)

    def body(*refs):
        mlp_kernel(*refs[:17], *refs[17 + len(after) :])

    return pl.pallas_call(
        body,
        grid=(steps + more,),
        out_shape=(
            jax.ShapeDtypeStruct((half, width), BF16),
            jax.ShapeDtypeStruct((half, width), BF16),
            jax.ShapeDtypeStruct((3, units, 2 * half), BF16),
            jax.ShapeDtypeStruct((2 * half, units), BF16),
        ),
        in_specs=[vmem] * 13
        + [
            pl.BlockSpec((width, each), lambda i: (0, first(i))),
            pl.BlockSpec((width, each), lambda i: (0, steps + first(i))),
            pl.BlockSpec((width, each), lambda i: (0, 2 * steps + first(i))),
            pl.BlockSpec((rows, 2 * units), lambda i: (second(i), 0)),
        ]
        + [pl.BlockSpec(memory_space=pl.ANY)] * len(after),
        out_specs=(
            pl.BlockSpec((half, rows), lambda i: (0, second(i))),
            pl.BlockSpec((half, rows), lambda i: (0, second(i))),
            pl.BlockSpec((3, each, 2 * half), lambda i: (0, first(i), 0)),
            pl.BlockSpec((2 * half, each), lambda i: (0, first(i))),
        ),
        scratch_shapes=[pltpu.VMEM((2 * half, width), BF16)] * 2
        + [pltpu.VMEM((2 * half, units), BF16)] * 2,
        compiler_params=pltpu.CompilerParams(vmem_limit_bytes=VMEM_LIMIT),
        cost_estimate=pl.CostEstimate(
            flops=20 * half * width * units, bytes_accessed=1, transcendentals=0
        ),
        name="mlp",
    )(*b_parts, *dy_parts, *[mlp_w] * 4, *after)


def down_kernel(hidden_ref, w_ref, keep_ref, send_ref):
    half = keep_ref.shape[0]
    for c in range(0, keep_ref.shape[1], 512):
        part = dot_nt(hidden_ref[...], w_ref[c : c + 512, :]).astype(BF16)
        keep_ref[:, c : c + 512] = part[:half]
        send_ref[:, c : c + 512] = part[half:]


def down(hidden, mlp_w, after):
    (rows, units), width = hidden.shape, mlp_w.shape[0]
    spec = pl.BlockSpec((width, units), lambda i: (0, 2))
    outs = [((rows // 2, width), BF16)] * 2
    flops = 2 * rows * width * units
    return call(down_kernel, "down", outs, [], [hidden, mlp_w], after, flops=flops, specs={1: spec})


def spread_rows(to_ref, parts):
    own, near, *other = parts
    half = own.shape[0] // 2
    other = other[0] if other else near.at[half:]
    put_rows(to_ref, [own.at[:half], near.at[:half], own.at[half:], other])


def put_blocks(out_ref, row, column, product):
    for r in range(0, product.shape[1], HEAD):
        for c in range(0, product.shape[0], HEAD):
            out_ref[row + r // HEAD, column + c // HEAD] = product[c : c + HEAD, r : r + HEAD]


def mlp_grads_kernel(*refs, units):
    b_parts, dy_parts = refs[:10], refs[10:13]
    left_ref, out_ref, b_ref, dy_ref = refs[13:]
    step = pl.program_id(0)
    later = 2 * units // left_ref.shape[0]

    @pl.when(step == 0)
    def _():
        put_rows(b_ref, b_parts)
        spread_rows(dy_ref, dy_parts)

    def work(right_ref):
        for r in range(0, right_ref.shape[1], 512):
            product = dot(left_ref[...], right_ref[:, r : r + 512]).astype(BF16)
            put_blocks(out_ref, r // HEAD, 0, product)

    pl.when(step < later)(lambda: work(b_ref))
    pl.when(step >= later)(lambda: work(dy_ref))


def mlp_grads(b_parts, dy_parts, turned):
    rows, tokens = turned.shape
    width, step = b_parts[0].shape[1], 512
    vmem = pl.BlockSpec(memory_space=pltpu.VMEM)
    return pl.pallas_call(
        functools.partial(mlp_grads_kernel, units=rows // 3),
        grid=(rows // step,),
        out_shape=jax.ShapeDtypeStruct((width // HEAD, rows // HEAD, HEAD, HEAD), BF16),
        in_specs=[vmem] * 13 + [pl.BlockSpec((step, tokens), lambda i: (i, 0))],
        out_specs=pl.BlockSpec(
            (width // HEAD, step // HEAD, HEAD, HEAD), lambda i: (0, i, 0, 0)
        ),
        scratch_shapes=[pltpu.VMEM((tokens, width), BF16)] * 2,
        compiler_params=pltpu.CompilerParams(vmem_limit_bytes=VMEM_LIMIT),
        cost_estimate=pl.CostEstimate(
            flops=2 * rows * tokens * width, bytes_accessed=1, transcendentals=0
        ),
        name="mlp_grads",
    )(*b_parts, *dy_parts, turned)


def output_grads_kernel(*refs):
    parts, (o_ref, out_ref, m_ref) = refs[:10], refs[10:]
    put_rows(m_ref, parts)
    left = jnp.concatenate([jnp.transpose(o_ref[k]) for k in range(2)], axis=0)
    for r in range(0, m_ref.shape[1], 512):
        put_blocks(out_ref, r // HEAD, 0, dot(left, m_ref[:, r : r + 512]).astype(BF16))


def output_grads(m_parts, o_heads, after):
    width, tokens = m_parts[0].shape[1], o_heads.shape[1]
    return call(
        output_grads_kernel,
        "output_grads",
        [((width // HEAD, 2, HEAD, HEAD), BF16)],
        [],
        [*m_parts, o_heads],
        after,
        scratch=[pltpu.VMEM((tokens, width), BF16)],
    )[0]


def outward_kernel(*refs):
    parts, (w_ref, do_ref, m_ref) = refs[:10], refs[10:]
    put_rows(m_ref, parts)
    part = dot(m_ref[...], w_ref[...]).astype(BF16)
    half = part.shape[0] // 2
    for head in range(2):
        for ds in range(2):
            do_ref[head * 2 + ds] = part[
                ds * half : (ds + 1) * half, head * HEAD : (head + 1) * HEAD
            ]


def outward(m_parts, attn_w):
    width = attn_w.shape[0]
    half = sum(v.shape[0] for v in m_parts) // 2
    return call(
        outward_kernel,
        "outward",
        [((4, half, HEAD), BF16)],
        [],
        [*m_parts, attn_w],
        scratch=[pltpu.VMEM((2 * half, width), BF16)],
        flops=8 * half * width * HEAD,
    )[0]


def back_kernel(*refs):
    parts, (dqkv_ref, cos_ref, sin_ref, w_ref) = refs[:3], refs[3:7]
    keep_ref, send_ref, out_ref, back_ref, a_ref = refs[7:]
    spread_rows(a_ref, parts)
    half = dqkv_ref.shape[2]
    cosine, sine = cos_ref[...], sin_ref[...]
    for part in range(3):
        for head in range(2):
            for ds in range(2):
                rows = slice(ds * half, (ds + 1) * half)
                e = dqkv_ref[head * 2 + ds, part].astype(F32)
                if part < 2:
                    e = e * cosine[rows] - pltpu.roll(e, HEAD // 2, 1) * sine[rows]
                column = (part * 2 + head) * HEAD
                back_ref[rows, column : column + HEAD] = e.astype(BF16)
    for c in range(0, keep_ref.shape[1], 512):
        part = dot_nt(back_ref[...], w_ref[c : c + 512, :]).astype(BF16)
        keep_ref[:, c : c + 512] = part[:half]
        send_ref[:, c : c + 512] = part[half:]
    for c in range(0, back_ref.shape[1], 2 * HEAD):
        left = jnp.transpose(back_ref[:, c : c + 2 * HEAD])
        for r in range(0, a_ref.shape[1], 512):
            product = dot(left, a_ref[:, r : r + 512]).astype(BF16)
            put_blocks(out_ref, r // HEAD, c // HEAD, product)


def backward(a_parts, dqkv, cosine, sine, attn_w, after):
    half, width = dqkv.shape[2], attn_w.shape[0]
    return call(
        back_kernel,
        "backward",
        [((half, width), BF16)] * 2 + [((width // HEAD, 6, HEAD, HEAD), BF16)],
        [],
        [*a_parts, dqkv, cosine, sine, attn_w],
        after,
        scratch=[
            pltpu.VMEM((2 * half, 6 * HEAD), BF16),
            pltpu.VMEM((2 * half, width), BF16),
        ],
        flops=48 * half * width * HEAD,
    )


def total_kernel(at, terms_ref, keep_ref, send_ref):
    rows = keep_ref.shape[1]
    for c in range(keep_ref.shape[0]):
        total = terms_ref[0, c].astype(F32)
        for p in range(1, terms_ref.shape[0]):
            total = total + terms_ref[p, c].astype(F32)
        total = jnp.transpose(total)
        first, second = total[:rows], total[rows:]
        keep_ref[c] = jnp.where(at[0] == 0, first, second).astype(BF16)
        send_ref[c] = jnp.where(at[0] == 0, second, first).astype(BF16)


def total(zl, terms, after=()):
    outs = [((terms.shape[1], HEAD // 2, HEAD), BF16)] * 2
    return call(total_kernel, "total", outs, [(zl,)], [terms], after)


def place_kernel(at, keep_ref, got_ref, *outs):
    block = 0
    for out_ref in outs:
        half = out_ref.shape[1] // 2
        for c in range(0, half, HEAD):
            keep, got = keep_ref[block].astype(F32), got_ref[block].astype(F32)
            out_ref[:, c : c + HEAD] = jnp.where(at[0] == 0, keep, got)
            out_ref[:, half + c : half + c + HEAD] = jnp.where(at[0] == 0, got, keep)
            block += 1


def place(zl, sums, widths, after=()):
    keep, send = total(zl, sums, after)
    outs = [((HEAD // 2, 2 * w), F32) for w in widths]
    return call(place_kernel, "place", outs, [(zl,)], [keep, flip(send, zl=1)])


def finish_kernel(at, own_ref, far_ref, pair_ref, out_ref):
    tile = own_ref.shape[0]
    co, zh = at[0], at[1]
    lane = lax.broadcasted_iota(jnp.int32, (tile, HEAD), 1)
    for k in range(4):
        ref, start = ((own_ref, 0), (far_ref, 0), (pair_ref, 0), (pair_ref, tile))[k]
        at_row = ((k // 2) ^ co) * 2 + ((k % 2) ^ zh)
        rows = pl.ds(pl.multiple_of(at_row * tile, tile), tile)
        for y in range(NY):
            for half in range(NX // 2):
                pair = [
                    ref[start : start + tile, c : c + HEAD].astype(F32)
                    for c in ((y * NX + 2 * half) * HEAD, (y * NX + 2 * half + 1) * HEAD)
                ]
                turned = [pltpu.roll(v, HEAD // 2, 1) for v in pair]
                low = jnp.where(lane < HEAD // 2, pair[0], turned[1])
                high = jnp.where(lane < HEAD // 2, turned[0], pair[1])
                for zl, value in enumerate((low, high)):
                    column = (y * NZL + zl) * NX * HEAD // 2 + half * HEAD
                    out_ref[rows, column : column + HEAD] = value.astype(out_ref.dtype)


def finish(co, zh, own, dtype):
    far = flip(own, zh=1)
    pair = flip(jnp.concatenate([own, far], axis=0), co=1)
    vmem = pl.BlockSpec(memory_space=pltpu.VMEM)
    return pl.pallas_call(
        finish_kernel,
        out_shape=jax.ShapeDtypeStruct((4 * own.shape[0], own.shape[1]), dtype),
        in_specs=[pl.BlockSpec(memory_space=pltpu.SMEM)] + [vmem] * 3,
        out_specs=vmem,
        compiler_params=pltpu.CompilerParams(vmem_limit_bytes=VMEM_LIMIT),
        cost_estimate=pl.CostEstimate(flops=1, bytes_accessed=1, transcendentals=0),
        name="finish",
    )(jnp.stack([co, zh]).astype(jnp.int32), own, far, pair)


def local(
    tokens_in,
    w_query,
    w_key,
    w_value,
    w_output,
    w_gate,
    w_up,
    w_down,
    grad_out,
    block_ids,
    tile_order,
):
    own, width = tokens_in.shape
    seqs, length = block_ids.shape
    tile = length // tile_order.shape[1]
    wide = w_query.shape[1] // 2
    units = w_gate.shape[1] // 2
    piece = w_query.shape[0]
    ctx, tp = lax.axis_index("ctx"), lax.axis_index("tp")
    y, zl, x = ctx // (NZL * NX), (ctx // NX) % NZL, ctx % NX
    zh, co = tp // 2, tp % 2

    def pair_rows(arrays):
        def cut(array, which):
            half = array.shape[1] // 2
            return lax.dynamic_slice_in_dim(array, which * half, half, 1)

        kept = jnp.concatenate([cut(array, zl) for array in arrays], axis=1)
        sent = jnp.concatenate([cut(array, 1 - zl) for array in arrays], axis=1)
        return turn(jnp.stack([kept, flip(sent, zl=1)]), 0, zl).reshape(2 * piece, -1)

    pair = pair_rows((w_query, w_key, w_value))
    copies = plane_copies(pair)
    attn_w = plane_gather(copies)
    first_own, grads, x_own = enter(co, zh, tokens_in, grad_out, [copies])
    near = flip(first_own[: own // 2], zl=1)
    first_low = [first_own, near, flip(near, co=1)]
    started = (near[0, 0] * 0).astype(jnp.int32)
    pair = pair_rows([hold(w, near) for w in (w_gate, w_up, w_down, w_output)])

    tiles = (tile_order + started).reshape(seqs, NY, NZL, NX, 2)
    tiles = turn(turn(turn(tiles, 0, co), 2, zl), 4, zh)
    row_tiles = lax.dynamic_index_in_dim(tiles, y, 1, keepdims=False)
    own_tiles = lax.dynamic_index_in_dim(row_tiles, x, 2, keepdims=False).reshape(-1)
    positions = (own_tiles[:, None] * tile + jnp.arange(tile, dtype=jnp.int32)).reshape(-1)
    inverse = 10000.0 ** (-jnp.arange(0, HEAD, 2, dtype=F32) / HEAD)
    angles = positions.astype(F32)[:, None] * inverse[None, :]
    cosine = jnp.concatenate([jnp.cos(angles)] * 2, axis=-1)
    sine = jnp.concatenate([-jnp.sin(angles), jnp.sin(angles)], axis=-1)
    ds_own = x % 2
    unit_tiles = lax.dynamic_index_in_dim(tiles, ds_own, 0, keepdims=False)
    turns = (y + jnp.arange(NY, dtype=jnp.int32)) % NY
    key_tiles = jnp.swapaxes(jnp.take(unit_tiles, turns, axis=0), 1, 2).reshape(-1)
    query_tiles = lax.dynamic_index_in_dim(unit_tiles, y, 0, keepdims=False)
    query_tiles = jnp.swapaxes(query_tiles, 0, 1).reshape(-1)
    tile_count, query_count = key_tiles.shape[0], query_tiles.shape[0]
    rank = jnp.sum(query_tiles[None, :] < query_tiles[:, None], axis=1)
    places = jnp.arange(query_count, dtype=jnp.int32)
    order = jnp.sum(
        jnp.where(rank[None, :] == places[:, None], places[None, :], 0), axis=1
    ).astype(jnp.int32)
    sorted_tiles = jnp.sum(
        jnp.where(rank[None, :] == places[:, None], query_tiles[None, :], 0), axis=1
    )
    key_blocks = lax.dynamic_index_in_dim(block_ids + started, ds_own ^ co, 0, keepdims=False)
    query_blocks = jnp.take(key_blocks.reshape(tile_count, tile), sorted_tiles, axis=0).reshape(-1)
    by_block = query_blocks.reshape(-1, QB)
    sure = jnp.sum(key_blocks[None, :] <= by_block[:, :1], axis=1) // KC
    most = (jnp.sum(key_blocks[None, :] <= by_block[:, -1:], axis=1) + KC - 1) // KC
    scalars = jnp.concatenate([key_tiles, order, sure, most]).astype(jnp.int32)
    query_rows = jnp.broadcast_to(by_block[:, None, :], (by_block.shape[0], 8, QB))

    query_column, key_column = query_blocks[:, None], key_blocks[:, None]
    tables = [scalars, query_column]
    qkv_send = project(first_low, attn_w, cosine, sine, tables)
    half = own

    def across(values):
        return lax.all_to_all(values, "ctx", 0, 0, tiled=True, axis_index_groups=X_GROUPS)

    line = across(qkv_send)
    q, kv_line = line[:, 0].reshape(query_count, tile, HEAD), line[:, 1:]
    near = flip(hold(grads[: own // 2], qkv_send), zl=1)
    kv = ring_gather(kv_line, (), dy=1)
    mlp_w = lax.all_gather(
        hold(pair[:, : 3 * units], kv_line), "ctx", axis=0, tiled=True, axis_index_groups=XY_GROUPS
    )
    w_out = plane_gather(plane_copies(hold(pair[:, 3 * units :], line)))
    o, o_full, lse = attend(
        scalars, q, kv, query_column, key_blocks[None, :], [near]
    )
    grad_all = [grads, near, flip(hold(near, o), co=1)]
    o_heads = across(hold(o.reshape(NX, half, HEAD), w_out)).reshape(2, 2 * half, HEAD)
    attn_sum = column_sum(*output(o_heads, w_out))

    x_own = x_own.astype(F32)
    dy_own = grads[:tile].astype(F32)
    middle = x_own + attn_sum
    normed_two, inverse_two = norm(middle)
    second_low = column_gather(normed_two.astype(BF16))
    keep, send, turned, hidden = mlp(second_low, grad_all, mlp_w, [key_column, query_rows])
    terms = mlp_grads(second_low, grad_all, turned.reshape(3 * units, -1))
    sums = lax.psum_scatter(
        terms, "ctx", scatter_dimension=0, tiled=True, axis_index_groups=XY_GROUPS
    )
    back_two = column_sum(keep, send, terms)
    grad_middle = dy_own + norm_back(back_two, normed_two, inverse_two)
    middle_low = column_gather(grad_middle.astype(BF16))

    do_send = outward(middle_low, w_out)
    do = across(do_send).reshape(query_count, tile, HEAD)
    out_terms = output_grads(middle_low, o_heads, [do_send])
    out_sums = lax.psum_scatter(
        out_terms, "ctx", scatter_dimension=0, tiled=True, axis_index_groups=XY_GROUPS
    )
    out_keep, out_send = down(hidden, mlp_w, [do_send])
    dq, dkv, *others = attend_back(
        scalars,
        q,
        kv,
        do,
        o_full,
        lse,
        query_rows,
        key_column,
        [out_keep, out_terms],
    )
    pairs = [(dkv[:2], dkv[2:])] + [tuple(others[2 * k : 2 * k + 2]) for k in range(3)]
    dkv = jnp.concatenate(ring_sum(pairs, dy=1), axis=0).astype(BF16)
    dqkv = across(jnp.concatenate([dq.reshape(NX, 1, half, HEAD), dkv], axis=1))
    keep, send, terms = backward(first_low, dqkv, cosine, sine, attn_w, [])
    out_low = (middle + column_sum(out_keep, hold(out_send, send))).astype(BF16)
    terms = lax.all_to_all(terms, "ctx", 0, 0, tiled=True, axis_index_groups=XY_GROUPS)
    back_one = column_sum(keep, send)
    normed_own, inverse_own = norm(x_own)
    grad_own = grad_middle + norm_back(back_one, normed_own, inverse_own)
    grad_in = finish(co, zh, grad_own.astype(BF16), F32)
    tokens_out = finish(co, zh, out_low, BF16)
    mlp_out = place(zl, sums, (units,) * 3, [send])
    output_out = place(zl, out_sums, (wide,), [send])
    after = [grad_in, tokens_out, mlp_out[0], output_out[0]]
    return (
        tokens_out,
        grad_in,
        *place(zl, terms, (wide,) * 3, after),
        *output_out,
        *mlp_out,
    )


def solution(mesh):
    row, both = P("ctx", None), P("ctx", "tp")
    return jax.shard_map(
        local,
        mesh=mesh,
        in_specs=(row,) + (both,) * 7 + (row, P(), P()),
        out_specs=(row, row) + (both,) * 7,
        check_vma=False,
    )
```

```python
import functools

import jax
import jax.numpy as jnp
from jax import lax
from jax.experimental import pallas as pl
from jax.experimental.pallas import tpu as pltpu
from jax.sharding import PartitionSpec as P

HEAD = 128
NY, NZL, NX = 4, 2, 4
BOTH = ("ctx", "tp")
QB = 256
KC = 1024
LOG2E = 1.4426950408889634
VMEM_LIMIT = 56 * 1024 * 1024
F32, BF16 = jnp.float32, jnp.bfloat16


def ctx_index(y, zl, x):
    return (y * NZL + zl) * NX + x


XY_GROUPS = [
    [ctx_index(y, zl, x) for y in range(NY) for x in range(NX)] for zl in range(NZL)
]
X_GROUPS = [
    [ctx_index(y, zl, x) for x in range(NX)] for y in range(NY) for zl in range(NZL)
]


def flip(values, zl=0, zh=0, co=0):
    pairs = []
    for y in range(NY):
        for a in range(NZL):
            for x in range(NX):
                for t in range(4):
                    here = ctx_index(y, a, x) * 4 + t
                    there = ctx_index(y, a ^ zl, x) * 4 + (t ^ (2 * zh + co))
                    pairs.append((here, there))
    return lax.ppermute(values, BOTH, pairs)


def ring(values, dx=0, dy=0):
    pairs = [
        (ctx_index(y, a, x), ctx_index((y + dy) % NY, a, (x + dx) % NX))
        for y in range(NY)
        for a in range(NZL)
        for x in range(NX)
    ]
    return lax.ppermute(values, "ctx", pairs)


def turn(values, axis, bit):
    return jnp.where(bit == 1, jnp.flip(values, axis), values)


def norm(values):
    average = jnp.mean(values, axis=-1, keepdims=True)
    centred = values - average
    inverse = lax.rsqrt(jnp.mean(centred * centred, axis=-1, keepdims=True) + 1e-05)
    return centred * inverse, inverse


def norm_back(grad, normed, inverse):
    first = jnp.mean(grad, axis=-1, keepdims=True)
    second = jnp.mean(grad * normed, axis=-1, keepdims=True)
    return inverse * (grad - first - normed * second)


def column_sum(keep, send, token=None):
    rows = keep.shape[0] // 4
    cut = rows // 2
    got = flip(send, co=1)
    half = keep.astype(F32) + got.astype(F32)
    if token is not None:
        half = hold(half, token)
    own, far, near, both = (half[k * rows : (k + 1) * rows] for k in range(4))
    for_both = flip(far[:cut].astype(BF16), zl=1)
    for_near = flip(far[cut:].astype(BF16), zl=1, zh=1)
    near = jnp.concatenate([near[:cut], near[cut:] + for_near.astype(F32)], axis=0).astype(BF16)
    both = jnp.concatenate([both[:cut] + for_both.astype(F32), both[cut:]], axis=0).astype(BF16)
    from_near, from_both = flip(near, zl=1), flip(both, zl=1, zh=1)
    return own + from_near.astype(F32) + from_both.astype(F32)


def column_gather(rows):
    cut = rows.shape[0] // 2
    near, both = flip(rows, zl=1), flip(rows, zl=1, zh=1)
    far_low, far_high = flip(both[:cut], zl=1), flip(near[cut:], zl=1, zh=1)
    half = [rows, far_low, far_high, near, both]
    return half + [flip(piece, co=1) for piece in half]


def ring_sum(parts, **step):
    forth, back = step, {k: -v for k, v in step.items()}
    ahead, behind = ring(parts[2][0], **forth), ring(parts[2][1], **back)
    from_back, from_forth = ring(parts[1][1], **forth), ring(parts[3][0], **back)
    low = parts[1][0].astype(F32) + ahead.astype(F32)
    high = parts[3][1].astype(F32) + behind.astype(F32)
    low, high = ring(low.astype(BF16), **forth), ring(high.astype(BF16), **back)
    return (
        parts[0][0].astype(F32) + low.astype(F32) + from_forth.astype(F32),
        parts[0][1].astype(F32) + from_back.astype(F32) + high.astype(F32),
    )


def ring_gather(rows, tokens, **step):
    forth, back = step, {k: -v for k, v in step.items()}
    cut = rows.shape[0] // 2
    before, after = ring(rows, **forth), ring(rows, **back)
    low, high = before[:cut], after[cut:]
    for one in tokens:
        low, high = hold(low, one), hold(high, one)
    low, high = ring(low, **forth), ring(high, **back)
    return rows, after, low, high, before


def plane_copies(rows):
    return jnp.broadcast_to(rows[None], (NY * NX,) + rows.shape)


def plane_gather(copies):
    every = lax.all_to_all(copies, "ctx", 0, 0, tiled=True, axis_index_groups=XY_GROUPS)
    return every.reshape(-1, copies.shape[2])


def dot(left, right):
    return jnp.dot(left, right, preferred_element_type=F32)


def dot_nt(left, right):
    return lax.dot_general(left, right, (((1,), (1,)), ((), ())), preferred_element_type=F32)


def dot_tn(left, right):
    return lax.dot_general(left, right, (((0,), (0,)), ((), ())), preferred_element_type=F32)


def call(kernel, name, outs, scalars, arrays, after=(), scratch=(), flops=1, specs=None):
    head, tail = len(scalars) + len(arrays), len(after)
    vmem = pl.BlockSpec(memory_space=pltpu.VMEM)
    specs = specs or {}
    grid = {"grid": (1,)} if specs else {}

    def body(*refs):
        kernel(*refs[:head], *refs[head + tail :])

    return pl.pallas_call(
        body,
        **grid,
        out_shape=tuple(jax.ShapeDtypeStruct(shape, dtype) for shape, dtype in outs),
        in_specs=[pl.BlockSpec(memory_space=pltpu.SMEM)] * len(scalars)
        + [specs.get(k, vmem) for k in range(len(arrays))]
        + [pl.BlockSpec(memory_space=pl.ANY)] * tail,
        out_specs=(vmem,) * len(outs),
        scratch_shapes=list(scratch),
        compiler_params=pltpu.CompilerParams(vmem_limit_bytes=VMEM_LIMIT),
        cost_estimate=pl.CostEstimate(flops=flops, bytes_accessed=1, transcendentals=0),
        name=name,
    )(*[jnp.stack(s).astype(jnp.int32) for s in scalars], *arrays, *after)


def hold(values, token):
    return values + (token[(0,) * token.ndim] * 0).astype(values.dtype)


def put_rows(to_ref, refs):
    row = 0
    for ref in refs:
        to_ref[row : row + ref.shape[0], :] = ref[...]
        row += ref.shape[0]


def enter_kernel(at, x_ref, dy_ref, a_ref, dy_out, own_ref):
    tile = own_ref.shape[0]
    lane = lax.broadcasted_iota(jnp.int32, (tile, HEAD), 1)
    for k in range(4):
        row = ((k // 2) ^ at[0]) * 2 + ((k % 2) ^ at[1])
        rows = pl.ds(pl.multiple_of(row * tile, tile), tile)
        x = x_ref[rows, :].astype(F32)
        values = [(norm(x)[0], a_ref), (dy_ref[rows, :].astype(F32), dy_out)]
        if k == 0:
            values.append((x, own_ref))
        for value, to_ref in values:
            for y in range(NY):
                for half in range(NX // 2):
                    pair = [
                        value[:, c : c + HEAD]
                        for c in [(y * NZL + z) * NX * HEAD // 2 + half * HEAD for z in range(2)]
                    ]
                    turned = [pltpu.roll(v, HEAD // 2, 1) for v in pair]
                    low = jnp.where(lane < HEAD // 2, pair[0], turned[1])
                    high = jnp.where(lane < HEAD // 2, turned[0], pair[1])
                    for n, v in enumerate((low, high)):
                        c = (y * NX + 2 * half + n) * HEAD
                        to_ref[k * tile : (k + 1) * tile, c : c + HEAD] = v.astype(BF16)


def enter(co, zh, x, dy, after):
    rows, width = x.shape
    outs = [((rows, width), BF16)] * 2 + [((rows // 4, width), BF16)]
    return call(enter_kernel, "enter", outs, [(co, zh)], [x, dy], after)


def each_piece(pairs):
    own, after, low, high, before = pairs
    for dy in range(NY):
        for x in range(NX):
            ref = (own, after, (low, high)[x // 2], before)[dy]
            for k in range(4):
                yield (dy * NX + x) * 4 + k, x % 2 if dy == 2 else x, k, ref


def sort_pairs(scalars, pairs, keys, values, tile):
    for slot, x, k, ref in each_piece(pairs):
        rows = pl.ds(pl.multiple_of(scalars[slot] * tile, tile), tile)
        keys[rows, :] = ref[x, 0, k * tile : (k + 1) * tile]
        values[rows, :] = ref[x, 1, k * tile : (k + 1) * tile]


def attend_kernel(
    scalars, q_ref, kv0, kv1, kv2, kv3, kv4, qblk, kblk, o_ref, full_ref, lse_ref, keys, values, queries, *, tile
):
    tiles = keys.shape[0] // tile
    per = QB // tile
    blocks = q_ref.shape[0] // per
    factor = HEAD**-0.5 * LOG2E
    sort_pairs(scalars, (kv0, kv1, kv2, kv3, kv4), keys, values, tile)

    def block(i, carry):
        for k in range(per):
            queries[k * tile : (k + 1) * tile, :] = q_ref[scalars[tiles + i * per + k]]
        q_own = queries[...]
        rows = pl.ds(pl.multiple_of(i * QB, QB), QB)

        def chunk(c, state, masked):
            top, total, acc = state
            where = pl.ds(pl.multiple_of(c * KC, KC), KC)
            s = dot_nt(q_own, keys[where, :])
            if masked:
                s = jnp.where(qblk[rows, :] >= kblk[:, where], s, -1e30)
            new = jnp.maximum(top, jnp.max(s, axis=-1, keepdims=True))
            p = jnp.exp2((s - new) * factor)
            shrink = jnp.exp2((top - new) * factor)
            total = total * shrink + jnp.sum(p, axis=-1, keepdims=True)
            acc = acc * shrink + dot(p.astype(BF16), values[where, :])
            return new, total, acc

        base = tiles + blocks * per
        state = (
            jnp.full((QB, 1), -1e30, F32),
            jnp.zeros((QB, 1), F32),
            jnp.zeros((QB, HEAD), F32),
        )
        first, last = scalars[base + i], scalars[base + blocks + i]
        state = lax.fori_loop(0, first, functools.partial(chunk, masked=False), state)
        top, total, acc = lax.fori_loop(first, last, functools.partial(chunk, masked=True), state)
        out = acc / total
        full_ref[rows, :] = out
        low = out.astype(BF16)
        for k in range(per):
            o_ref[scalars[tiles + i * per + k]] = low[k * tile : (k + 1) * tile]
        lse = top * factor + jnp.log2(total)
        lse_ref[i] = jnp.transpose(jnp.broadcast_to(lse, (QB, HEAD)))[:8]
        return carry

    lax.fori_loop(0, blocks, block, 0)


def attend(scalars, q, kv, qblk, kblk, after):
    tile = q.shape[1]
    count = q.shape[0] * tile
    length = kblk.shape[1]
    vmem = pl.BlockSpec(memory_space=pltpu.VMEM)
    kernel = functools.partial(attend_kernel, tile=tile)

    def body(*refs):
        kernel(*refs[:9], *refs[9 + len(after) :])

    return pl.pallas_call(
        body,
        out_shape=(
            jax.ShapeDtypeStruct(q.shape, BF16),
            jax.ShapeDtypeStruct((count, HEAD), F32),
            jax.ShapeDtypeStruct((count // QB, 8, QB), F32),
        ),
        in_specs=[pl.BlockSpec(memory_space=pltpu.SMEM)]
        + [vmem] * 8
        + [pl.BlockSpec(memory_space=pl.ANY)] * len(after),
        out_specs=(vmem,) * 3,
        scratch_shapes=[
            pltpu.VMEM((length, HEAD), BF16),
            pltpu.VMEM((length, HEAD), BF16),
            pltpu.VMEM((QB, HEAD), BF16),
        ],
        compiler_params=pltpu.CompilerParams(vmem_limit_bytes=VMEM_LIMIT),
        cost_estimate=pl.CostEstimate(
            flops=32 * count * length * HEAD, bytes_accessed=1 << 22, transcendentals=count * length
        ),
        name="attend",
    )(scalars, q, *kv, qblk, kblk, *after)


def attend_back_kernel(
    scalars,
    q_ref,
    kv0,
    kv1,
    kv2,
    kv3,
    kv4,
    do_ref,
    full_ref,
    lse_ref,
    qblk,
    kblk,
    dq_ref,
    own_ref,
    after_low,
    after_high,
    far_low,
    far_high,
    before_low,
    before_high,
    keys,
    values,
    queries,
    grads,
    dk,
    dv,
    *,
    tile,
):
    tiles = keys.shape[0] // tile
    per = QB // tile
    blocks = q_ref.shape[0] // per
    scale = HEAD**-0.5
    factor = scale * LOG2E
    sort_pairs(scalars, (kv0, kv1, kv2, kv3, kv4), keys, values, tile)
    dk[...] = jnp.zeros_like(dk)
    dv[...] = jnp.zeros_like(dv)

    def block(i, carry):
        for k in range(per):
            slot = scalars[tiles + i * per + k]
            queries[k * tile : (k + 1) * tile, :] = q_ref[slot]
            grads[k * tile : (k + 1) * tile, :] = do_ref[slot]
        q_own = queries[...]
        do_own = grads[...]
        rows = pl.ds(pl.multiple_of(i * QB, QB), QB)
        product = do_own.astype(F32) * full_ref[rows, :]
        delta = jnp.sum(jnp.transpose(product), axis=0, keepdims=True)
        lse = lse_ref[i][:1]
        q_blocks = qblk[i][:1]

        def chunk(c, acc, masked):
            where = pl.ds(pl.multiple_of(c * KC, KC), KC)
            k_own = keys[where, :]
            s = dot_nt(k_own, q_own)
            if masked:
                s = jnp.where(kblk[where, :] <= q_blocks, s, -1e30)
            p = jnp.exp2(s * factor - lse)
            dp = dot_nt(values[where, :], do_own)
            ds = (p * (dp - delta)).astype(BF16)
            dv[where, :] += dot(p.astype(BF16), do_own)
            dk[where, :] += dot(ds, q_own)
            return acc + dot_tn(ds, k_own)

        base = tiles + blocks * per
        first, last = scalars[base + i], scalars[base + blocks + i]
        acc = jnp.zeros((QB, HEAD), F32)
        acc = lax.fori_loop(0, first, functools.partial(chunk, masked=False), acc)
        acc = lax.fori_loop(first, last, functools.partial(chunk, masked=True), acc)
        low = (acc * scale).astype(BF16)
        for k in range(per):
            dq_ref[scalars[tiles + i * per + k]] = low[k * tile : (k + 1) * tile]
        return carry

    lax.fori_loop(0, blocks, block, 0)

    outs = ((own_ref, own_ref), (after_low, after_high), (far_low, far_high), (before_low, before_high))
    for slot in range(tiles):
        dy, x, k = slot // 16, slot // 4 % 4, slot % 4
        rows = pl.ds(pl.multiple_of(scalars[slot] * tile, tile), tile)
        ref, x = outs[dy][x // 2], x if dy == 0 else x % 2
        here = slice(k * tile, (k + 1) * tile)
        ref[x, 0, here] = (dk[rows, :] * scale).astype(BF16)
        ref[x, 1, here] = dv[rows, :].astype(BF16)


def attend_back(scalars, q, kv, do, full, lse, qblk, kblk, after):
    tile = q.shape[1]
    count = q.shape[0] * tile
    length = kblk.shape[0]
    vmem = pl.BlockSpec(memory_space=pltpu.VMEM)
    kernel = functools.partial(attend_back_kernel, tile=tile)

    def body(*refs):
        kernel(*refs[:12], *refs[12 + len(after) :])

    return pl.pallas_call(
        body,
        out_shape=(
            jax.ShapeDtypeStruct(q.shape, BF16),
            jax.ShapeDtypeStruct(kv[0].shape, BF16),
        )
        + (jax.ShapeDtypeStruct(kv[2].shape, BF16),) * 6,
        in_specs=[pl.BlockSpec(memory_space=pltpu.SMEM)]
        + [vmem] * 11
        + [pl.BlockSpec(memory_space=pl.ANY)] * len(after),
        out_specs=(vmem,) * 8,
        scratch_shapes=[
            pltpu.VMEM((length, HEAD), BF16),
            pltpu.VMEM((length, HEAD), BF16),
            pltpu.VMEM((QB, HEAD), BF16),
            pltpu.VMEM((QB, HEAD), BF16),
            pltpu.VMEM((length, HEAD), F32),
            pltpu.VMEM((length, HEAD), F32),
        ],
        compiler_params=pltpu.CompilerParams(vmem_limit_bytes=VMEM_LIMIT),
        cost_estimate=pl.CostEstimate(
            flops=40 * count * length * HEAD, bytes_accessed=1 << 23, transcendentals=count * length
        ),
        name="attend_back",
    )(scalars, q, *kv, do, full, lse, qblk, kblk, *after)


def project_kernel(own_ref, near_ref, other_ref, w_ref, cos_ref, sin_ref, qkv_ref, a_ref):
    half = own_ref.shape[0]
    spread_rows(a_ref, (own_ref, near_ref, other_ref))
    cosine, sine = cos_ref[...], sin_ref[...]
    for part in range(3):
        product = dot(a_ref[...], w_ref[:, part * 2 * HEAD : (part + 1) * 2 * HEAD])
        for head in range(2):
            u = product[:, head * HEAD : (head + 1) * HEAD]
            if part < 2:
                u = u * cosine + pltpu.roll(u, HEAD // 2, 1) * sine
            u = u.astype(BF16)
            for ds in range(2):
                rows = u[ds * half : (ds + 1) * half]
                qkv_ref[head * 2 + ds, part] = rows


def project(a, weights, cosine, sine, after):
    half, width = a[0].shape
    return call(
        project_kernel,
        "project",
        [((4, 3, half, HEAD), BF16)],
        [],
        [*a, weights, cosine, sine],
        after,
        scratch=[pltpu.VMEM((2 * half, width), BF16)],
        flops=4 * half * width * 6 * HEAD,
    )[0]


def output_kernel(o_ref, w_ref, keep_ref, send_ref):
    half = keep_ref.shape[0]
    o = jnp.concatenate([o_ref[0], o_ref[1]], axis=1)
    for c in range(0, keep_ref.shape[1], 512):
        part = dot_nt(o, w_ref[c : c + 512, :]).astype(BF16)
        keep_ref[:, c : c + 512] = part[:half]
        send_ref[:, c : c + 512] = part[half:]


def output(o_heads, weights):
    rows, width = o_heads.shape[1], weights.shape[0]
    outs = [((rows // 2, width), BF16)] * 2
    flops = 4 * rows * width * HEAD
    return call(output_kernel, "output", outs, [], [o_heads, weights], flops=flops)


def mlp_kernel(*refs):
    b_parts, dy_parts = refs[:10], refs[10:13]
    gate_ref, up_ref, down_ref, rows_ref, keep_ref, send_ref, turned_ref, hidden_ref = refs[13:21]
    b_ref, dy_ref, dg_ref, du_ref = refs[21:]
    step = pl.program_id(0)
    half, units, each = dy_parts[0].shape[0], dg_ref.shape[1], gate_ref.shape[1]
    steps = units // each

    @pl.when(step == 0)
    def _():
        put_rows(b_ref, b_parts)
        spread_rows(dy_ref, dy_parts)

    @pl.when(step < steps)
    def _():
        here = pl.ds(pl.multiple_of(step * each, each), each)
        gate = dot(b_ref[...], gate_ref[...])
        upper = dot(b_ref[...], up_ref[...])
        grad = dot(dy_ref[...], down_ref[...])
        sigmoid = 1.0 / (1.0 + jnp.exp(-gate))
        swish = gate * sigmoid
        made = (
            (grad * upper * sigmoid * (1.0 + gate * (1.0 - sigmoid))).astype(BF16),
            (grad * swish).astype(BF16),
            (swish * upper).astype(BF16),
        )
        for k, value in enumerate(made):
            turned_ref[k] = jnp.transpose(value)
        dg_ref[:, here] = made[0]
        du_ref[:, here] = made[1]
        hidden_ref[...] = made[2]

    @pl.when(step >= steps)
    def _():
        part = dot_nt(dg_ref[...], rows_ref[:, :units])
        part = (part + dot_nt(du_ref[...], rows_ref[:, units:])).astype(BF16)
        keep_ref[...] = part[:half]
        send_ref[...] = part[half:]


def mlp(b_parts, dy_parts, mlp_w, after):
    half, width = dy_parts[0].shape
    units, each, rows = mlp_w.shape[1] // 3, 512, 512
    steps, more = units // each, width // rows
    vmem = pl.BlockSpec(memory_space=pltpu.VMEM)

    def first(i):
        return jnp.minimum(i, steps - 1)

    def second(i):
        return jnp.maximum(i - steps, 0)

    def body(*refs):
        mlp_kernel(*refs[:17], *refs[17 + len(after) :])

    return pl.pallas_call(
        body,
        grid=(steps + more,),
        out_shape=(
            jax.ShapeDtypeStruct((half, width), BF16),
            jax.ShapeDtypeStruct((half, width), BF16),
            jax.ShapeDtypeStruct((3, units, 2 * half), BF16),
            jax.ShapeDtypeStruct((2 * half, units), BF16),
        ),
        in_specs=[vmem] * 13
        + [
            pl.BlockSpec((width, each), lambda i: (0, first(i))),
            pl.BlockSpec((width, each), lambda i: (0, steps + first(i))),
            pl.BlockSpec((width, each), lambda i: (0, 2 * steps + first(i))),
            pl.BlockSpec((rows, 2 * units), lambda i: (second(i), 0)),
        ]
        + [pl.BlockSpec(memory_space=pl.ANY)] * len(after),
        out_specs=(
            pl.BlockSpec((half, rows), lambda i: (0, second(i))),
            pl.BlockSpec((half, rows), lambda i: (0, second(i))),
            pl.BlockSpec((3, each, 2 * half), lambda i: (0, first(i), 0)),
            pl.BlockSpec((2 * half, each), lambda i: (0, first(i))),
        ),
        scratch_shapes=[pltpu.VMEM((2 * half, width), BF16)] * 2
        + [pltpu.VMEM((2 * half, units), BF16)] * 2,
        compiler_params=pltpu.CompilerParams(vmem_limit_bytes=VMEM_LIMIT),
        cost_estimate=pl.CostEstimate(
            flops=20 * half * width * units, bytes_accessed=1, transcendentals=0
        ),
        name="mlp",
    )(*b_parts, *dy_parts, *[mlp_w] * 4, *after)


def down_kernel(hidden_ref, w_ref, keep_ref, send_ref):
    half = keep_ref.shape[0]
    for c in range(0, keep_ref.shape[1], 512):
        part = dot_nt(hidden_ref[...], w_ref[c : c + 512, :]).astype(BF16)
        keep_ref[:, c : c + 512] = part[:half]
        send_ref[:, c : c + 512] = part[half:]


def down(hidden, mlp_w, after):
    (rows, units), width = hidden.shape, mlp_w.shape[0]
    spec = pl.BlockSpec((width, units), lambda i: (0, 2))
    outs = [((rows // 2, width), BF16)] * 2
    flops = 2 * rows * width * units
    return call(down_kernel, "down", outs, [], [hidden, mlp_w], after, flops=flops, specs={1: spec})


def spread_rows(to_ref, parts):
    own, near, *other = parts
    half = own.shape[0] // 2
    other = other[0] if other else near.at[half:]
    put_rows(to_ref, [own.at[:half], near.at[:half], own.at[half:], other])


def put_blocks(out_ref, row, column, product):
    for r in range(0, product.shape[1], HEAD):
        for c in range(0, product.shape[0], HEAD):
            out_ref[row + r // HEAD, column + c // HEAD] = product[c : c + HEAD, r : r + HEAD]


def mlp_grads_kernel(*refs, units):
    b_parts, dy_parts = refs[:10], refs[10:13]
    left_ref, out_ref, b_ref, dy_ref = refs[13:]
    step = pl.program_id(0)
    later = 2 * units // left_ref.shape[0]

    @pl.when(step == 0)
    def _():
        put_rows(b_ref, b_parts)
        spread_rows(dy_ref, dy_parts)

    def work(right_ref):
        for r in range(0, right_ref.shape[1], 512):
            product = dot(left_ref[...], right_ref[:, r : r + 512]).astype(BF16)
            put_blocks(out_ref, r // HEAD, 0, product)

    pl.when(step < later)(lambda: work(b_ref))
    pl.when(step >= later)(lambda: work(dy_ref))


def mlp_grads(b_parts, dy_parts, turned):
    rows, tokens = turned.shape
    width, step = b_parts[0].shape[1], 512
    vmem = pl.BlockSpec(memory_space=pltpu.VMEM)
    return pl.pallas_call(
        functools.partial(mlp_grads_kernel, units=rows // 3),
        grid=(rows // step,),
        out_shape=jax.ShapeDtypeStruct((width // HEAD, rows // HEAD, HEAD, HEAD), BF16),
        in_specs=[vmem] * 13 + [pl.BlockSpec((step, tokens), lambda i: (i, 0))],
        out_specs=pl.BlockSpec(
            (width // HEAD, step // HEAD, HEAD, HEAD), lambda i: (0, i, 0, 0)
        ),
        scratch_shapes=[pltpu.VMEM((tokens, width), BF16)] * 2,
        compiler_params=pltpu.CompilerParams(vmem_limit_bytes=VMEM_LIMIT),
        cost_estimate=pl.CostEstimate(
            flops=2 * rows * tokens * width, bytes_accessed=1, transcendentals=0
        ),
        name="mlp_grads",
    )(*b_parts, *dy_parts, turned)


def outward_kernel(*refs):
    parts, (w_ref, do_ref, m_ref) = refs[:10], refs[10:]
    put_rows(m_ref, parts)
    part = dot(m_ref[...], w_ref[...]).astype(BF16)
    half = part.shape[0] // 2
    for head in range(2):
        for ds in range(2):
            do_ref[head * 2 + ds] = part[
                ds * half : (ds + 1) * half, head * HEAD : (head + 1) * HEAD
            ]


def outward(m_parts, attn_w):
    width = attn_w.shape[0]
    half = sum(v.shape[0] for v in m_parts) // 2
    return call(
        outward_kernel,
        "outward",
        [((4, half, HEAD), BF16)],
        [],
        [*m_parts, attn_w],
        scratch=[pltpu.VMEM((2 * half, width), BF16)],
        flops=8 * half * width * HEAD,
    )[0]


def back_kernel(*refs):
    parts, m_parts, (dqkv_ref, cos_ref, sin_ref, o_ref, w_ref) = refs[:3], refs[3:13], refs[13:18]
    keep_ref, send_ref, out_ref, back_ref, a_ref = refs[18:]
    spread_rows(a_ref, parts)
    half = dqkv_ref.shape[2]
    cosine, sine = cos_ref[...], sin_ref[...]
    for part in range(3):
        for head in range(2):
            for ds in range(2):
                rows = slice(ds * half, (ds + 1) * half)
                e = dqkv_ref[head * 2 + ds, part].astype(F32)
                if part < 2:
                    e = e * cosine[rows] - pltpu.roll(e, HEAD // 2, 1) * sine[rows]
                column = (part * 2 + head) * HEAD
                back_ref[rows, column : column + HEAD] = e.astype(BF16)
    for c in range(0, keep_ref.shape[1], 512):
        part = dot_nt(back_ref[...], w_ref[c : c + 512, :]).astype(BF16)
        keep_ref[:, c : c + 512] = part[:half]
        send_ref[:, c : c + 512] = part[half:]
    for c in range(0, back_ref.shape[1], 2 * HEAD):
        left = jnp.transpose(back_ref[:, c : c + 2 * HEAD])
        for r in range(0, a_ref.shape[1], 512):
            product = dot(left, a_ref[:, r : r + 512]).astype(BF16)
            put_blocks(out_ref, r // HEAD, c // HEAD, product)
    put_rows(a_ref, m_parts)
    left = jnp.concatenate([jnp.transpose(o_ref[k]) for k in range(2)], axis=0)
    for r in range(0, a_ref.shape[1], 512):
        put_blocks(out_ref, r // HEAD, 6, dot(left, a_ref[:, r : r + 512]).astype(BF16))


def backward(a_parts, m_parts, dqkv, cosine, sine, o_heads, attn_w, after):
    half, width = dqkv.shape[2], attn_w.shape[0]
    return call(
        back_kernel,
        "backward",
        [((half, width), BF16)] * 2 + [((width // HEAD, 8, HEAD, HEAD), BF16)],
        [],
        [*a_parts, *m_parts, dqkv, cosine, sine, o_heads, attn_w],
        after,
        scratch=[
            pltpu.VMEM((2 * half, 6 * HEAD), BF16),
            pltpu.VMEM((2 * half, width), BF16),
        ],
        flops=48 * half * width * HEAD,
    )


def total_kernel(at, terms_ref, keep_ref, send_ref):
    rows = keep_ref.shape[1]
    for c in range(keep_ref.shape[0]):
        total = terms_ref[0, c].astype(F32)
        for p in range(1, terms_ref.shape[0]):
            total = total + terms_ref[p, c].astype(F32)
        total = jnp.transpose(total)
        first, second = total[:rows], total[rows:]
        keep_ref[c] = jnp.where(at[0] == 0, first, second).astype(BF16)
        send_ref[c] = jnp.where(at[0] == 0, second, first).astype(BF16)


def total(zl, terms, after=()):
    outs = [((terms.shape[1], HEAD // 2, HEAD), BF16)] * 2
    return call(total_kernel, "total", outs, [(zl,)], [terms], after)


def place_kernel(at, keep_ref, got_ref, *outs):
    block = 0
    for out_ref in outs:
        half = out_ref.shape[1] // 2
        for c in range(0, half, HEAD):
            keep, got = keep_ref[block].astype(F32), got_ref[block].astype(F32)
            out_ref[:, c : c + HEAD] = jnp.where(at[0] == 0, keep, got)
            out_ref[:, half + c : half + c + HEAD] = jnp.where(at[0] == 0, got, keep)
            block += 1


def place(zl, sums, widths, after=()):
    keep, send = total(zl, sums, after)
    outs = [((HEAD // 2, 2 * w), F32) for w in widths]
    return call(place_kernel, "place", outs, [(zl,)], [keep, flip(send, zl=1)])


def finish_kernel(at, own_ref, far_ref, pair_ref, out_ref):
    tile = own_ref.shape[0]
    co, zh = at[0], at[1]
    lane = lax.broadcasted_iota(jnp.int32, (tile, HEAD), 1)
    for k in range(4):
        ref, start = ((own_ref, 0), (far_ref, 0), (pair_ref, 0), (pair_ref, tile))[k]
        at_row = ((k // 2) ^ co) * 2 + ((k % 2) ^ zh)
        rows = pl.ds(pl.multiple_of(at_row * tile, tile), tile)
        for y in range(NY):
            for half in range(NX // 2):
                pair = [
                    ref[start : start + tile, c : c + HEAD].astype(F32)
                    for c in ((y * NX + 2 * half) * HEAD, (y * NX + 2 * half + 1) * HEAD)
                ]
                turned = [pltpu.roll(v, HEAD // 2, 1) for v in pair]
                low = jnp.where(lane < HEAD // 2, pair[0], turned[1])
                high = jnp.where(lane < HEAD // 2, turned[0], pair[1])
                for zl, value in enumerate((low, high)):
                    column = (y * NZL + zl) * NX * HEAD // 2 + half * HEAD
                    out_ref[rows, column : column + HEAD] = value.astype(out_ref.dtype)


def finish(co, zh, own, dtype):
    far = flip(own, zh=1)
    pair = flip(jnp.concatenate([own, far], axis=0), co=1)
    vmem = pl.BlockSpec(memory_space=pltpu.VMEM)
    return pl.pallas_call(
        finish_kernel,
        out_shape=jax.ShapeDtypeStruct((4 * own.shape[0], own.shape[1]), dtype),
        in_specs=[pl.BlockSpec(memory_space=pltpu.SMEM)] + [vmem] * 3,
        out_specs=vmem,
        compiler_params=pltpu.CompilerParams(vmem_limit_bytes=VMEM_LIMIT),
        cost_estimate=pl.CostEstimate(flops=1, bytes_accessed=1, transcendentals=0),
        name="finish",
    )(jnp.stack([co, zh]).astype(jnp.int32), own, far, pair)


def local(
    tokens_in,
    w_query,
    w_key,
    w_value,
    w_output,
    w_gate,
    w_up,
    w_down,
    grad_out,
    block_ids,
    tile_order,
):
    own, width = tokens_in.shape
    seqs, length = block_ids.shape
    tile = length // tile_order.shape[1]
    wide = w_query.shape[1] // 2
    units = w_gate.shape[1] // 2
    piece = w_query.shape[0]
    ctx, tp = lax.axis_index("ctx"), lax.axis_index("tp")
    y, zl, x = ctx // (NZL * NX), (ctx // NX) % NZL, ctx % NX
    zh, co = tp // 2, tp % 2

    def pair_rows(arrays):
        def cut(array, which):
            half = array.shape[1] // 2
            return lax.dynamic_slice_in_dim(array, which * half, half, 1)

        kept = jnp.concatenate([cut(array, zl) for array in arrays], axis=1)
        sent = jnp.concatenate([cut(array, 1 - zl) for array in arrays], axis=1)
        return turn(jnp.stack([kept, flip(sent, zl=1)]), 0, zl).reshape(2 * piece, -1)

    pair = pair_rows((w_query, w_key, w_value))
    copies = plane_copies(pair)
    attn_w = plane_gather(copies)
    first_own, grads, x_own = enter(co, zh, tokens_in, grad_out, [copies])
    near = flip(first_own[: own // 2], zl=1)
    first_low = [first_own, near, flip(near, co=1)]
    started = (near[0, 0] * 0).astype(jnp.int32)
    pair = pair_rows([hold(w, near) for w in (w_gate, w_up, w_down, w_output)])

    tiles = (tile_order + started).reshape(seqs, NY, NZL, NX, 2)
    tiles = turn(turn(turn(tiles, 0, co), 2, zl), 4, zh)
    row_tiles = lax.dynamic_index_in_dim(tiles, y, 1, keepdims=False)
    own_tiles = lax.dynamic_index_in_dim(row_tiles, x, 2, keepdims=False).reshape(-1)
    positions = (own_tiles[:, None] * tile + jnp.arange(tile, dtype=jnp.int32)).reshape(-1)
    inverse = 10000.0 ** (-jnp.arange(0, HEAD, 2, dtype=F32) / HEAD)
    angles = positions.astype(F32)[:, None] * inverse[None, :]
    cosine = jnp.concatenate([jnp.cos(angles)] * 2, axis=-1)
    sine = jnp.concatenate([-jnp.sin(angles), jnp.sin(angles)], axis=-1)
    ds_own = x % 2
    unit_tiles = lax.dynamic_index_in_dim(tiles, ds_own, 0, keepdims=False)
    turns = (y + jnp.arange(NY, dtype=jnp.int32)) % NY
    key_tiles = jnp.swapaxes(jnp.take(unit_tiles, turns, axis=0), 1, 2).reshape(-1)
    query_tiles = lax.dynamic_index_in_dim(unit_tiles, y, 0, keepdims=False)
    query_tiles = jnp.swapaxes(query_tiles, 0, 1).reshape(-1)
    tile_count, query_count = key_tiles.shape[0], query_tiles.shape[0]
    rank = jnp.sum(query_tiles[None, :] < query_tiles[:, None], axis=1)
    places = jnp.arange(query_count, dtype=jnp.int32)
    order = jnp.sum(
        jnp.where(rank[None, :] == places[:, None], places[None, :], 0), axis=1
    ).astype(jnp.int32)
    sorted_tiles = jnp.sum(
        jnp.where(rank[None, :] == places[:, None], query_tiles[None, :], 0), axis=1
    )
    key_blocks = lax.dynamic_index_in_dim(block_ids + started, ds_own ^ co, 0, keepdims=False)
    query_blocks = jnp.take(key_blocks.reshape(tile_count, tile), sorted_tiles, axis=0).reshape(-1)
    by_block = query_blocks.reshape(-1, QB)
    sure = jnp.sum(key_blocks[None, :] <= by_block[:, :1], axis=1) // KC
    most = (jnp.sum(key_blocks[None, :] <= by_block[:, -1:], axis=1) + KC - 1) // KC
    scalars = jnp.concatenate([key_tiles, order, sure, most]).astype(jnp.int32)
    query_rows = jnp.broadcast_to(by_block[:, None, :], (by_block.shape[0], 8, QB))

    query_column, key_column = query_blocks[:, None], key_blocks[:, None]
    tables = [scalars, query_column]
    qkv_send = project(first_low, attn_w, cosine, sine, tables)
    half = own

    def across(values):
        return lax.all_to_all(values, "ctx", 0, 0, tiled=True, axis_index_groups=X_GROUPS)

    line = across(qkv_send)
    q, kv_line = line[:, 0].reshape(query_count, tile, HEAD), line[:, 1:]
    near = flip(hold(grads[: own // 2], qkv_send), zl=1)
    kv = ring_gather(kv_line, (), dy=1)
    mlp_w = lax.all_gather(
        hold(pair[:, : 3 * units], kv[1]), "ctx", axis=0, tiled=True, axis_index_groups=XY_GROUPS
    )
    w_out = plane_gather(plane_copies(hold(pair[:, 3 * units :], line)))
    o, o_full, lse = attend(
        scalars, q, kv, query_column, key_blocks[None, :], [near]
    )
    grad_all = [grads, near, flip(hold(near, o), co=1)]
    o_heads = across(hold(o.reshape(NX, half, HEAD), w_out)).reshape(2, 2 * half, HEAD)
    attn_sum = column_sum(*output(o_heads, w_out))

    x_own = x_own.astype(F32)
    dy_own = grads[:tile].astype(F32)
    middle = x_own + attn_sum
    normed_two, inverse_two = norm(middle)
    second_low = column_gather(normed_two.astype(BF16))
    keep, send, turned, hidden = mlp(second_low, grad_all, mlp_w, [key_column, query_rows])
    terms = mlp_grads(second_low, grad_all, turned.reshape(3 * units, -1))
    sums = lax.psum_scatter(
        terms, "ctx", scatter_dimension=0, tiled=True, axis_index_groups=XY_GROUPS
    )
    back_two = column_sum(keep, send, terms)
    grad_middle = dy_own + norm_back(back_two, normed_two, inverse_two)
    middle_low = column_gather(grad_middle.astype(BF16))

    do_send = outward(middle_low, w_out)
    do = across(do_send).reshape(query_count, tile, HEAD)
    out_keep, out_send = down(hidden, mlp_w, [do_send])
    dq, dkv, *others = attend_back(
        scalars,
        q,
        kv,
        do,
        o_full,
        lse,
        query_rows,
        key_column,
        [out_keep],
    )
    pairs = [(dkv[:2], dkv[2:])] + [tuple(others[2 * k : 2 * k + 2]) for k in range(3)]
    dkv = jnp.concatenate(ring_sum(pairs, dy=1), axis=0).astype(BF16)
    dqkv = across(jnp.concatenate([dq.reshape(NX, 1, half, HEAD), dkv], axis=1))
    keep, send, terms = backward(
        first_low, middle_low, dqkv, cosine, sine, o_heads, attn_w, []
    )
    out_low = (middle + column_sum(out_keep, hold(out_send, send))).astype(BF16)
    terms = lax.all_to_all(terms, "ctx", 0, 0, tiled=True, axis_index_groups=XY_GROUPS)
    back_one = column_sum(keep, send)
    normed_own, inverse_own = norm(x_own)
    grad_own = grad_middle + norm_back(back_one, normed_own, inverse_own)
    grad_in = finish(co, zh, grad_own.astype(BF16), F32)
    tokens_out = finish(co, zh, out_low, BF16)
    mlp_out = place(zl, sums, (units,) * 3, [send])
    return (
        tokens_out,
        grad_in,
        *place(zl, terms, (wide,) * 4, [grad_in, tokens_out, mlp_out[0]]),
        *mlp_out,
    )


def solution(mesh):
    row, both = P("ctx", None), P("ctx", "tp")
    return jax.shard_map(
        local,
        mesh=mesh,
        in_specs=(row,) + (both,) * 7 + (row, P(), P()),
        out_specs=(row, row) + (both,) * 7,
        check_vma=False,
    )
```
